32 devices in a mesh: seq: 8 (over z, y), dp: 4 (over x, core).
Axes of the slice: x: 2, y: 2, z: 4, core: 2. Of those that a mesh axis runs over, the one named last changes fastest.
Arguments:
- tokens: bfloat16 [4, 1024, 1152], P('dp', 'seq'), may hold values from -6 to 6
- block_ids: int32 [4, 1024], P('dp'), may hold values from 0 to 7, never falling along the last dimension, each value on 1 to 256 neighbouring positions
- w_qkv: bfloat16 [1152, 1536], P('dp'), may hold values from -0.1875 to 0.1875
- w_out: bfloat16 [1024, 1152], P('dp'), may hold values from -0.1875 to 0.1875
- w_gate: bfloat16 [1152, 6912], P('dp'), may hold values from -0.1875 to 0.1875
- w_up: bfloat16 [1152, 6912], P('dp'), may hold values from -0.1875 to 0.1875
- w_down: bfloat16 [6912, 1152], P('dp'), may hold values from -0.078125 to 0.078125
- gain_in: float32 [1152], replicated, may hold values from 0.25 to 1.75
- gain_query: float32 [256], replicated, may hold values from 0.25 to 1.75
- gain_key: float32 [256], replicated, may hold values from 0.25 to 1.75
- gain_attn: float32 [1152], replicated, may hold values from 0.25 to 1.75
- gain_pre: float32 [1152], replicated, may hold values from 0.25 to 1.75
- gain_post: float32 [1152], replicated, may hold values from 0.25 to 1.75
- cotangent: bfloat16 [4, 1024, 1152], P('dp', 'seq'), may hold values from -6 to 6
Outputs:
- output: bfloat16 [4, 1024, 1152], P('dp', 'seq')
- grad_tokens: float32 [4, 1024, 1152], P('dp', 'seq')
- grad_qkv: float32 [1152, 1536], P('dp', 'seq')
- grad_out: float32 [1024, 1152], P('dp', 'seq')
- grad_gate: float32 [1152, 6912], P('dp', 'seq')
- grad_up: float32 [1152, 6912], P('dp', 'seq')
- grad_down: float32 [6912, 1152], P('dp', 'seq')
- grad_gain_in: float32 [1152], replicated
- grad_gain_query: float32 [256], replicated
- grad_gain_key: float32 [256], replicated
- grad_gain_attn: float32 [1152], replicated
- grad_gain_pre: float32 [1152], replicated
- grad_gain_post: float32 [1152], replicated
The draws below stay inside these ranges and needn't reach their ends.
Inputs may be any that keep to these rules, and one draw needn't show every extreme that they name: `block_ids`: along each sequence the block numbers never fall; every block holds 1 to 256 positions and some block holds exactly 256.
All inputs are finite; a program needn't handle non-finite values.
Results may differ from the reference program's by a relative error of at most 0.019.
Values may be sent and summed in bfloat16 or wider, within the bound.
No kernel may reach another device: no remote copies, remote signals or barrier semaphores. Data moves between devices by JAX's collectives and lax.ppermute only.
A program may use at most 256 MiB of HBM per device.

```python
import math
import jax
import jax.numpy as jnp
import numpy as np
from jax import lax

D = 1152
HQ = 4
HD = 256
FF = 6912
WINDOW = 512
BLOCK = 256
LEN = 1024
BATCH = 4
QKV = 1536


def levels(key, extent, pieces, least, largest):
    level, own = 1.0, jax.random.fold_in(key, 6)
    for position, shards_of in pieces:
        steps = jnp.exp(jax.random.uniform(jax.random.fold_in(own, position), (shards_of,), jnp.float32, least / len(pieces), largest / len(pieces)))
        level = level * jnp.repeat(steps, extent[position] // shards_of).reshape([-1 if axis == position else 1 for axis in range(len(extent))])
    return level


def split_up(number_of, total, limit, slope):
    weights = [(1 << 20) // math.isqrt(grade ** slope) + 1 for grade in range(2, number_of + 1)]
    spare, given = total - limit - (number_of - 1), [1] * (number_of - 1)
    while spare > 0:
        candidates = [i for i in range(number_of - 1) if given[i] < limit]
        mass, budget = sum([weights[i] for i in candidates]), spare
        for i in candidates:
            addition = min(limit - given[i], max(1, budget * weights[i] // mass), spare)
            given[i] = given[i] + addition
            spare = spare - addition
    return np.array([limit] + given)


def uneven_parts(key, count, total, reach, skew):
    if count == 2:
        one = jax.random.randint(key, (), max(1, total - reach), min(reach, total - 1) + 1)
        return jnp.stack([one, total - one])
    tallies = jnp.asarray(split_up(count, total, reach, skew), jnp.int32)
    pairs = (count - 1) // 2
    giver, taker = tallies[1:1 + 2 * pairs:2], tallies[2:2 + 2 * pairs:2]
    room = jnp.minimum(giver - 1, reach - taker)
    passed = jax.random.randint(jax.random.fold_in(key, 1), (pairs,), 0, 1 << 20) % (room + 1)
    tallies = tallies.at[1:1 + 2 * pairs:2].set(giver - passed).at[2:2 + 2 * pairs:2].set(taker + passed)
    return tallies[jax.random.permutation(jax.random.fold_in(key, 2), count)]


def centred(stream_key, dims, width, reach, split=(), held_as=jnp.bfloat16):
    array = width * jax.random.normal(stream_key, dims, jnp.float32)
    if split:
        array = array * levels(stream_key, dims, split, -0.22, 0.18)
    return jnp.clip(array, -reach, reach).astype(held_as)


def setup_inputs(seed: int = 0) -> dict:
    streams_of = jax.random.split(jax.random.key(seed), 15)
    tokens = centred(streams_of[0], (BATCH, LEN, D), 1.0, 6.0, ((0, 4), (1, 8)))
    block_ids = jax.vmap(lambda own: jnp.searchsorted(jnp.cumsum(uneven_parts(own, 2 * LEN // BLOCK, LEN, BLOCK, 0)), jnp.arange(LEN), side="right"))(jax.random.split(streams_of[1], BATCH)).reshape((BATCH, LEN)).astype(jnp.int32)
    w_qkv = centred(streams_of[2], (D, QKV), D ** -0.5, 0.1875, ((0, 4),))
    w_out = centred(streams_of[3], (HQ * HD, D), (HQ * HD) ** -0.5, 0.1875, ((0, 4),))
    w_gate = centred(streams_of[4], (D, FF), D ** -0.5, 0.1875, ((0, 4),))
    w_up = centred(streams_of[5], (D, FF), D ** -0.5, 0.1875, ((0, 4),))
    w_down = centred(streams_of[6], (FF, D), FF ** -0.5, 0.078125, ((0, 4),))
    gain_in = jnp.clip(1.0 + 0.15 * jax.random.normal(streams_of[7], (D,), jnp.float32), 0.25, 1.75)
    gain_query = jnp.clip(1.0 + 0.15 * jax.random.normal(streams_of[8], (HD,), jnp.float32), 0.25, 1.75)
    gain_key = jnp.clip(1.0 + 0.15 * jax.random.normal(streams_of[9], (HD,), jnp.float32), 0.25, 1.75)
    gain_attn = jnp.clip(1.0 + 0.15 * jax.random.normal(streams_of[10], (D,), jnp.float32), 0.25, 1.75)
    gain_pre = jnp.clip(1.0 + 0.15 * jax.random.normal(streams_of[11], (D,), jnp.float32), 0.25, 1.75)
    gain_post = jnp.clip(1.0 + 0.15 * jax.random.normal(streams_of[12], (D,), jnp.float32), 0.25, 1.75)
    cotangent = centred(streams_of[13], (BATCH, LEN, D), 1.0, 6.0, ((0, 4), (1, 8)))
    return dict(tokens=tokens, block_ids=block_ids, w_qkv=w_qkv, w_out=w_out, w_gate=w_gate, w_up=w_up, w_down=w_down, gain_in=gain_in, gain_query=gain_query, gain_key=gain_key, gain_attn=gain_attn, gain_pre=gain_pre, gain_post=gain_post, cotangent=cotangent)


epsilon = 1e-06
exact_precision = lax.Precision.HIGHEST

@jax.custom_vjp
def low(v):
    return lax.optimization_barrier(v.astype(jnp.bfloat16)).astype(jnp.float32)

@jax.custom_vjp
def low_back(v):
    return v

def low_keep(v):
    return (low(v), None)

def low_pass(kept, grad):
    return (grad,)

def back_keep(v):
    return (v, None)

def back_low(kept, grad):
    return (low(grad),)
low.defvjp(low_keep, low_pass)
low_back.defvjp(back_keep, back_low)

def rms_scale(vector, gain):
    return vector * lax.rsqrt(lax.optimization_barrier(jnp.mean(vector * vector, axis=-1, keepdims=True)) + epsilon) * gain

def rotate(vector, positions):
    half_width = vector.shape[-1] // 2
    frequency = 10000.0 ** (-jnp.arange(half_width, dtype=jnp.float32) * 2.0 / vector.shape[-1])
    angles = positions.astype(jnp.float32)[:, None] * frequency[None, :]
    cosine = jnp.cos(angles)
    sine_part = jnp.sin(angles)
    front_half = vector[..., :half_width]
    back_half = vector[..., half_width:]
    return jnp.concatenate([front_half * cosine - back_half * sine_part, back_half * cosine + front_half * sine_part], axis=-1)

def layer_forward(inputs, seq_ids, w_qkv, w_out, w_gate, w_up, w_down, gain_in, gain_query, gain_key, gain_attn, gain_pre, gain_post):
    length = inputs.shape[0]
    query_width = HQ * HD
    normed_in = low(rms_scale(inputs, gain_in))
    projected = low_back(jnp.dot(normed_in, w_qkv, precision=exact_precision))
    positions = jnp.arange(length, dtype=jnp.int32)
    queries = projected[:, :query_width].reshape(length, HQ, HD).transpose(1, 0, 2)
    queries = low(rotate(rms_scale(queries, gain_query), positions))
    keys_all = low(rotate(rms_scale(projected[:, query_width:query_width + HD], gain_key), positions))
    values_all = low(projected[:, query_width + HD:])
    keys_pad = jnp.pad(keys_all, ((WINDOW, BLOCK), (0, 0)))
    values_pad = jnp.pad(values_all, ((WINDOW, BLOCK), (0, 0)))
    ids_pad = jnp.pad(seq_ids, (WINDOW, BLOCK), constant_values=-1)
    block_rows = min(512, length)
    key_span = block_rows + WINDOW + BLOCK
    score_scale = HD ** (-0.5)

    def attend_block(start):
        query_block = lax.dynamic_slice_in_dim(queries, start, block_rows, 1)
        key_block = lax.dynamic_slice_in_dim(keys_pad, start, key_span, 0)
        value_block = lax.dynamic_slice_in_dim(values_pad, start, key_span, 0)
        key_ids = lax.dynamic_slice_in_dim(ids_pad, start, key_span, 0)
        query_ids = lax.dynamic_slice_in_dim(seq_ids, start, block_rows, 0)
        query_place = start + jnp.arange(block_rows, dtype=jnp.int32)
        key_place = start - WINDOW + jnp.arange(key_span, dtype=jnp.int32)
        inside = (key_place >= 0) & (key_place < length)
        same_block = key_ids[None, :] == query_ids[:, None]
        earlier_block = (key_ids[None, :] < query_ids[:, None]) & (query_place[:, None] - key_place[None, :] <= WINDOW)
        allowed = inside[None, :] & (same_block | earlier_block)
        scores = low_back(jnp.einsum('hqd,kd->hqk', query_block, key_block, precision=exact_precision) * score_scale)
        scores = jnp.where(allowed[None], scores, -1e+30)
        highest = lax.optimization_barrier(jnp.max(scores, axis=-1, keepdims=True))
        weights = jnp.exp(scores - highest)
        chances = weights / lax.optimization_barrier(jnp.sum(weights, axis=-1, keepdims=True))
        return jnp.einsum('hqk,kd->hqd', low(chances), value_block, precision=exact_precision)
    starts = jnp.arange(length // block_rows, dtype=jnp.int32) * block_rows
    blocks = lax.map(jax.checkpoint(attend_block), starts)
    heads_out = blocks.transpose(0, 2, 1, 3).reshape(length, query_width)
    heads_out = low(low_back(heads_out))
    attn_out = low_back(jnp.dot(heads_out, w_out, precision=exact_precision))
    residual = inputs + rms_scale(attn_out, gain_attn)
    normed_pre = low(rms_scale(residual, gain_pre))
    gate_proj = low_back(jnp.dot(normed_pre, w_gate, precision=exact_precision))
    up_proj = low_back(jnp.dot(normed_pre, w_up, precision=exact_precision))
    hidden = low(jax.nn.gelu(gate_proj, approximate=True) * up_proj)
    down_proj = low_back(jnp.dot(hidden, w_down, precision=exact_precision))
    return residual + rms_scale(down_proj, gain_post)

def reference(tokens, block_ids, w_qkv, w_out, w_gate, w_up, w_down, gain_in, gain_query, gain_key, gain_attn, gain_pre, gain_post, cotangent):
    weights = (w_qkv.astype(jnp.float32), w_out.astype(jnp.float32), w_gate.astype(jnp.float32), w_up.astype(jnp.float32), w_down.astype(jnp.float32))
    gains = (gain_in, gain_query, gain_key, gain_attn, gain_pre, gain_post)
    params = weights + gains

    def one_sequence(carry, item):
        seq_tokens, seq_ids, seq_cotangent = item

        def forward(inputs, *values):
            return layer_forward(inputs, seq_ids, *values)
        result, pullback = jax.vjp(forward, seq_tokens.astype(jnp.float32), *params)
        grads = pullback(seq_cotangent.astype(jnp.float32))
        carry = tuple((total + piece for total, piece in zip(carry, grads[1:])))
        return (carry, (result.astype(jnp.bfloat16), grads[0]))
    initial = tuple((jnp.zeros_like(value) for value in params))
    totals, (output, grad_tokens) = lax.scan(one_sequence, initial, (tokens, block_ids, cotangent))
    return (output, grad_tokens, totals[0], totals[1], totals[2], totals[3], totals[4], totals[5], totals[6], totals[7], totals[8], totals[9], totals[10])
```

```python
import jax
import jax.numpy as jnp
from jax import lax
from jax.sharding import Mesh, PartitionSpec as P

HQ = 4
WINDOW = 512
BLOCK = 256


epsilon = 1e-06
bf16 = jnp.bfloat16
f32 = jnp.float32

SEQ = ("far", "near")
DP = ("chip", "core")
SQUARE = ("near", "chip", "core")


def from_behind(shard, by):
    length = lax.axis_size(SEQ)
    pairs = [(i, i + by) for i in range(length) if 0 <= i + by < length]
    return lax.ppermute(shard, SEQ, pairs)


def swap(value, axis):
    return lax.ppermute(value, axis, [(0, 1), (1, 0)])


def diagonal(value):
    return lax.ppermute(value, ("near", "chip"), [(i, 3 - i) for i in range(4)])


def share_square(value):
    return jnp.concatenate(
        [value, swap(value, "chip"), swap(value, "near"), diagonal(value)], axis=0
    )


def sum_square(parts):
    rows = parts.shape[0] // 4
    low = parts.astype(bf16)
    total = parts[:rows]
    total = total + swap(low[rows : 2 * rows], "chip").astype(f32)
    total = total + swap(low[2 * rows : 3 * rows], "near").astype(f32)
    return total + diagonal(low[3 * rows :]).astype(f32)


def in_order(own, other, axis):
    place = lax.axis_index(axis)
    pair = jnp.zeros((2, *own.shape), own.dtype)
    pair = lax.dynamic_update_index_in_dim(pair, own, place, 0)
    return lax.dynamic_update_index_in_dim(pair, other, 1 - place, 0)


def gather_pair(value, axis):
    return in_order(value, swap(value, axis), axis)


def gather_rows(weight):
    pair = gather_pair(weight, "chip")
    both = gather_pair(pair, "core")
    return both.transpose(1, 0, 2, 3).reshape(-1, weight.shape[1])


def add_all(value):
    for axis in ("core", "chip", "near", "far"):
        size, step = lax.axis_size(axis), 1
        while step < size:
            value = value + lax.ppermute(value, axis, [(i, i ^ step) for i in range(size)])
            step *= 2
    return value


def rms_scale(vector, gain):
    return vector * lax.rsqrt(jnp.mean(vector * vector, axis=-1, keepdims=True) + epsilon) * gain


def rotate(vector, positions):
    half_width = vector.shape[-1] // 2
    frequency = 10000.0 ** (-jnp.arange(half_width, dtype=jnp.float32) * 2.0 / vector.shape[-1])
    angles = positions.astype(jnp.float32)[:, None] * frequency[None, :]
    cosine = jnp.cos(angles)
    sine_part = jnp.sin(angles)
    front_half = vector[..., :half_width]
    back_half = vector[..., half_width:]
    return jnp.concatenate(
        [front_half * cosine - back_half * sine_part, back_half * cosine + front_half * sine_part],
        axis=-1,
    )


def gated_unit(gate_values, up_values):
    return jax.nn.gelu(gate_values, approximate=True) * up_values


def dot(a, b, dims, dtype=f32):
    return lax.dot_general(a, b, ((dims[0], dims[1]), ((), ())), preferred_element_type=dtype)


def shards(
    tokens,
    block_ids,
    w_qkv,
    w_out,
    w_gate,
    w_up,
    w_down,
    gain_in,
    gain_query,
    gain_key,
    gain_attn,
    gain_pre,
    gain_post,
    cotangent,
):
    seq_count, local_len, model_width = tokens.shape
    row_count = seq_count * local_len
    head_dim = gain_query.shape[0]
    head_count = HQ
    query_width = head_count * head_dim
    key_span = WINDOW + local_len + BLOCK
    steps_behind = WINDOW // local_len
    steps_ahead = BLOCK // local_len
    full_len = block_ids.shape[1]
    far_count = lax.axis_size("far")
    near, chip, core = lax.axis_index("near"), lax.axis_index("chip"), lax.axis_index("core")
    offset = lax.axis_index(SEQ) * local_len
    positions = offset + jnp.arange(local_len, dtype=jnp.int32)
    score_scale = head_dim ** (-0.5)
    ff = w_gate.shape[1]
    part = ff // (far_count * 4)

    weight_qkv = gather_rows(w_qkv)
    weight_out = gather_rows(w_out)

    def chip_columns(weight):
        rows = weight.shape[0]
        split = weight.reshape(rows, far_count, 2, 2, part)
        split = lax.dynamic_index_in_dim(split, near, 2, keepdims=False)
        own = lax.dynamic_index_in_dim(split, chip, 2, keepdims=False).reshape(rows, -1)
        other = lax.dynamic_index_in_dim(split, 1 - chip, 2, keepdims=False).reshape(rows, -1)
        return own, other

    def chip_rows(weight):
        split = weight.reshape(-1, 2, 2, part, weight.shape[1])
        split = lax.dynamic_index_in_dim(split, near, 1, keepdims=False)
        own = lax.dynamic_index_in_dim(split, chip, 1, keepdims=False)
        other = lax.dynamic_index_in_dim(split, 1 - chip, 1, keepdims=False)
        return own.reshape(-1, weight.shape[1]), other.reshape(-1, weight.shape[1])

    def chip_weight(own, other):
        pair = in_order(own, swap(other, "chip"), "chip")
        both = gather_pair(pair, "core")
        return both.transpose(1, 0, 2, 3).reshape(-1, own.shape[1])

    weight_gate = chip_weight(*chip_columns(w_gate))
    weight_up = chip_weight(*chip_columns(w_up))
    weight_down = chip_weight(*chip_rows(w_down))

    tokens_flat = tokens.astype(jnp.float32).reshape(row_count, model_width)
    normed_first, input_back = jax.vjp(rms_scale, tokens_flat, gain_in)
    normed_in = normed_first.astype(bf16)
    projected = jnp.dot(normed_in, weight_qkv, preferred_element_type=f32)

    def query_key(query_raw, key_raw, query_gain, key_gain):
        shaped = query_raw.reshape(seq_count, local_len, head_count, head_dim).transpose(0, 2, 1, 3)
        query_rot = rotate(rms_scale(shaped, query_gain), positions)
        key_rot = rotate(
            rms_scale(key_raw.reshape(seq_count, local_len, head_dim), key_gain), positions
        )
        return (query_rot, key_rot)

    (query_float, key_float), rotate_back = jax.vjp(
        query_key,
        projected[:, :query_width],
        projected[:, query_width : query_width + head_dim],
        gain_query,
        gain_key,
    )
    queries = query_float.astype(bf16)
    local_values = projected[:, query_width + head_dim :].reshape(seq_count, local_len, head_dim)
    key_value = jnp.stack([key_float.astype(bf16), local_values.astype(bf16)], axis=1)
    sections = [from_behind(key_value, distance) for distance in range(steps_behind, 0, -1)]
    sections = (
        sections
        + [key_value]
        + [from_behind(key_value, -distance) for distance in range(1, steps_ahead + 1)]
    )
    extended = jnp.concatenate(sections, axis=2)
    far_keys = extended[:, 0]
    far_values = extended[:, 1]
    padded_ids = jnp.pad(block_ids, ((0, 0), (WINDOW, BLOCK)), constant_values=-1)
    key_ids = lax.dynamic_slice_in_dim(padded_ids, offset, key_span, 1)
    query_ids = lax.dynamic_slice_in_dim(block_ids, offset, local_len, 1)
    key_place = offset - WINDOW + jnp.arange(key_span, dtype=jnp.int32)
    inside = (key_place >= 0) & (key_place < full_len)
    same_block = key_ids[:, None, :] == query_ids[:, :, None]
    near_enough = positions[:, None] - key_place[None, :] <= WINDOW
    earlier_block = (key_ids[:, None, :] < query_ids[:, :, None]) & near_enough[None]
    allowed = (inside[None, None, :] & (same_block | earlier_block))[:, None]

    def score_of(query_values):
        raw_scores = (
            jnp.einsum("shqd,skd->shqk", query_values, far_keys, preferred_element_type=f32)
            * score_scale
        )
        return jnp.where(allowed, raw_scores, -1e30)

    scores = score_of(queries)
    highest = jnp.max(scores, axis=-1, keepdims=True)
    log_total = highest + jnp.log(jnp.sum(jnp.exp(scores - highest), axis=-1, keepdims=True))
    chances = jnp.exp(scores - log_total)
    attended = jnp.einsum(
        "shqk,skd->shqd", chances.astype(bf16), far_values, preferred_element_type=f32
    )
    heads_out = attended.transpose(0, 2, 1, 3).reshape(row_count, query_width).astype(bf16)
    attn_out = jnp.dot(heads_out, weight_out, preferred_element_type=f32)
    normed_attn, attn_back = jax.vjp(rms_scale, attn_out, gain_attn)
    residual = tokens_flat + normed_attn
    normed_second, pre_back = jax.vjp(rms_scale, residual, gain_pre)
    normed_pre = share_square(normed_second.astype(bf16))

    gate_proj = jnp.dot(normed_pre, weight_gate, preferred_element_type=f32)
    up_proj = jnp.dot(normed_pre, weight_up, preferred_element_type=f32)
    activated, gelu_back = jax.vjp(gated_unit, gate_proj, up_proj)
    hidden = activated.astype(bf16)
    down_proj = sum_square(jnp.dot(hidden, weight_down, preferred_element_type=f32))
    normed_down, post_back = jax.vjp(rms_scale, down_proj, gain_post)
    output = (residual + normed_down).astype(bf16).reshape(seq_count, local_len, model_width)

    incoming = cotangent.astype(f32).reshape(row_count, model_width)
    grad_down_proj, grad_gain_post = post_back(incoming)
    down_low = share_square(grad_down_proj.astype(bf16))
    grad_hidden = dot(down_low, weight_down, ((1,), (1,)))
    grad_gate_proj, grad_up_proj = gelu_back(grad_hidden)
    gate_low = grad_gate_proj.astype(bf16)
    up_low = grad_up_proj.astype(bf16)
    grad_normed_pre = sum_square(
        dot(gate_low, weight_gate, ((1,), (1,))) + dot(up_low, weight_up, ((1,), (1,)))
    )

    def both_cores(own, other):
        return jnp.concatenate([own, swap(other, "core")], axis=0)

    all_normed = both_cores(normed_pre, normed_pre)
    all_down = both_cores(down_low, down_low)
    hidden_split = hidden.reshape(-1, far_count, 2, part // 2)
    all_hidden = both_cores(
        lax.dynamic_index_in_dim(hidden_split, core, 2, keepdims=False),
        lax.dynamic_index_in_dim(hidden_split, 1 - core, 2, keepdims=False),
    ).reshape(all_down.shape[0], -1)
    first = core == 0
    all_gates = both_cores(
        jnp.where(first, gate_low, up_low), jnp.where(first, up_low, gate_low)
    )
    grad_down = dot(all_down, all_hidden, ((0,), (0,)), bf16)
    grad_down = lax.psum_scatter(grad_down, "far", scatter_dimension=0, tiled=True)
    grad_gates = dot(all_gates, all_normed, ((0,), (0,)), bf16)
    grad_gates = lax.psum_scatter(grad_gates, "far", scatter_dimension=0, tiled=True)

    grad_residual_norm, grad_gain_pre = pre_back(grad_normed_pre)
    grad_residual = incoming + grad_residual_norm
    grad_attn_out, grad_gain_attn = attn_back(grad_residual)
    attn_low = grad_attn_out.astype(bf16)
    grad_heads = dot(attn_low, weight_out, ((1,), (1,))).astype(bf16)
    grad_heads = grad_heads.reshape(seq_count, local_len, head_count, head_dim).transpose(
        0, 2, 1, 3
    )
    grad_chances = jnp.einsum("shqd,skd->shqk", grad_heads, far_values, preferred_element_type=f32)
    grad_far_values = jnp.einsum(
        "shqk,shqd->skd", chances.astype(bf16), grad_heads, preferred_element_type=f32
    )
    row_dot = jnp.sum(chances * grad_chances, axis=-1, keepdims=True)
    grad_scores = (chances * (grad_chances - row_dot)).astype(bf16)
    grad_queries = (
        jnp.einsum("shqk,skd->shqd", grad_scores, far_keys, preferred_element_type=f32)
        * score_scale
    )
    grad_far_keys = (
        jnp.einsum("shqk,shqd->skd", grad_scores, queries, preferred_element_type=f32)
        * score_scale
    )
    grad_pair = jnp.stack([grad_far_keys, grad_far_values], axis=1)
    pair_low = grad_pair.astype(bf16)
    summed = grad_pair[:, :, WINDOW : WINDOW + local_len]
    for distance in range(1, steps_behind + 1):
        start_row = (steps_behind - distance) * local_len
        summed = summed + from_behind(
            pair_low[:, :, start_row : start_row + local_len], -distance
        ).astype(f32)
    for distance in range(1, steps_ahead + 1):
        start_row = WINDOW + distance * local_len
        summed = summed + from_behind(
            pair_low[:, :, start_row : start_row + local_len], distance
        ).astype(f32)
    grad_query_raw, grad_key_raw, grad_gain_query, grad_gain_key = rotate_back(
        (grad_queries, summed[:, 0])
    )
    grad_projected = jnp.concatenate(
        [grad_query_raw, grad_key_raw, summed[:, 1].reshape(row_count, head_dim)], axis=1
    ).astype(bf16)
    grad_normed_in = dot(grad_projected, weight_qkv, ((1,), (1,)))
    grad_tokens_norm, grad_gain_in = input_back(grad_normed_in)
    grad_tokens = (grad_residual + grad_tokens_norm).reshape(seq_count, local_len, model_width)

    def by_rows(left):
        split = left.reshape(row_count, 4, -1).transpose(1, 0, 2)
        return jnp.concatenate([split, split], axis=0)

    def by_columns(right):
        split = right.reshape(row_count, far_count, 2, 1, -1)
        split = jnp.broadcast_to(
            split, (row_count, far_count, 2, 4, split.shape[-1])
        ).transpose(2, 3, 0, 1, 4)
        return split.reshape(8, row_count, -1)

    def weight_sum(left, right):
        left = lax.all_to_all(by_rows(left), SQUARE, 0, 0, tiled=True)
        right = lax.all_to_all(by_columns(right), SQUARE, 0, 0, tiled=True)
        left = left.reshape(8 * row_count, -1)
        right = right.reshape(8 * row_count, -1)
        block = right.shape[1] // far_count
        partial = dot(left, right, ((0,), (0,)), bf16)
        partial = partial.reshape(-1, far_count, block).transpose(1, 0, 2)
        return lax.psum_scatter(partial, "far", scatter_dimension=0, tiled=True)[0].astype(f32)

    out_total = weight_sum(heads_out, attn_low)
    qkv_total = weight_sum(normed_in, grad_projected)

    gate_parts = grad_gates.reshape(part, 4, -1).transpose(1, 0, 2)
    gate_parts = lax.all_to_all(gate_parts, DP, 0, 0, tiled=True)
    gate_parts = gate_parts.reshape(2, 2, part, -1).astype(f32)
    gate_total = gate_parts[:, 0].reshape(2 * part, -1).T
    up_total = gate_parts[:, 1].reshape(2 * part, -1).T

    wide = model_width // far_count // 2
    down_parts = grad_down.reshape(2, wide, 4, -1).transpose(0, 2, 1, 3).reshape(8, wide, -1)
    down_parts = lax.all_to_all(down_parts, SQUARE, 0, 0, tiled=True)
    down_parts = down_parts.reshape(8, wide, far_count // 4, part // 2)
    down_total = down_parts.transpose(2, 0, 3, 1).reshape(-1, wide).astype(f32)

    gains = jnp.concatenate(
        [
            grad_gain_in,
            grad_gain_attn,
            grad_gain_pre,
            grad_gain_post,
            grad_gain_query,
            grad_gain_key,
        ]
    )
    gains = add_all(gains)
    gain_totals = [gains[i * model_width : (i + 1) * model_width] for i in range(4)]
    gain_totals += [gains[4 * model_width :][:head_dim], gains[4 * model_width + head_dim :]]
    return (
        output,
        grad_tokens,
        qkv_total,
        out_total,
        gate_total,
        up_total,
        down_total,
        gain_totals[0],
        gain_totals[4],
        gain_totals[5],
        gain_totals[1],
        gain_totals[2],
        gain_totals[3],
    )


def solution(mesh):
    seq, dp = mesh.devices.shape
    parts = Mesh(mesh.devices.reshape(seq // 2, 2, 2, dp // 2), (*SEQ, *DP))
    rows = P(DP, None)
    whole = P(None)
    placed = (P(DP, SEQ, None), P(DP, None), *[rows] * 5, *[whole] * 6, P(DP, SEQ, None))
    return jax.shard_map(
        shards,
        mesh=parts,
        in_specs=placed,
        out_specs=(*[P(DP, SEQ, None)] * 2, *[P(DP, SEQ)] * 5, *[whole] * 6),
        check_vma=False,
    )
```

```python
import functools

import jax
import jax.numpy as jnp
from jax import lax
from jax.experimental import pallas as pl
from jax.experimental.pallas import tpu as pltpu
from jax.sharding import Mesh, PartitionSpec as P

HQ = 4
WINDOW = 512
BLOCK = 256


epsilon = 1e-06
bf16 = jnp.bfloat16
f32 = jnp.float32
ROOT = 0.7978845608028654

SEQ = ("far", "near")
DP = ("chip", "core")
SQUARE = ("near", "chip", "core")

ANYWHERE = pl.BlockSpec(memory_space=pl.ANY)
VECTORS = pl.BlockSpec(memory_space=pltpu.VMEM)
SCALARS = pl.BlockSpec(memory_space=pltpu.SMEM)


def low(*shape):
    return jax.ShapeDtypeStruct(shape, bf16)


def wide(*shape):
    return jax.ShapeDtypeStruct(shape, f32)


def call(kernel, microseconds, out_shape, in_specs, scratch, *args):
    return pl.pallas_call(
        kernel,
        out_shape=out_shape,
        in_specs=in_specs,
        out_specs=jax.tree.map(lambda _: VECTORS, out_shape),
        scratch_shapes=scratch,
        cost_estimate=pl.CostEstimate(
            flops=microseconds * 1_000_000_000, bytes_accessed=1 << 20, transcendentals=0
        ),
        compiler_params=pltpu.CompilerParams(vmem_limit_bytes=48 << 20),
    )(*args)


def steps(total, size):
    return [(first, min(first + size, total)) for first in range(0, total, size)]


NEAR, CHIP, CORE, PARITY, HALF, BIT = range(6)


def slots(place):
    chip, core = place[CHIP], place[CORE]
    return chip * 2 + core, (1 - chip) * 2 + core, chip * 2 + 1 - core, (1 - chip) * 2 + 1 - core


def at(start, size, multiple=16):
    return pl.ds(pl.multiple_of(start, multiple), size)


def begin(pairs, sem):
    copies = [pltpu.make_async_copy(a, b, sem.at[i]) for i, (a, b) in enumerate(pairs)]
    for c in copies:
        c.start()
    return copies


def fetch(place, pieces, target, sem):
    rows = target.shape[0] // 4
    return begin([(p, target.at[at(s * rows, rows)]) for s, p in zip(slots(place), pieces)], sem)


def fetch_gates(place, pieces, target, sem):
    own, core, chip, other = pieces[0], pieces[1], pieces[2:6], pieces[6:10]
    rows = target.shape[1] // 4
    half = rows // 2
    a, b, c, d = (s * rows for s in slots(place))
    pairs = [(own, target.at[:, at(a, rows)]), (core, target.at[:, at(c, rows)])]
    for start, four in ((b, chip), (d, other)):
        for k in range(2):
            pairs.append((four[k], target.at[place[PARITY], at(start + k * half, half)]))
            pairs.append((four[2 + k], target.at[1 - place[PARITY], at(start + k * half, half)]))
    return begin(pairs, sem)


def fetch_downs(place, pieces, target, sem):
    own, core, chip0, chip1, other0, other1 = pieces
    rows, more = target.shape[0] // 4, chip0.shape[0]
    less, parity = rows - more, place[PARITY]
    a, b, c, d = (s * rows for s in slots(place))
    pairs = [(own, target.at[at(a, rows)]), (core, target.at[at(c, rows)])]
    for start, first, second in ((b, chip0, chip1), (d, other0, other1)):
        pairs.append((first, target.at[at(start + parity * less, more)]))
        rest = second.at[at((1 - parity) * (more - less), less)]
        pairs.append((rest, target.at[at(start + (1 - parity) * more, less)]))
    return begin(pairs, sem)


def wait(copies):
    for c in copies:
        c.wait()


def nn(a, b):
    return jnp.dot(a, b, preferred_element_type=f32)


def nt(a, b):
    return lax.dot_general(a, b, (((1,), (1,)), ((), ())), preferred_element_type=f32)


def tn(a, b):
    return lax.dot_general(a, b, (((0,), (0,)), ((), ())), preferred_element_type=f32)


def rms(value, gain):
    return value * lax.rsqrt(jnp.mean(value * value, axis=-1, keepdims=True) + epsilon) * gain


def rms_back(value, gain, grad):
    scale = lax.rsqrt(jnp.mean(value * value, axis=-1, keepdims=True) + epsilon)
    unit = value * scale
    slope = grad * gain
    back = scale * (slope - unit * jnp.mean(slope * unit, axis=-1, keepdims=True))
    return back, jnp.sum(grad * unit, axis=0, keepdims=True)


def turn(value, cosine, sine):
    half = value.shape[-1] // 2
    a, b = value[:, :half], value[:, half:]
    return jnp.concatenate([a * cosine - b * sine, b * cosine + a * sine], axis=-1)


def half_plane(which, rows):
    return pl.ds(pl.multiple_of(which * rows, 128), rows)


def slice_kernel(far, part, place, gate, up, own, other0, other1, source, sem):
    rows, ff = gate.shape
    copies = begin([(w, source.at[i, :, :ff]) for i, w in enumerate((gate, up))], sem)
    near, chip = place[NEAR], place[CHIP]
    block = 48
    half = rows // 2

    def cut(i, which, target, from_row, to_row):
        for z in range(far):
            first, last = z * part, (z + 1) * part
            lo, hi = first // 128 * 128, min(-(-last // 128) * 128, far * part)
            span = -(-(hi - lo) // 128) * 128 + 128
            shift = (z * 3 + near * 2 + which) * part
            coarse = shift // 128 * 128
            x = source[i, from_row, at(lo + coarse, span, 128)]
            x = pltpu.roll(x, (span - (shift - coarse)) % span, 1)[:, : hi - lo]
            if first > lo:
                column = lax.broadcasted_iota(jnp.int32, x.shape, 1)
                x = jnp.where(column < first - lo, target[to_row, lo:hi], x)
            target[to_row, lo:hi] = x

    wait(copies)
    for k, other in enumerate((other0, other1)):

        def send(r, _):
            cut(place[PARITY], 1 - chip, other, at(k * half + r * block, block), at(r * block, block))
            return 0

        lax.fori_loop(0, half // block, send, 0)
    for i in range(2):

        def keep(r, _):
            here = at(r * block, block)
            cut(i, chip, own.at[i], here, here)
            return 0

        lax.fori_loop(0, rows // block, keep, 0)


def chip_columns(place, gate, up, far):
    rows, ff = gate.shape
    part = ff // (4 * far)
    source = -(-ff // 128) * 128 + 768
    return call(
        functools.partial(slice_kernel, far, part),
        6,
        (low(2, rows, ff // 4), low(rows // 2, ff // 4), low(rows // 2, ff // 4)),
        [SCALARS, ANYWHERE, ANYWHERE],
        [pltpu.VMEM((2, rows, source), bf16), pltpu.SemaphoreType.DMA((2,))],
        place,
        gate,
        up,
    )


def key_columns(own, chip, core, other):
    first = own.shape[1] - chip.shape[1]
    return own.at[:, first:], chip, core.at[:, first:], other


def query_columns(own, chip, core, other):
    last = chip.shape[1]
    return own.at[:, :last], chip, core.at[:, :last], other


def keys_kernel(place, own, peer, gain_in, gain_key, table, k0, k1, k2, k3, normed, pair, raw, every, weight, sem):
    copies = fetch(place, key_columns(k0, k1, k2, k3), weight, sem)
    rows, near, width = own.shape[0], place[0], raw.shape[1]
    mine = rms(own[...].astype(f32), gain_in[...]).astype(bf16)
    normed[...] = mine
    every[half_plane(near, rows)] = mine
    every[half_plane(1 - near, rows)] = rms(peer[...].astype(f32), gain_in[...]).astype(bf16)
    wait(copies)
    projected = nn(every[...], weight[...])
    raw[...] = projected[:, :width]
    pair[0] = turn(rms(projected[:, :width], gain_key[...]), table[0], table[1]).astype(bf16)
    pair[1] = projected[:, width:].astype(bf16)


def keys_of(place, own, peer, gain_in, gain_key, table, pieces):
    rows, model = own.shape
    dim = gain_key.shape[1]
    return call(
        keys_kernel,
        2,
        (low(rows, model), low(2, 2 * rows, dim), wide(2 * rows, dim)),
        [SCALARS, *[VECTORS] * 5, *[ANYWHERE] * 4],
        [pltpu.VMEM((2 * rows, model), bf16), pltpu.VMEM((model, 2 * dim), bf16), pltpu.SemaphoreType.DMA((4,))],
        place, own, peer, gain_in, gain_key, table, *pieces,
    )


def queries_kernel(place, normed, gain, table, q0, q1, q2, q3, queries, raw, weight, sem):
    wait(fetch(place, query_columns(q0, q1, q2, q3), weight, sem))
    rows, dim = normed.shape[0], gain.shape[1]
    here = half_plane(place[0], rows)
    cosine, sine = table[0, here], table[1, here]
    for h in range(HQ):
        projected = nn(normed[...], weight[:, h * dim : (h + 1) * dim])
        raw[h * rows : (h + 1) * rows] = projected
        turned = turn(rms(projected, gain[...]), cosine, sine).astype(bf16)
        queries[h * rows : (h + 1) * rows] = turned * jnp.asarray(dim**-0.5, bf16)


def queries_of(place, normed, gain, table, pieces):
    rows, model = normed.shape
    dim = gain.shape[1]
    return call(
        queries_kernel,
        3,
        (low(HQ * rows, dim), wide(HQ * rows, dim)),
        [SCALARS, *[VECTORS] * 3, *[ANYWHERE] * 4],
        [pltpu.VMEM((model, HQ * dim), bf16), pltpu.SemaphoreType.DMA((4,))],
        place, normed, gain, table, *pieces,
    )


def attend_kernel(
    place, queries, kv0, kv1, kv2, kv3, key_ids, query_ids, tokens, gain_attn, gain_pre, o0, o1, o2, o3,
    chances, heads, attn_out, residual, normed_pre, keys, values, weight, sem,
):
    copies = fetch(place, (o0, o1, o2, o3), weight, sem)
    plane, dim = kv0.shape[1], kv0.shape[2]
    for i, kv in enumerate((kv0, kv1, kv2, kv3)):
        keys[i * plane : (i + 1) * plane] = kv[0]
        values[i * plane : (i + 1) * plane] = kv[1]
    rows, span = query_ids.shape[0], key_ids.shape[1]
    row = lax.broadcasted_iota(jnp.int32, (rows, span), 0) + place[0] * rows
    column = lax.broadcasted_iota(jnp.int32, (rows, span), 1)
    same = key_ids[...] == query_ids[...]
    allowed = same | ((key_ids[...] < query_ids[...]) & (column >= row))
    for h in range(HQ):
        here = slice(h * rows, (h + 1) * rows)
        scores = jnp.where(allowed, nt(queries[here], keys[...]), -1e30)
        grown = jnp.exp(scores - jnp.max(scores, axis=-1, keepdims=True))
        share = grown / jnp.sum(grown, axis=-1, keepdims=True)
        chances[here] = share
        heads[:, h * dim : (h + 1) * dim] = nn(share.astype(bf16), values[...]).astype(bf16)
    wait(copies)
    out = nn(heads[...], weight[...])
    attn_out[...] = out
    total = tokens[...].astype(f32) + rms(out, gain_attn[...])
    residual[...] = total
    normed_pre[...] = rms(total, gain_pre[...]).astype(bf16)


def attend(place, queries, planes, key_ids, query_ids, tokens, gain_attn, gain_pre, pieces):
    rows, model = tokens.shape
    dim, span = queries.shape[1], key_ids.shape[1]
    return call(
        attend_kernel,
        5,
        (wide(HQ * rows, span), low(rows, HQ * dim), wide(rows, model), wide(rows, model), low(rows, model)),
        [SCALARS, *[VECTORS] * 10, *[ANYWHERE] * 4],
        [
            pltpu.VMEM((span, dim), bf16),
            pltpu.VMEM((span, dim), bf16),
            pltpu.VMEM((HQ * dim, model), bf16),
            pltpu.SemaphoreType.DMA((4,)),
        ],
        place, queries, *planes, key_ids, query_ids, tokens, gain_attn, gain_pre, *pieces,
    )


def gated(gate, up):
    square = gate * gate
    wave = jnp.tanh(ROOT * gate * (1.0 + 0.044715 * square))
    half = 0.5 * (1.0 + wave)
    value = gate * half
    bend = half + 0.5 * ROOT * gate * (1.0 - wave * wave) * (1.0 + 3.0 * 0.044715 * square)
    return (value * up).astype(bf16), (bend * up).astype(bf16), value.astype(bf16)


def forward_kernel(place, x0, x1, x2, x3, *refs):
    gates, downs = refs[:10], refs[10:16]
    whole, hidden, slope, gelu, total, p1, p2, p3 = refs[16:24]
    w_gates, w_down, sem, late_sem = refs[24:]
    copies = fetch_gates(place, gates, w_gates, sem)
    late = fetch_downs(place, downs, w_down, late_sem)
    rows = x0.shape[0]
    for i, x in enumerate((x0, x1, x2, x3)):
        whole[i * rows : (i + 1) * rows] = x[...]
    wait(copies)
    for first, last in steps(w_down.shape[0], 256):
        gate = nn(whole[...], w_gates[0, :, first:last])
        up = nn(whole[...], w_gates[1, :, first:last])
        hidden[:, first:last], slope[:, first:last], gelu[:, first:last] = gated(gate, up)
    wait(late)
    for first, last in steps(w_down.shape[1], 384):
        part = nn(hidden[...], w_down[:, first:last])
        total[:, first:last] = part[:rows]
        for i, p in enumerate((p1, p2, p3)):
            p[:, first:last] = part[(i + 1) * rows : (i + 2) * rows].astype(bf16)


def weight_room(model, ff):
    return [
        pltpu.VMEM((2, model, ff), bf16),
        pltpu.VMEM((ff, model), bf16),
        pltpu.SemaphoreType.DMA((10,)),
        pltpu.SemaphoreType.DMA((6,)),
    ]


def forward(place, blocks, gates, downs):
    rows, model = blocks[0].shape
    ff = gates[0].shape[2]
    return call(
        forward_kernel,
        13,
        (low(4 * rows, model), *[low(4 * rows, ff)] * 3, wide(rows, model), *[low(rows, model)] * 3),
        [SCALARS, *[VECTORS] * 4, *[ANYWHERE] * 16],
        weight_room(model, ff),
        place, *blocks, *gates, *downs,
    )


def backward_kernel(place, x0, x1, x2, x3, slope, gelu, *refs):
    gates, downs = refs[:10], refs[10:16]
    whole, gate_low, up_low, total, p1, p2, p3 = refs[16:23]
    w_gates, w_down, late_sem, sem = refs[23:]
    copies = fetch_downs(place, downs, w_down, sem)
    late = fetch_gates(place, gates, w_gates, late_sem)
    rows = x0.shape[0]
    for i, x in enumerate((x0, x1, x2, x3)):
        whole[i * rows : (i + 1) * rows] = x[...]
    wait(copies)
    for first, last in steps(w_down.shape[0], 256):
        back = nt(whole[...], w_down[first:last])
        gate_low[:, first:last] = (back * slope[:, first:last].astype(f32)).astype(bf16)
        up_low[:, first:last] = (back * gelu[:, first:last].astype(f32)).astype(bf16)
    wait(late)
    for first, last in steps(w_down.shape[1], 384):
        part = nt(gate_low[...], w_gates[0, first:last]) + nt(up_low[...], w_gates[1, first:last])
        total[:, first:last] = part[:rows]
        for i, p in enumerate((p1, p2, p3)):
            p[:, first:last] = part[(i + 1) * rows : (i + 2) * rows].astype(bf16)


def backward(place, blocks, slope, gelu, gates, downs):
    rows, model = blocks[0].shape
    ff = gates[0].shape[2]
    return call(
        backward_kernel,
        15,
        (low(4 * rows, model), *[low(4 * rows, ff)] * 2, wide(rows, model), *[low(rows, model)] * 3),
        [SCALARS, *[VECTORS] * 6, *[ANYWHERE] * 16],
        weight_room(model, ff),
        place, *blocks, slope, gelu, *gates, *downs,
    )


def far_kernel(window, place, n0, n1, n2, n3, *refs):
    gates, (hidden, slope, gelu, w_gates, tokens, room, sem) = refs[:10], refs[10:]
    start, width = window
    copies = fetch_gates(place, gates, w_gates, sem)
    rows = n0.shape[0]
    for i, n in enumerate((n0, n1, n2, n3)):
        tokens[i * rows : (i + 1) * rows] = n[...]
    wait(copies)
    for first, last in steps(hidden.shape[1], 256):
        gate = nn(tokens[...], w_gates[0, :, first:last])
        up = nn(tokens[...], w_gates[1, :, first:last])
        hidden[:, first:last], room[0, :, first:last], room[1, :, first:last] = gated(gate, up)
    here = at(place[HALF] * start, width, 128)
    slope[...] = room[0, :, here]
    gelu[...] = room[1, :, here]


def window_of(ff):
    start = ff // 2 // 128 * 128
    return start, ff - start


def far_hidden(place, far_normed, gates):
    rows, model = far_normed[0].shape
    ff = gates[0].shape[2]
    start, width = window_of(ff)
    return call(
        functools.partial(far_kernel, (start, width)),
        11,
        (low(4 * rows, ff), low(4 * rows, width), low(4 * rows, width)),
        [SCALARS, *[VECTORS] * 4, *[ANYWHERE] * 10],
        [
            pltpu.VMEM((2, model, ff), bf16),
            pltpu.VMEM((4 * rows, model), bf16),
            pltpu.VMEM((2, 4 * rows, ff), bf16),
            pltpu.SemaphoreType.DMA((10,)),
        ],
        place, *far_normed, *gates,
    )


def weights_kernel(
    window, place, normed, down, hidden, gate_low, up_low, n0, n1, n2, n3, d0, d1, d2, d3, far_hiddens, slope, gelu, *refs
):
    downs = refs[:6]
    keep_gates, send_gates, keep_down, send_down = refs[6:10]
    w_down, hiddens, grads, tokens, backs, sem = refs[10:]
    start, width = window
    half, core, bit = place[HALF], place[CORE], place[BIT]
    columns = at(half * start, width, 128)
    copies = fetch_downs(place, downs, w_down, sem)
    rows, own = n0.shape[0], normed.shape[0]
    kept = hidden.shape[1] // 2
    hiddens[:, :own] = hidden[...].T
    grads[core, :, :own] = gate_low[:, columns].T
    grads[1 - core, :, :own] = up_low[:, columns].T
    hiddens[:, own:] = far_hiddens[...].T
    tokens[:own] = normed[...]
    backs[:own] = down[...]
    for i, (n, d) in enumerate(zip((n0, n1, n2, n3), (d0, d1, d2, d3))):
        here = slice(own + i * rows, own + (i + 1) * rows)
        tokens[here] = n[...]
        backs[here] = d[...]
    wait(copies)
    for first, last in steps(width, 256):
        back = nt(backs[own:], w_down[at(half * start + first, last - first)])
        c = slice(first, last)
        grads[core, c, own:] = (back * slope[:, c].astype(f32)).astype(bf16).T
        grads[1 - core, c, own:] = (back * gelu[:, c].astype(f32)).astype(bf16).T
    part = kept // 2
    for i in range(2):
        r = at(half * (kept - start) + i * part, part)
        slot = i ^ bit
        keep_gates[slot] = nn(grads[0, r], tokens[...]).astype(bf16)
        send_gates[slot] = nn(grads[1, r], tokens[...]).astype(bf16)
    span = keep_down.shape[2]
    columns = at(half * (backs.shape[1] - span), span, 128)
    for i in range(4):
        result = nn(hiddens[i * part : (i + 1) * part], backs[:, columns]).astype(bf16)

        @pl.when(core == i % 2)
        def _():
            keep_down[i // 2] = result

        @pl.when(core != i % 2)
        def _():
            send_down[i // 2] = result


def weight_grads(place, normed, down, hidden, gate_low, up_low, far_normed, far_down, far_kept, downs):
    own, model = normed.shape
    ff = hidden.shape[1]
    start, width = window_of(ff)
    part = ff // 4
    span = -(-model // 256) * 128
    return call(
        functools.partial(weights_kernel, (start, width)),
        16,
        (low(2, part, model), low(2, part, model), low(2, part, span), low(2, part, span)),
        [SCALARS, *[VECTORS] * 16, *[ANYWHERE] * 6],
        [
            pltpu.VMEM((ff, model), bf16),
            pltpu.VMEM((ff, 2 * own), bf16),
            pltpu.VMEM((2, width, 2 * own), bf16),
            pltpu.VMEM((2 * own, model), bf16),
            pltpu.VMEM((2 * own, model), bf16),
            pltpu.SemaphoreType.DMA((6,)),
        ],
        place, normed, down, hidden, gate_low, up_low, *far_normed, *far_down, *far_kept, *downs,
    )


def turning_kernel(own, r1, r2, r3, residual, cotangent, gain, output, grad, grad_gain):
    down = own[...] + r1[...].astype(f32) + r2[...].astype(f32) + r3[...].astype(f32)
    output[...] = (residual[...] + rms(down, gain[...])).astype(bf16)
    back, grad_gain[...] = rms_back(down, gain[...], cotangent[...].astype(f32))
    grad[...] = back.astype(bf16)


def turning(parts, residual, cotangent, gain):
    rows, model = residual.shape
    return call(
        turning_kernel,
        1,
        (low(rows, model), low(rows, model), wide(1, model)),
        [VECTORS] * 7,
        [],
        *parts, residual, cotangent, gain,
    )


def cores_kernel(place, keep_gates, got_gates, keep_down, got_down, gates, send_gates, down, send_down, turned):
    gates[...] = keep_gates[0].astype(f32) + got_gates[0].astype(f32)
    send_gates[...] = (keep_gates[1].astype(f32) + got_gates[1].astype(f32)).astype(bf16)
    part = down.shape[1]
    first = place[HALF] * (turned.shape[1] - 2 * part)
    for i in range(2):
        turned[i] = (keep_down[i].astype(f32) + got_down[i].astype(f32)).T
        for target, bit in ((down, place[BIT]), (send_down, 1 - place[BIT])):
            target[i] = turned[i, at(first + bit * part, part)].astype(target.dtype)


def add_cores(place, keep_gates, got_gates, keep_down, got_down):
    part, model = keep_gates.shape[1:]
    return call(
        cores_kernel,
        4,
        (wide(part, model), low(part, model), wide(2, model // 4, part), low(2, model // 4, part)),
        [SCALARS, *[VECTORS] * 4],
        [pltpu.VMEM((2, keep_down.shape[2], part), f32)],
        place, keep_gates, got_gates, keep_down, got_down,
    )


def gates_kernel(gates, got, total):
    turned = (gates[...] + got[...].astype(f32)).T.astype(bf16)
    part = total.shape[1]
    for i in range(4):
        total[i] = turned[i * part : (i + 1) * part]


def add_gates(gates, got):
    part, model = gates.shape
    return call(gates_kernel, 3, low(4, model // 4, part), [VECTORS] * 2, [], gates, got)


def down_kernel(down, got, total):
    total[...] = (down[...] + got[...].astype(f32)).astype(bf16)


def add_down(down, got):
    return call(down_kernel, 1, low(*down.shape), [VECTORS] * 2, [], down, got)


def attend_back_kernel(
    place, own, r1, r2, r3, residual, attn_out, cotangent, gain_pre, gain_attn, chances, queries, raw, table, gain_query,
    kv0, kv1, kv2, kv3, o0, o1, o2, o3,
    grad_residual, attn_low, grad_gains, grad_gain_query, grad_projected, g0, g1, g2, g3,
    keys, values, heads, dull, weight, sem,
):
    copies = fetch(place, (o0, o1, o2, o3), weight, sem)
    plane, dim = kv0.shape[1], kv0.shape[2]
    for i, kv in enumerate((kv0, kv1, kv2, kv3)):
        keys[i * plane : (i + 1) * plane] = kv[0]
        values[i * plane : (i + 1) * plane] = kv[1]
    normed = own[...] + r1[...].astype(f32) + r2[...].astype(f32) + r3[...].astype(f32)
    back, grad_gains[0:1] = rms_back(residual[...], gain_pre[...], normed)
    total = cotangent[...].astype(f32) + back
    grad_residual[...] = total
    back, grad_gains[1:2] = rms_back(attn_out[...], gain_attn[...], total)
    attn_low[...] = back.astype(bf16)
    wait(copies)
    rows = own.shape[0]
    here = half_plane(place[0], rows)
    cosine, sine = table[0, here], table[1, here]
    gain_total = jnp.zeros_like(grad_gain_query)
    for h in range(HQ):
        r = slice(h * rows, (h + 1) * rows)
        heads[r] = nt(attn_low[...], weight[h * dim : (h + 1) * dim]).astype(bf16)
        share = chances[r]
        grad_share = nt(heads[r], values[...])
        mean = jnp.sum(share * grad_share, axis=-1, keepdims=True)
        grad_scores = (share * (grad_share - mean)).astype(bf16)
        dull[r] = grad_scores
        turned = nn(grad_scores, keys[...]) * (dim**-0.5)
        back, gain_part = rms_back(raw[r], gain_query[...], turn(turned, cosine, -sine))
        gain_total = gain_total + gain_part
        grad_projected[:, h * dim : (h + 1) * dim] = back.astype(bf16)
    grad_gain_query[...] = gain_total
    for i, g in enumerate((g0, g1, g2, g3)):
        c = slice(i * plane, (i + 1) * plane)
        g[0] = tn(dull[:, c], queries[...]).astype(g.dtype)
        g[1] = tn(chances[:, c].astype(bf16), heads[...]).astype(g.dtype)


def attend_back(place, parts, residual, attn_out, cotangent, gain_pre, gain_attn, chances, queries, raw, table, gain_query, planes, pieces):
    rows, model = residual.shape
    dim, span = queries.shape[1], chances.shape[1]
    plane = planes[0].shape[1]
    sent = low(2, plane, dim)
    return call(
        attend_back_kernel,
        8,
        (
            wide(rows, model), low(rows, model), wide(2, model), wide(1, dim), low(rows, HQ * dim),
            sent, sent, wide(2, plane, dim), sent,
        ),
        [SCALARS, *[VECTORS] * 18, *[ANYWHERE] * 4],
        [
            pltpu.VMEM((span, dim), bf16),
            pltpu.VMEM((span, dim), bf16),
            pltpu.VMEM((HQ * rows, dim), bf16),
            pltpu.VMEM((HQ * rows, span), bf16),
            pltpu.VMEM((HQ * dim, model), bf16),
            pltpu.SemaphoreType.DMA((4,)),
        ],
        place, *parts, residual, attn_out, cotangent, gain_pre, gain_attn, chances, queries, raw, table, gain_query, *planes, *pieces,
    )


def queries_back_kernel(place, grad, q0, q1, q2, q3, result, weight, sem):
    wait(fetch(place, query_columns(q0, q1, q2, q3), weight, sem))
    result[...] = nt(grad[...], weight[...])


def queries_back(place, grad, pieces):
    rows, width = grad.shape
    model = pieces[1].shape[0] * 4
    return call(
        queries_back_kernel,
        3,
        wide(rows, model),
        [SCALARS, VECTORS, *[ANYWHERE] * 4],
        [pltpu.VMEM((model, width), bf16), pltpu.SemaphoreType.DMA((4,))],
        place, grad, *pieces,
    )


def columns_of(value, near, blocks, size):
    return [value[:, (2 * f + near) * size : (2 * f + near + 1) * size] for f in blocks]


def exchange_kernel(far, early, heads, normed, grad_queries, attn_low, result):
    rows = heads.shape[0]
    head, unit = heads.shape[1] // 4, normed.shape[1] // 4
    block, size = (heads.shape[1] * 3 // 2) // (2 * far), attn_low.shape[1] // (2 * far)
    first, second = head + early * block, head + early * block + far * size
    for near in range(2):
        left = jnp.concatenate(columns_of(grad_queries[...], near, range(early), block), axis=1)
        right = jnp.concatenate(columns_of(attn_low[...], near, range(far), size), axis=1)
        for i in range(4):
            n = near * 4 + i
            result[n, :, :head] = heads[:, i * head : (i + 1) * head]
            result[n, :, head:first] = left
            result[n, :, first:second] = right
            result[n, :, second : second + unit] = normed[:, i * unit : (i + 1) * unit]
            result[n, :, second + unit :] = jnp.zeros((rows, result.shape[2] - second - unit), bf16)


def exchanged(far, early, heads, normed, grad_queries, attn_low):
    rows, width = heads.shape
    block = width * 3 // 2 // (2 * far)
    size = width // 4 + early * block + (attn_low.shape[1] + normed.shape[1] // 2) // 2
    size = -(-size // 128) * 128
    return call(
        functools.partial(exchange_kernel, far, early),
        3,
        low(8, rows, size),
        [VECTORS] * 4,
        [],
        heads, normed, grad_queries, attn_low,
    )


def first_products_kernel(far, early, place, got, out_keep, out_send, queries):
    head = out_keep.shape[1]
    width = queries.shape[1]
    size = 2 * out_keep.shape[0]
    rows = got.shape[0] * got.shape[1]

    def part(first, count):
        return got[:, :, first : first + count].reshape(rows, count)

    heads = part(0, head)
    out = tn(part(head + width, size), heads)
    half = size // 2
    for i in range(2):

        @pl.when(place[HALF] == i)
        def _():
            out_keep[...] = out[i * half : (i + 1) * half]
            out_send[...] = out[(1 - i) * half : (2 - i) * half].astype(bf16)

    queries[...] = tn(part(head + width + size, queries.shape[0]), part(head, width))


def first_products(far, early, place, got, head, model, block):
    half = model // 4
    return call(
        functools.partial(first_products_kernel, far, early),
        4,
        (wide(half, head), low(half, head), wide(model // 4, early * block)),
        [SCALARS, VECTORS],
        [],
        place, got,
    )


def last_products_kernel(first, place, got, late, queries, keep, send, gains, room):
    rows = got.shape[1]
    model = queries.shape[0]
    left = got[:, :, first : first + model].reshape(8 * rows, model)
    width, early = late.shape[2], queries.shape[1]
    room[:, :early] = queries[...]
    room[:, early:] = tn(left, late[:, :rows].reshape(8 * rows, width))
    half = keep.shape[1]
    for i in range(2):

        @pl.when(place[HALF] == i)
        def _():
            keep[...] = room[:, i * half : (i + 1) * half]
            send[...] = room[:, (1 - i) * half : (2 - i) * half].astype(bf16)

    gains[...] = jnp.sum(late[:, rows:].astype(f32), axis=0)


def last_products(first, place, got, late, queries):
    unit, early = queries.shape
    rows, width = late.shape[1] - got.shape[1], late.shape[2]
    half = (early + width) // 2
    return call(
        functools.partial(last_products_kernel, first),
        3,
        (wide(unit, half), low(unit, half), wide(rows, width)),
        [SCALARS, *[VECTORS] * 3],
        [pltpu.VMEM((unit, early + width), f32)],
        place, got, late, queries,
    )


def down_rows_kernel(part, parts, result):
    for i in range(4):
        for z in range(parts.shape[2] // part):
            first = (4 * z + i) * part
            result[:, first : first + part] = parts[i, :, z * part : (z + 1) * part].astype(f32)


def down_rows(parts, part):
    _, columns, rows = parts.shape
    return call(functools.partial(down_rows_kernel, part), 2, wide(columns, 4 * rows), [VECTORS], [], parts)


def keys_back_kernel(
    early, place, total, received, raw, table, gain_key, partial, grad_residual, tokens, gain_in, grad_queries, grad_gains,
    grad_gain_post, grad_gain_query, k0, k1, k2, k3, grad_tokens, late, grad_projected, gains, weight, sem,
):
    copies = fetch(place, key_columns(k0, k1, k2, k3), weight, sem)
    rows, dim = tokens.shape[0], raw.shape[1]
    here = half_plane(place[0], rows)
    keys = total[0, here] + received[0].astype(f32)
    values = total[1, here] + received[1].astype(f32)
    back, grad_gain_key = rms_back(raw[here], gain_key[...], turn(keys, table[0, here], -table[1, here]))
    grad_projected[:, :dim] = back.astype(bf16)
    grad_projected[:, dim:] = values.astype(bf16)
    wait(copies)
    normed = partial[...] + nt(grad_projected[...], weight[...])
    back, grad_gain_in = rms_back(tokens[...].astype(f32), gain_in[...], normed)
    grad_tokens[...] = grad_residual[...] + back
    model, width = tokens.shape[1], late.shape[2]
    gains[...] = jnp.zeros_like(gains)
    gains[:, :model] = grad_gain_in
    for i in range(2):
        gains[:, (i + 1) * model : (i + 2) * model] = grad_gains[i : i + 1]
    gains[:, 3 * model : 4 * model] = grad_gain_post[...]
    gains[:, 4 * model : 4 * model + dim] = grad_gain_query[...]
    gains[:, 4 * model + dim : 4 * model + 2 * dim] = grad_gain_key
    more = late.shape[1] - rows
    block = grad_queries.shape[1] * 3 // 2 // (2 * early[0])
    every = jnp.concatenate([grad_queries[:, early[1] * 2 * block :], grad_projected[...]], axis=1)
    extra = jnp.concatenate([gains[:, i * width : (i + 1) * width] for i in range(more)], axis=0).astype(bf16)
    for near in range(2):
        mine = jnp.concatenate(columns_of(every, near, range(early[0] - early[1]), block), axis=1)
        for i in range(4):
            late[near * 4 + i, :rows] = mine
            late[near * 4 + i, rows:] = extra


def keys_back(
    far, early, place, total, received, raw, table, gain_key, partial, grad_residual, tokens, gain_in, grad_queries, grad_gains,
    grad_gain_post, grad_gain_query, pieces,
):
    rows, model = tokens.shape
    dim = raw.shape[1]
    width = (far - early) * (HQ + 2) * dim // (2 * far)
    more = -(-(4 * model + 2 * dim) // (16 * width)) * 16
    return call(
        functools.partial(keys_back_kernel, (far, early)),
        4,
        (wide(rows, model), low(8, rows + more, width)),
        [SCALARS, *[VECTORS] * 13, *[ANYWHERE] * 4],
        [
            pltpu.VMEM((rows, 2 * dim), bf16),
            pltpu.VMEM((1, more * width), f32),
            pltpu.VMEM((model, 2 * dim), bf16),
            pltpu.SemaphoreType.DMA((4,)),
        ],
        place, total, received, raw, table, gain_key, partial, grad_residual, tokens, gain_in, grad_queries, grad_gains,
        grad_gain_post, grad_gain_query, *pieces,
    )


def shift(value, by):
    length = lax.axis_size("far")
    pairs = [(i, i + by) for i in range(length) if 0 <= i + by < length]
    return lax.ppermute(value, "far", pairs)


def swap(value, axis):
    return lax.ppermute(value, axis, [(0, 1), (1, 0)])


def diagonal(value):
    return lax.ppermute(value, ("near", "chip"), [(i, 3 - i) for i in range(4)])


def around(values):
    return swap(values[0], "chip"), swap(values[1], "near"), diagonal(values[2])


def far_swap(value, step):
    return lax.ppermute(value, "far", [(i, i ^ step) for i in range(lax.axis_size("far"))])


def after(value, *others):
    return lax.optimization_barrier((value, others))[0]


def halving(value, axis, steps):
    place = lax.axis_index("far")
    for step in steps:
        shape = (*value.shape[:axis], 2, value.shape[axis] // 2, *value.shape[axis + 1 :])
        value = value.reshape(shape)
        bit = place // step % 2
        mine = lax.dynamic_index_in_dim(value, bit, axis, keepdims=False)
        other = lax.dynamic_index_in_dim(value, 1 - bit, axis, keepdims=False)
        value = mine + far_swap(other.astype(bf16), step).astype(f32)
    return value


def add_planes(value):
    step = 1
    while step < lax.axis_size("far"):
        value = value + far_swap(value, step)
        step *= 2
    return value


def shards(
    tokens,
    block_ids,
    w_qkv,
    w_out,
    w_gate,
    w_up,
    w_down,
    gain_in,
    gain_query,
    gain_key,
    gain_attn,
    gain_pre,
    gain_post,
    cotangent,
):
    seq_count, rows, model = tokens.shape
    dim = gain_query.shape[0]
    query_width = HQ * dim
    plane = 2 * rows
    span = WINDOW + plane + BLOCK
    full_len = block_ids.shape[1]
    far_count = lax.axis_size("far")
    near, chip, core = lax.axis_index("near"), lax.axis_index("chip"), lax.axis_index("core")
    far = lax.axis_index("far")
    half_far = far_count // 2
    far_bits = [1 << i for i in reversed(range(far_count.bit_length() - 1))]
    low_bits = far_bits[1:]
    half = far // half_far
    bit = far // low_bits[0] % 2
    place = jnp.stack([near, chip, core, far % 2, half, bit]).astype(jnp.int32)
    start = far * plane
    ff = w_gate.shape[1]
    part = ff // (far_count * 4)
    tokens = tokens.reshape(rows, model)
    cotangent = cotangent.reshape(rows, model)
    gain_in, gain_query, gain_key, gain_attn, gain_pre, gain_post = (
        g.reshape(1, -1) for g in (gain_in, gain_query, gain_key, gain_attn, gain_pre, gain_post)
    )

    w_key, w_query = w_qkv[:, query_width:], w_qkv[:, :query_width]
    key_chip, query_chip, peer_tokens = swap(w_key, "chip"), swap(w_query, "chip"), swap(tokens, "near")
    gates_own, *gates_other = chip_columns(place, w_gate, w_up, far_count)
    split = lax.dynamic_index_in_dim(w_down.reshape(-1, 2, 2, part, model), near, 1, keepdims=False)
    down_own = lax.dynamic_index_in_dim(split, chip, 1, keepdims=False).reshape(-1, model)
    other_rows = lax.dynamic_index_in_dim(split, 1 - chip, 1, keepdims=False).reshape(-1, model)
    more = -(-other_rows.shape[0] // 32) * 16
    down_other = lax.dynamic_slice_in_dim(other_rows, far % 2 * (other_rows.shape[0] - more), more, 0)
    qkv_core, out_core = swap(w_qkv, "core"), swap(w_out, "core")
    gates_core, down_core = swap(gates_own, "core"), swap(down_own, "core")
    key_pieces = w_qkv, key_chip, qkv_core, swap(key_chip, "core")

    frequency = 10000.0 ** (-jnp.arange(dim // 2, dtype=f32) * 2.0 / dim)
    angles = (start + jnp.arange(plane)).astype(f32)[:, None] * frequency[None, :]
    table = jnp.stack([jnp.cos(angles), jnp.sin(angles)])
    normed_in, pair, raw_keys = keys_of(
        place, after(tokens, gates_core, down_core, out_core), peer_tokens, gain_in, gain_key, table, key_pieces
    )
    query_chip = after(query_chip, pair)
    query_pieces = w_qkv, query_chip, qkv_core, swap(query_chip, "core")
    out_chip = swap(after(w_out, key_chip), "chip")
    first = swap(after(gates_other[0], query_chip), "chip")
    second = swap(after(gates_other[1], out_chip), "chip")
    down_chip = swap(after(down_other, first), "chip")
    out_pieces = w_out, out_chip, out_core, swap(out_chip, "core")
    first_rest, second_rest, down_rest = far_swap(first, 1), far_swap(second, 1), far_swap(down_chip, 1)
    four = first, second, first_rest, second_rest
    gates = gates_own, gates_core, *four, *(swap(p, "core") for p in four)
    downs = down_own, down_core, down_chip, down_rest, swap(down_chip, "core"), swap(down_rest, "core")

    padded = jnp.pad(block_ids, ((0, 0), (WINDOW, BLOCK)), constant_values=1 << 30)
    key_ids = lax.dynamic_slice_in_dim(padded, start, span, 1)
    query_ids = lax.dynamic_slice_in_dim(block_ids, start + near * rows, rows, 1).reshape(rows, 1)

    planes = (shift(pair, 2), shift(pair, 1), pair, shift(pair, -1))
    queries, raw_queries = queries_of(place, normed_in, gain_query, table, query_pieces)
    chances, heads_out, attn_out, residual, normed_pre = attend(
        place, after(queries, first), planes, key_ids, query_ids, tokens, gain_attn, gain_pre, out_pieces
    )

    far_normed = far_swap(after(normed_pre, first_rest, second), half_far)
    blocks = (normed_pre, *around([normed_pre] * 3))
    all_normed, hidden, slope, gelu, own, *sent = forward(place, after(blocks, far_normed), gates, downs)
    far_normed = after(far_normed, second_rest)
    far_normed = (far_normed, *around([far_normed] * 3))
    sent = after(sent, *far_normed)
    output, grad_down_proj, grad_gain_post = turning((own, *around(sent)), residual, cotangent, gain_post)
    far_down = far_swap(grad_down_proj, half_far)
    blocks = (grad_down_proj, *around([grad_down_proj] * 3))
    far_kept = far_hidden(place, after(far_normed, grad_down_proj), gates)
    blocks = after(blocks, far_down, *far_kept)
    all_down, gate_low, up_low, own, *sent = backward(place, blocks, slope, gelu, gates, downs)
    far_down = (far_down, *around([far_down] * 3))
    sent = after(sent, *far_down)
    parts = (own, *around(sent))
    keep_gates, send_gates, keep_down, send_down = weight_grads(
        place, all_normed, all_down, hidden, after(gate_low, *sent), up_low, far_normed, far_down, far_kept, downs
    )
    (
        grad_residual, attn_low, grad_gains, grad_gain_query, grad_queries, *sent,
    ) = attend_back(
        place, after(parts, keep_down), residual, attn_out, cotangent, gain_pre, gain_attn, chances, queries, raw_queries, table, gain_query,
        planes, out_pieces,
    )
    total = sent[2] + shift(sent[0], -2).astype(f32)
    total = total + shift(sent[1], -1).astype(f32) + shift(sent[3], 1).astype(f32)
    received = swap(
        lax.dynamic_slice_in_dim(total, (1 - near) * rows, rows, 1).astype(bf16), "near"
    )
    partial = queries_back(place, grad_queries, query_pieces)

    send_gates, send_down = after((send_gates, send_down), grad_queries)
    got_gates, got_down = swap(send_gates, "core"), swap(send_down, "core")
    grad_gates, send_gates, grad_down, send_down = add_cores(place, keep_gates, got_gates, keep_down, got_down)
    send_gates, send_down, total = after((send_gates, send_down, total))
    got_down, got_gates = far_swap(send_down, low_bits[0]), far_swap(send_gates, low_bits[0])
    grad_down, grad_gates = add_down(grad_down, got_down), add_gates(grad_gates, got_gates)

    block = w_qkv.shape[1] // far_count // 2
    early = query_width // (2 * block)
    got = exchanged(far_count, early, heads_out, normed_in, grad_queries, attn_low)
    got = lax.all_to_all(got, SQUARE, 0, 0, tiled=True)
    out_keep, out_send, query_part = first_products(far_count, early, place, got, query_width // 4, model, block)
    out_total = halving(out_keep + far_swap(out_send, half_far).astype(f32), 0, low_bits).T

    grad_tokens, late = keys_back(
        far_count, early, place, total, received, raw_keys, table, gain_key, partial, grad_residual, tokens, gain_in,
        grad_queries, grad_gains, grad_gain_post, grad_gain_query, key_pieces,
    )
    late = lax.all_to_all(after(late, got, got_down), SQUARE, 0, 0, tiled=True)
    keep, send, gains = last_products(query_width // 4 + early * block + model // 2, place, got, late, query_part)
    qkv_total = halving(keep + far_swap(send, half_far).astype(f32), 1, low_bits)
    gains = add_planes(gains.reshape(-1))

    columns = model // far_count // 2
    down_parts = halving(grad_down, 1, low_bits[1:]).astype(bf16).reshape(2, 2, columns, -1)
    down_parts = down_parts.transpose(1, 0, 2, 3).reshape(4, columns, -1)
    down_parts = lax.all_to_all(down_parts, ("near", "chip"), 0, 0, tiled=True)
    down_total = down_rows(down_parts, part).T

    gate_parts = halving(grad_gates, 2, low_bits[1:]).astype(bf16)
    gate_parts = lax.all_to_all(gate_parts, DP, 0, 0, tiled=True)
    gate_parts = gate_parts.reshape(2, 2, -1, part)
    gate_total = jnp.concatenate([gate_parts[0, 0], gate_parts[1, 0]], axis=1).astype(f32)
    up_total = jnp.concatenate([gate_parts[0, 1], gate_parts[1, 1]], axis=1).astype(f32)

    gain_in, gain_pre, gain_attn, gain_post = (gains[i * model : (i + 1) * model] for i in range(4))
    gain_query, gain_key = gains[4 * model :][:dim], gains[4 * model + dim :][:dim]
    return (
        output.reshape(seq_count, rows, model),
        grad_tokens.reshape(seq_count, rows, model),
        qkv_total,
        out_total,
        gate_total,
        up_total,
        down_total,
        gain_in,
        gain_query,
        gain_key,
        gain_attn,
        gain_pre,
        gain_post,
    )


def solution(mesh):
    seq, dp = mesh.devices.shape
    parts = Mesh(mesh.devices.reshape(seq // 2, 2, 2, dp // 2), (*SEQ, *DP))
    rows = P(DP, None)
    whole = P(None)
    placed = (P(DP, SEQ, None), P(DP, None), *[rows] * 5, *[whole] * 6, P(DP, SEQ, None))
    return jax.shard_map(
        shards,
        mesh=parts,
        in_specs=placed,
        out_specs=(*[P(DP, SEQ, None)] * 2, *[P(DP, SEQ)] * 5, *[whole] * 6),
        check_vma=False,
    )
```

```python
import functools

import jax
import jax.numpy as jnp
from jax import lax
from jax.experimental import pallas as pl
from jax.experimental.pallas import tpu as pltpu
from jax.sharding import Mesh, PartitionSpec as P

HQ = 4
WINDOW = 512
BLOCK = 256


epsilon = 1e-06
bf16 = jnp.bfloat16
f32 = jnp.float32
ROOT = 0.7978845608028654

SEQ = ("far", "near")
DP = ("chip", "core")
SQUARE = ("near", "chip", "core")

ANYWHERE = pl.BlockSpec(memory_space=pl.ANY)
VECTORS = pl.BlockSpec(memory_space=pltpu.VMEM)
SCALARS = pl.BlockSpec(memory_space=pltpu.SMEM)


def low(*shape):
    return jax.ShapeDtypeStruct(shape, bf16)


def wide(*shape):
    return jax.ShapeDtypeStruct(shape, f32)


def call(kernel, microseconds, out_shape, in_specs, scratch, *args, megabytes=48):
    return pl.pallas_call(
        kernel,
        out_shape=out_shape,
        in_specs=in_specs,
        out_specs=jax.tree.map(lambda _: VECTORS, out_shape),
        scratch_shapes=scratch,
        cost_estimate=pl.CostEstimate(
            flops=microseconds * 1_000_000_000, bytes_accessed=1 << 20, transcendentals=0
        ),
        compiler_params=pltpu.CompilerParams(vmem_limit_bytes=megabytes << 20),
    )(*args)


def steps(total, size):
    return [(first, min(first + size, total)) for first in range(0, total, size)]


NEAR, CHIP, CORE, PARITY, HALF, BIT = range(6)


def slots(place):
    chip, core = place[CHIP], place[CORE]
    return chip * 2 + core, (1 - chip) * 2 + core, chip * 2 + 1 - core, (1 - chip) * 2 + 1 - core


def at(start, size, multiple=16):
    return pl.ds(pl.multiple_of(start, multiple), size)


def begin(pairs, sem):
    copies = [pltpu.make_async_copy(a, b, sem.at[i]) for i, (a, b) in enumerate(pairs)]
    for c in copies:
        c.start()
    return copies


def fetch(place, pieces, target, sem):
    rows = target.shape[0] // 4
    return begin([(p, target.at[at(s * rows, rows)]) for s, p in zip(slots(place), pieces)], sem)


def fetch_gates(place, pieces, target, sem):
    own, core, chip, other = pieces[0], pieces[1], pieces[2:6], pieces[6:10]
    rows = target.shape[1] // 4
    half = rows // 2
    a, b, c, d = (s * rows for s in slots(place))
    pairs = [(own, target.at[:, at(a, rows)]), (core, target.at[:, at(c, rows)])]
    for start, four in ((b, chip), (d, other)):
        for k in range(2):
            pairs.append((four[k], target.at[place[PARITY], at(start + k * half, half)]))
            pairs.append((four[2 + k], target.at[1 - place[PARITY], at(start + k * half, half)]))
    return begin(pairs, sem)


def wait(copies):
    for c in copies:
        c.wait()


def nn(a, b):
    return jnp.dot(a, b, preferred_element_type=f32)


def nt(a, b):
    return lax.dot_general(a, b, (((1,), (1,)), ((), ())), preferred_element_type=f32)


def tn(a, b):
    return lax.dot_general(a, b, (((0,), (0,)), ((), ())), preferred_element_type=f32)


def rms(value, gain):
    return value * lax.rsqrt(jnp.mean(value * value, axis=-1, keepdims=True) + epsilon) * gain


def rms_back(value, gain, grad):
    scale = lax.rsqrt(jnp.mean(value * value, axis=-1, keepdims=True) + epsilon)
    unit = value * scale
    slope = grad * gain
    back = scale * (slope - unit * jnp.mean(slope * unit, axis=-1, keepdims=True))
    return back, jnp.sum(grad * unit, axis=0, keepdims=True)


def turn(value, cosine, sine):
    half = value.shape[-1] // 2
    a, b = value[:, :half], value[:, half:]
    return jnp.concatenate([a * cosine - b * sine, b * cosine + a * sine], axis=-1)


def half_plane(which, rows):
    return pl.ds(pl.multiple_of(which * rows, 128), rows)


def slice_kernel(far, part, place, gate, up, own, other0, other1, source, sem):
    rows, ff = gate.shape
    copies = begin([(w, source.at[i, :, :ff]) for i, w in enumerate((gate, up))], sem)
    near, chip = place[NEAR], place[CHIP]
    block = 48
    half = rows // 2

    def cut(i, which, target, from_row, to_row):
        for z in range(far):
            first, last = z * part, (z + 1) * part
            lo, hi = first // 128 * 128, min(-(-last // 128) * 128, far * part)
            span = -(-(hi - lo) // 128) * 128 + 128
            shift = (z * 3 + near * 2 + which) * part
            coarse = shift // 128 * 128
            x = source[i, from_row, at(lo + coarse, span, 128)]
            x = pltpu.roll(x, (span - (shift - coarse)) % span, 1)[:, : hi - lo]
            if first > lo:
                column = lax.broadcasted_iota(jnp.int32, x.shape, 1)
                x = jnp.where(column < first - lo, target[to_row, lo:hi], x)
            target[to_row, lo:hi] = x

    wait(copies)
    for k, other in enumerate((other0, other1)):

        def send(r, _):
            cut(place[PARITY], 1 - chip, other, at(k * half + r * block, block), at(r * block, block))
            return 0

        lax.fori_loop(0, half // block, send, 0)
    for i in range(2):

        def keep(r, _):
            here = at(r * block, block)
            cut(i, chip, own.at[i], here, here)
            return 0

        lax.fori_loop(0, rows // block, keep, 0)


def chip_columns(place, gate, up, far):
    rows, ff = gate.shape
    part = ff // (4 * far)
    source = -(-ff // 128) * 128 + 768
    return call(
        functools.partial(slice_kernel, far, part),
        6,
        (low(2, rows, ff // 4), low(rows // 2, ff // 4), low(rows // 2, ff // 4)),
        [SCALARS, ANYWHERE, ANYWHERE],
        [pltpu.VMEM((2, rows, source), bf16), pltpu.SemaphoreType.DMA((2,))],
        place,
        gate,
        up,
    )


def key_columns(pieces, count):
    return [p.at[:, p.shape[1] - count :] for p in pieces]


def query_columns(pieces, count):
    return [p.at[:, :count] for p in pieces]


def keys_kernel(place, own, peer, gain_in, gain_key, table, k0, k1, k2, k3, normed, pair, raw, every, weight, sem):
    copies = fetch(place, key_columns((k0, k1, k2, k3), weight.shape[1]), weight, sem)
    rows, near, width = own.shape[0], place[0], raw.shape[1]
    mine = rms(own[...].astype(f32), gain_in[...]).astype(bf16)
    normed[...] = mine
    every[half_plane(near, rows)] = mine
    every[half_plane(1 - near, rows)] = rms(peer[...].astype(f32), gain_in[...]).astype(bf16)
    wait(copies)
    projected = nn(every[...], weight[...])
    raw[...] = projected[:, :width]
    pair[0] = turn(rms(projected[:, :width], gain_key[...]), table[0], table[1]).astype(bf16)
    pair[1] = projected[:, width:].astype(bf16)


def keys_of(place, own, peer, gain_in, gain_key, table, pieces):
    rows, model = own.shape
    dim = gain_key.shape[1]
    return call(
        keys_kernel,
        2,
        (low(rows, model), low(2, 2 * rows, dim), wide(2 * rows, dim), low(2 * rows, model)),
        [SCALARS, *[VECTORS] * 5, *[ANYWHERE] * 4],
        [pltpu.VMEM((model, 2 * dim), bf16), pltpu.SemaphoreType.DMA((4,))],
        place, own, peer, gain_in, gain_key, table, *pieces,
    )


def queries_kernel(place, normed, gain, table, q0, q1, q2, q3, queries, raw, weight, sem):
    wait(fetch(place, query_columns((q0, q1, q2, q3), weight.shape[1]), weight, sem))
    rows, dim = normed.shape[0], gain.shape[1]
    here = half_plane(place[0], rows)
    cosine, sine = table[0, here], table[1, here]
    for h in range(HQ):
        projected = nn(normed[...], weight[:, h * dim : (h + 1) * dim])
        raw[h * rows : (h + 1) * rows] = projected
        turned = turn(rms(projected, gain[...]), cosine, sine).astype(bf16)
        queries[h * rows : (h + 1) * rows] = turned * jnp.asarray(dim**-0.5, bf16)


def queries_of(place, normed, gain, table, pieces):
    rows, model = normed.shape
    dim = gain.shape[1]
    return call(
        queries_kernel,
        3,
        (low(HQ * rows, dim), wide(HQ * rows, dim)),
        [SCALARS, *[VECTORS] * 3, *[ANYWHERE] * 4],
        [pltpu.VMEM((model, HQ * dim), bf16), pltpu.SemaphoreType.DMA((4,))],
        place, normed, gain, table, *pieces,
    )


def attend_kernel(
    place, queries, kv0, kv1, kv2, kv3, key_ids, query_ids, tokens, gain_attn, gain_pre, o0, o1, o2, o3,
    chances, heads, attn_out, residual, normed_pre, keys, values, weight, sem,
):
    copies = fetch(place, (o0, o1, o2, o3), weight, sem)
    plane, dim = kv0.shape[1], kv0.shape[2]
    for i, kv in enumerate((kv0, kv1, kv2, kv3)):
        keys[i * plane : (i + 1) * plane] = kv[0]
        values[i * plane : (i + 1) * plane] = kv[1]
    rows, span = query_ids.shape[0], key_ids.shape[1]
    row = lax.broadcasted_iota(jnp.int32, (rows, span), 0) + place[0] * rows
    column = lax.broadcasted_iota(jnp.int32, (rows, span), 1)
    same = key_ids[...] == query_ids[...]
    allowed = same | ((key_ids[...] < query_ids[...]) & (column >= row))
    for h in range(HQ):
        here = slice(h * rows, (h + 1) * rows)
        scores = jnp.where(allowed, nt(queries[here], keys[...]), -1e30)
        grown = jnp.exp(scores - jnp.max(scores, axis=-1, keepdims=True))
        share = grown / jnp.sum(grown, axis=-1, keepdims=True)
        chances[here] = share
        heads[:, h * dim : (h + 1) * dim] = nn(share.astype(bf16), values[...]).astype(bf16)
    wait(copies)
    out = nn(heads[...], weight[...])
    attn_out[...] = out
    total = tokens[...].astype(f32) + rms(out, gain_attn[...])
    residual[...] = total
    normed_pre[...] = rms(total, gain_pre[...]).astype(bf16)


def attend(place, queries, planes, key_ids, query_ids, tokens, gain_attn, gain_pre, pieces):
    rows, model = tokens.shape
    dim, span = queries.shape[1], key_ids.shape[1]
    return call(
        attend_kernel,
        5,
        (wide(HQ * rows, span), low(rows, HQ * dim), wide(rows, model), wide(rows, model), low(rows, model)),
        [SCALARS, *[VECTORS] * 10, *[ANYWHERE] * 4],
        [
            pltpu.VMEM((span, dim), bf16),
            pltpu.VMEM((span, dim), bf16),
            pltpu.VMEM((HQ * dim, model), bf16),
            pltpu.SemaphoreType.DMA((4,)),
        ],
        place, queries, *planes, key_ids, query_ids, tokens, gain_attn, gain_pre, *pieces,
    )


def gated(gate, up):
    square = gate * gate
    wave = jnp.tanh(ROOT * gate * (1.0 + 0.044715 * square))
    half = 0.5 * (1.0 + wave)
    value = gate * half
    bend = half + 0.5 * ROOT * gate * (1.0 - wave * wave) * (1.0 + 3.0 * 0.044715 * square)
    return (value * up).astype(bf16), (bend * up).astype(bf16), value.astype(bf16)


def forward_kernel(place, x0, x1, x2, x3, *refs):
    gates, downs = refs[:10], refs[10:14]
    whole, hidden, slope, gelu, total, p1, p2, p3 = refs[14:22]
    w_gates, w_down, sem, late_sem = refs[22:]
    copies = fetch_gates(place, gates, w_gates, sem)
    late = fetch(place, downs, w_down, late_sem)
    rows = x0.shape[0]
    for i, x in enumerate((x0, x1, x2, x3)):
        whole[i * rows : (i + 1) * rows] = x[...]
    wait(copies)
    for first, last in steps(w_down.shape[0], 256):
        gate = nn(whole[...], w_gates[0, :, first:last])
        up = nn(whole[...], w_gates[1, :, first:last])
        hidden[:, first:last], slope[:, first:last], gelu[:, first:last] = gated(gate, up)
    wait(late)
    for first, last in steps(w_down.shape[1], 384):
        part = nn(hidden[...], w_down[:, first:last])
        total[:, first:last] = part[:rows]
        for i, p in enumerate((p1, p2, p3)):
            p[:, first:last] = part[(i + 1) * rows : (i + 2) * rows].astype(bf16)


def weight_room(model, ff):
    return [
        pltpu.VMEM((2, model, ff), bf16),
        pltpu.VMEM((ff, model), bf16),
        pltpu.SemaphoreType.DMA((10,)),
        pltpu.SemaphoreType.DMA((6,)),
    ]


def forward(place, blocks, gates, downs):
    rows, model = blocks[0].shape
    ff = gates[0].shape[2]
    return call(
        forward_kernel,
        13,
        (low(4 * rows, model), *[low(4 * rows, ff)] * 3, wide(rows, model), *[low(rows, model)] * 3),
        [SCALARS, *[VECTORS] * 4, *[ANYWHERE] * 14],
        weight_room(model, ff),
        place, *blocks, *gates, *downs,
    )


def backward_kernel(place, x0, x1, x2, x3, slope, gelu, *refs):
    gates, downs = refs[:10], refs[10:14]
    whole, gate_low, up_low, total, p1, p2, p3 = refs[14:21]
    w_gates, w_down, late_sem, sem = refs[21:]
    copies = fetch(place, downs, w_down, sem)
    late = fetch_gates(place, gates, w_gates, late_sem)
    rows = x0.shape[0]
    for i, x in enumerate((x0, x1, x2, x3)):
        whole[i * rows : (i + 1) * rows] = x[...]
    wait(copies)
    for first, last in steps(w_down.shape[0], 256):
        back = nt(whole[...], w_down[first:last])
        gate_low[:, first:last] = (back * slope[:, first:last].astype(f32)).astype(bf16)
        up_low[:, first:last] = (back * gelu[:, first:last].astype(f32)).astype(bf16)
    wait(late)
    for first, last in steps(w_down.shape[1], 384):
        part = nt(gate_low[...], w_gates[0, first:last]) + nt(up_low[...], w_gates[1, first:last])
        total[:, first:last] = part[:rows]
        for i, p in enumerate((p1, p2, p3)):
            p[:, first:last] = part[(i + 1) * rows : (i + 2) * rows].astype(bf16)


def backward(place, blocks, slope, gelu, gates, downs):
    rows, model = blocks[0].shape
    ff = gates[0].shape[2]
    return call(
        backward_kernel,
        15,
        (low(4 * rows, model), *[low(4 * rows, ff)] * 2, wide(rows, model), *[low(rows, model)] * 3),
        [SCALARS, *[VECTORS] * 6, *[ANYWHERE] * 14],
        weight_room(model, ff),
        place, *blocks, slope, gelu, *gates, *downs,
    )


def far_kernel(window, place, n0, n1, n2, n3, *refs):
    gates, (hidden, slope, gelu, w_gates, tokens, room, sem) = refs[:10], refs[10:]
    start, width = window
    copies = fetch_gates(place, gates, w_gates, sem)
    rows = n0.shape[0]
    for i, n in enumerate((n0, n1, n2, n3)):
        tokens[i * rows : (i + 1) * rows] = n[...]
    wait(copies)
    for first, last in steps(hidden.shape[1], 256):
        gate = nn(tokens[...], w_gates[0, :, first:last])
        up = nn(tokens[...], w_gates[1, :, first:last])
        hidden[:, first:last], room[0, :, first:last], room[1, :, first:last] = gated(gate, up)
    here = at(place[HALF] * start, width, 128)
    slope[...] = room[0, :, here]
    gelu[...] = room[1, :, here]


def window_of(ff):
    start = ff // 2 // 128 * 128
    return start, ff - start


def far_hidden(place, far_normed, gates):
    rows, model = far_normed[0].shape
    ff = gates[0].shape[2]
    start, width = window_of(ff)
    return call(
        functools.partial(far_kernel, (start, width)),
        11,
        (low(4 * rows, ff), low(4 * rows, width), low(4 * rows, width)),
        [SCALARS, *[VECTORS] * 4, *[ANYWHERE] * 10],
        [
            pltpu.VMEM((2, model, ff), bf16),
            pltpu.VMEM((4 * rows, model), bf16),
            pltpu.VMEM((2, 4 * rows, ff), bf16),
            pltpu.SemaphoreType.DMA((10,)),
        ],
        place, *far_normed, *gates,
    )


def weights_kernel(
    window, place, normed, down, hidden, gate_low, up_low, n0, n1, n2, n3, d0, d1, d2, d3, far_hiddens, slope, gelu, *refs
):
    downs = refs[:4]
    keep, send = refs[4:6]
    w_down, hiddens, grads, tokens, backs, sem = refs[6:]
    model = normed.shape[1]
    start, width = window
    half, core, bit = place[HALF], place[CORE], place[BIT]
    columns = at(half * start, width, 128)
    copies = fetch(place, downs, w_down, sem)
    rows, own = n0.shape[0], normed.shape[0]
    kept = hidden.shape[1] // 2
    hiddens[:, :own] = hidden[...].T
    grads[core, :, :own] = gate_low[:, columns].T
    grads[1 - core, :, :own] = up_low[:, columns].T
    hiddens[:, own:] = far_hiddens[...].T
    tokens[:own] = normed[...]
    backs[:own] = down[...]
    for i, (n, d) in enumerate(zip((n0, n1, n2, n3), (d0, d1, d2, d3))):
        here = slice(own + i * rows, own + (i + 1) * rows)
        tokens[here] = n[...]
        backs[here] = d[...]
    wait(copies)
    for first, last in steps(width, 256):
        back = nt(backs[own:], w_down[at(half * start + first, last - first)])
        c = slice(first, last)
        grads[core, c, own:] = (back * slope[:, c].astype(f32)).astype(bf16).T
        grads[1 - core, c, own:] = (back * gelu[:, c].astype(f32)).astype(bf16).T
    part = kept // 2
    for i in range(2):
        r = at(half * (kept - start) + i * part, part)
        slot = i ^ bit
        keep[slot, :, :model] = nn(grads[0, r], tokens[...]).astype(bf16)
        send[slot, :, :model] = nn(grads[1, r], tokens[...]).astype(bf16)
    span = keep.shape[2] - model
    columns = at(half * (backs.shape[1] - span), span, 128)
    for i in range(4):
        result = nn(hiddens[i * part : (i + 1) * part], backs[:, columns]).astype(bf16)

        @pl.when(core == i % 2)
        def _():
            keep[i // 2, :, model:] = result

        @pl.when(core != i % 2)
        def _():
            send[i // 2, :, model:] = result


def weight_grads(place, normed, down, hidden, gate_low, up_low, far_normed, far_down, far_kept, downs):
    own, model = normed.shape
    ff = hidden.shape[1]
    start, width = window_of(ff)
    part = ff // 4
    span = -(-model // 256) * 128
    return call(
        functools.partial(weights_kernel, (start, width)),
        16,
        (low(2, part, model + span), low(2, part, model + span)),
        [SCALARS, *[VECTORS] * 16, *[ANYWHERE] * 4],
        [
            pltpu.VMEM((ff, model), bf16),
            pltpu.VMEM((ff, 2 * own), bf16),
            pltpu.VMEM((2, width, 2 * own), bf16),
            pltpu.VMEM((2 * own, model), bf16),
            pltpu.VMEM((2 * own, model), bf16),
            pltpu.SemaphoreType.DMA((6,)),
        ],
        place, normed, down, hidden, gate_low, up_low, *far_normed, *far_down, *far_kept, *downs,
    )


def turning_kernel(own, r1, r2, r3, residual, cotangent, gain, output, grad, grad_gain):
    down = own[...] + r1[...].astype(f32) + r2[...].astype(f32) + r3[...].astype(f32)
    output[...] = (residual[...] + rms(down, gain[...])).astype(bf16)
    back, grad_gain[...] = rms_back(down, gain[...], cotangent[...].astype(f32))
    grad[...] = back.astype(bf16)


def turning(parts, residual, cotangent, gain):
    rows, model = residual.shape
    return call(
        turning_kernel,
        1,
        (low(rows, model), low(rows, model), wide(1, model)),
        [VECTORS] * 7,
        [],
        *parts, residual, cotangent, gain,
    )


def cores_kernel(place, keep, got, gates, send_other, send_own, down, send_down, turned):
    model = gates.shape[1]
    gates[...] = keep[0, :, :model].astype(f32) + got[0, :, :model].astype(f32)
    sent = (keep[1, :, :model].astype(f32) + got[1, :, :model].astype(f32)).astype(bf16)
    half = send_own.shape[1]
    for i in range(2):

        @pl.when(place[CHIP] == i)
        def _():
            send_own[...] = sent[:, i * half : (i + 1) * half]
            send_other[...] = sent[:, (1 - i) * half : (2 - i) * half]

    part = down.shape[1]
    first = place[HALF] * (turned.shape[1] - 2 * part)
    for i in range(2):
        turned[i] = (keep[i, :, model:].astype(f32) + got[i, :, model:].astype(f32)).T
        for target, bit in ((down, place[BIT]), (send_down, 1 - place[BIT])):
            target[i] = turned[i, at(first + bit * part, part)].astype(target.dtype)


def add_cores(place, keep, got, model):
    part = keep.shape[1]
    return call(
        cores_kernel,
        4,
        (
            wide(part, model), low(part, model // 2), low(part, model // 2),
            wide(2, model // 4, part), low(2, model // 4, part),
        ),
        [SCALARS, *[VECTORS] * 2],
        [pltpu.VMEM((2, keep.shape[2] - model, part), f32)],
        place, keep, got,
    )


def gates_kernel(flip, place, gates, got, total):
    half, unit = got.shape[1], total.shape[1]
    for i in range(2):

        @pl.when(place[CHIP] == (1 - i if flip else i))
        def _():
            turned = (gates[:, i * half : (i + 1) * half] + got[...].astype(f32)).T.astype(bf16)
            for k in range(2):
                total[k] = turned[k * unit : (k + 1) * unit]


def add_gates(flip, place, gates, got):
    part, half = got.shape
    return call(
        functools.partial(gates_kernel, flip), 2, low(2, half // 2, part), [SCALARS, *[VECTORS] * 2], [], place, gates, got
    )


def gather_gates_kernel(place, own, peer, got_own, got_peer, gate, up):
    part = own.shape[1]
    for core in range(2):
        for chip in range(2):

            @pl.when((place[CORE] == core) & (place[CHIP] == chip))
            def _():
                here, there = (gate, up) if core == 0 else (up, gate)
                for target, first, second in ((here, own, peer), (there, got_own, got_peer)):
                    target[:, chip * part : (chip + 1) * part] = first[...].astype(f32)
                    target[:, (1 - chip) * part : (2 - chip) * part] = second[...].astype(f32)


def gather_gates(place, own, peer, got_own, got_peer):
    rows, part = own.shape
    return call(
        gather_gates_kernel,
        2,
        (wide(rows, 2 * part), wide(rows, 2 * part)),
        [SCALARS, *[VECTORS] * 4],
        [],
        place, own, peer, got_own, got_peer,
    )


def down_kernel(down, got, total):
    total[...] = (down[...] + got[...].astype(f32)).astype(bf16)


def add_down(down, got):
    return call(down_kernel, 1, low(*down.shape), [VECTORS] * 2, [], down, got)


def attend_back_kernel(
    far, early, place, h_own, h_r1, h_r2, h_r3, h_residual, h_attn_out, h_cotangent, h_chances, h_queries, h_raw, h_table,
    gain_pre, gain_attn, gain_query,
    kv0, kv1, kv2, kv3, o0, o1, o2, o3,
    grad_residual, keep, send, grad_gains, grad_gain_query, grad_projected, g0, g1, g2, g3,
    own, r1, r2, r3, residual, attn_out, cotangent, chances, queries, raw, table,
    keys, values, attn_low, heads, dull, weight, sem, soon_sem, late_sem,
):
    plane, dim = kv0.shape[1], kv0.shape[2]
    soon = begin(
        [
            (h_own, own), (h_r1, r1), (h_r2, r2), (h_r3, r3),
            (h_residual, residual), (h_attn_out, attn_out), (h_cotangent, cotangent),
        ],
        soon_sem,
    )
    copies = fetch(place, (o0, o1, o2, o3), weight, sem)
    late = [(h_chances, chances), (h_queries, queries), (h_raw, raw), (h_table, table)]
    for i, kv in enumerate((kv0, kv1, kv2, kv3)):
        late += [(kv.at[0], keys.at[i * plane : (i + 1) * plane]), (kv.at[1], values.at[i * plane : (i + 1) * plane])]
    copies += begin(late, late_sem)
    wait(soon)
    normed = own[...] + r1[...].astype(f32) + r2[...].astype(f32) + r3[...].astype(f32)
    back, grad_gains[0:1] = rms_back(residual[...], gain_pre[...], normed)
    total = cotangent[...].astype(f32) + back
    grad_residual[...] = total
    back, grad_gains[1:2] = rms_back(attn_out[...], gain_attn[...], total)
    attn_low[...] = back.astype(bf16)
    wait(copies)
    rows = own.shape[0]
    here = half_plane(place[0], rows)
    cosine, sine = table[0, here], table[1, here]
    gain_total = jnp.zeros_like(grad_gain_query)
    for h in range(HQ):
        r = slice(h * rows, (h + 1) * rows)
        heads[r] = nt(attn_low[...], weight[h * dim : (h + 1) * dim]).astype(bf16)
        share = chances[r]
        grad_share = nt(heads[r], values[...])
        mean = jnp.sum(share * grad_share, axis=-1, keepdims=True)
        grad_scores = (share * (grad_share - mean)).astype(bf16)
        dull[r] = grad_scores
        turned = nn(grad_scores, keys[...]) * (dim**-0.5)
        back, gain_part = rms_back(raw[r], gain_query[...], turn(turned, cosine, -sine))
        gain_total = gain_total + gain_part
        grad_projected[:, h * dim : (h + 1) * dim] = back.astype(bf16)
    grad_gain_query[...] = gain_total
    for i, g in enumerate((g0, g1, g2, g3)):
        c = slice(i * plane, (i + 1) * plane)
        g[0] = tn(dull[:, c], queries[...]).astype(g.dtype)
        g[1] = tn(chances[:, c].astype(bf16), heads[...]).astype(g.dtype)
    block, size = grad_projected.shape[1] * 3 // 2 // (2 * far), attn_low.shape[1] // (2 * far)
    parts = [
        columns_of(grad_projected[...], i, range(early), block) + columns_of(attn_low[...], i, range(far), size) for i in range(2)
    ]
    for i in range(2):

        @pl.when(place[NEAR] == i)
        def _():
            keep[...] = jnp.concatenate(parts[i], axis=1)
            send[...] = jnp.concatenate(parts[1 - i], axis=1)


def attend_back(far, early, place, parts, residual, attn_out, cotangent, gain_pre, gain_attn, chances, queries, raw, table, gain_query, planes, pieces):
    rows, model = residual.shape
    dim, span = queries.shape[1], chances.shape[1]
    plane = planes[0].shape[1]
    sent = low(2, plane, dim)
    width = early * HQ * dim * 3 // 2 // (2 * far) + model // 2
    return call(
        functools.partial(attend_back_kernel, far, early),
        8,
        (
            wide(rows, model), low(rows, width), low(rows, width), wide(2, model), wide(1, dim), low(rows, HQ * dim),
            sent, sent, wide(2, plane, dim), sent,
        ),
        [SCALARS, *[ANYWHERE] * 11, *[VECTORS] * 3, *[ANYWHERE] * 8],
        [
            pltpu.VMEM((rows, model), f32),
            *[pltpu.VMEM((rows, model), bf16)] * 3,
            *[pltpu.VMEM((rows, model), f32)] * 2,
            pltpu.VMEM((rows, model), bf16),
            pltpu.VMEM((HQ * rows, span), f32),
            pltpu.VMEM((HQ * rows, dim), bf16),
            pltpu.VMEM((HQ * rows, dim), f32),
            pltpu.VMEM((2, 2 * rows, dim // 2), f32),
            pltpu.VMEM((span, dim), bf16),
            pltpu.VMEM((span, dim), bf16),
            pltpu.VMEM((rows, model), bf16),
            pltpu.VMEM((HQ * rows, dim), bf16),
            pltpu.VMEM((HQ * rows, span), bf16),
            pltpu.VMEM((HQ * dim, model), bf16),
            pltpu.SemaphoreType.DMA((4,)),
            pltpu.SemaphoreType.DMA((7,)),
            pltpu.SemaphoreType.DMA((12,)),
        ],
        place, *parts, residual, attn_out, cotangent, chances, queries, raw, table, gain_pre, gain_attn, gain_query, *planes, *pieces,
        megabytes=56,
    )


def queries_back_kernel(place, grad, q0, q1, q2, q3, result, weight, sem):
    wait(fetch(place, query_columns((q0, q1, q2, q3), weight.shape[1]), weight, sem))
    result[...] = nt(grad[...], weight[...])


def queries_back(place, grad, pieces):
    rows, width = grad.shape
    model = pieces[0].shape[0] * 4
    return call(
        queries_back_kernel,
        3,
        wide(rows, model),
        [SCALARS, VECTORS, *[ANYWHERE] * 4],
        [pltpu.VMEM((model, width), bf16), pltpu.SemaphoreType.DMA((4,))],
        place, grad, *pieces,
    )


def columns_of(value, near, blocks, size):
    return [value[:, (2 * f + near) * size : (2 * f + near + 1) * size] for f in blocks]


def by_place(index, choices):
    for i, choice in enumerate(choices):
        pl.when(index == i)(choice)


def first_products_kernel(place, every, own_heads, got_heads, own, got, keep, send, right, heads):
    rows, near, core = own.shape[0], place[NEAR], place[CORE]
    for target, mine, theirs in ((right, own, got), (heads, own_heads, got_heads)):
        target[half_plane(near, rows)] = mine[...]
        target[half_plane(1 - near, rows)] = theirs[...]
    unit, head = keep.shape[1], heads.shape[1] // 4
    width = keep.shape[2] - 2 * head
    part = tn(every[...], right[:, :width])
    out = tn(right[:, width:], heads[...])
    for i in range(4):
        here = part[i * unit : (i + 1) * unit]
        there = [out[k * unit : (k + 1) * unit, i * head : (i + 1) * head] for k in range(2)]
        for target, chosen in ((keep, core == i % 2), (send, core != i % 2)):

            @pl.when(chosen)
            def _():
                target[i // 2, :, :width] = here.astype(target.dtype)
                for k in range(2):
                    first = width + k * head
                    target[i // 2, :, first : first + head] = there[k].astype(target.dtype)


def first_products(place, every, own_heads, got_heads, own, got):
    rows, model = own_heads.shape[0], every.shape[1]
    width = own.shape[1] - model // 2 + own_heads.shape[1] // 2
    return call(
        first_products_kernel,
        4,
        (wide(2, model // 4, width), low(2, model // 4, width)),
        [SCALARS, *[VECTORS] * 5],
        [pltpu.VMEM((2 * rows, own.shape[1]), bf16), pltpu.VMEM((2 * rows, own_heads.shape[1]), bf16)],
        place, every, own_heads, got_heads, own, got,
    )


def first_cores_kernel(place, keep, got, new, send):
    chip = place[CHIP]
    new[...] = keep[chip] + got[chip].astype(f32)
    send[...] = (keep[1 - chip] + got[1 - chip].astype(f32)).astype(bf16)


def first_cores(place, keep, got):
    shape = keep.shape[1:]
    return call(first_cores_kernel, 2, (wide(*shape), low(*shape)), [SCALARS, *[VECTORS] * 2], [], place, keep, got)


def last_products_kernel(place, every, own, got, gains, keep, send, total_gains, right):
    rows, near, core = own.shape[0], place[NEAR], place[CORE]
    right[half_plane(near, rows)] = own[...]
    right[half_plane(1 - near, rows)] = got[:rows]
    sums = gains[...] + got[rows:].astype(f32)
    total_gains[...] = sums
    unit = keep.shape[1]
    part = tn(every[...], right[...])
    for i in range(4):
        x, c = i // 2, i % 2
        here = part[i * unit : (i + 1) * unit]

        @pl.when(core == c)
        def _():
            keep[x] = here

        @pl.when(core != c)
        def _():
            send[x * unit : (x + 1) * unit] = here.astype(bf16)

    send[2 * unit :] = sums.astype(bf16)


def last_products(place, every, own, got, gains):
    rows, width = own.shape
    unit, more = every.shape[1] // 4, gains.shape[0]
    return call(
        last_products_kernel,
        3,
        (wide(2, unit, width), low(2 * unit + more, width), wide(more, width)),
        [SCALARS, *[VECTORS] * 4],
        [pltpu.VMEM((2 * rows, width), bf16)],
        place, every, own, got, gains,
    )


def last_cores_kernel(place, keep, got, gains, new, send, total_gains):
    unit, chip = new.shape[0], place[CHIP]
    new[...] = keep[chip] + got[at(chip * unit, unit)].astype(f32)
    send[:unit] = (keep[1 - chip] + got[at((1 - chip) * unit, unit)].astype(f32)).astype(bf16)
    sums = gains[...] + got[2 * unit :].astype(f32)
    total_gains[...] = sums
    send[unit:] = sums.astype(bf16)


def last_cores(place, keep, got, gains):
    _, unit, width = keep.shape
    more = gains.shape[0]
    return call(
        last_cores_kernel,
        1,
        (wide(unit, width), low(unit + more, width), wide(more, width)),
        [SCALARS, *[VECTORS] * 3],
        [],
        place, keep, got, gains,
    )


def chips_kernel(first, got_first, keep, got, gains, out, room, line):
    unit, early = first.shape[0], room.shape[1] - keep.shape[1]
    far, rows, lanes = out.shape
    size = room.shape[1] // far
    across = lanes - size
    head = (first.shape[1] - early) // 2
    room[:, :early] = first[:, :early] + got_first[:, :early].astype(f32)
    room[:, early:] = keep[...] + got[:unit].astype(f32)
    sums = gains[...] + got[unit:].astype(f32)
    width = gains.shape[1]
    line[...] = jnp.zeros_like(line)
    for i in range(gains.shape[0]):
        line[:, i * width : (i + 1) * width] = sums[i : i + 1]
    extra = jnp.concatenate([line[:, i * lanes : (i + 1) * lanes] for i in range(rows - unit)], axis=0).astype(bf16)
    short = 2 * unit // far
    for half in range(2):
        start = early + half * head
        part = (first[:, start : start + head] + got_first[:, start : start + head].astype(f32)).astype(bf16)
        for k in range(far // 2):
            f = half * (far // 2) + k
            out[f, :unit, :size] = room[:, f * size : (f + 1) * size].astype(bf16)
            block = part[k * short : (k + 1) * short]
            for g in range(far // 2):
                out[f, g * short : (g + 1) * short, size:] = block[:, g * across : (g + 1) * across]
            out[f, unit:] = extra


def last_chips(far, first, got_first, keep, got, gains, head):
    unit, width = keep.shape
    early = first.shape[1] - 2 * head
    lanes = (early + width + 2 * head) // far
    rows = -(-gains.size // (16 * lanes)) * 16
    return call(
        chips_kernel,
        3,
        low(far, unit + rows, lanes),
        [VECTORS] * 5,
        [pltpu.VMEM((unit, early + width), f32), pltpu.VMEM((1, rows * lanes), f32)],
        first, got_first, keep, got, gains,
    )


def last_sum_kernel(parts, total, out, gains):
    unit, size = total.shape
    sums = jnp.sum(parts[...].astype(f32), axis=0)
    total[...] = sums[:unit, :size]
    short, across = out.shape[0], sums.shape[1] - size
    for g in range(unit // short):
        out[:, g * across : (g + 1) * across] = sums[g * short : (g + 1) * short, size:]
    gains[...] = sums[unit:]


def last_sum(parts, unit, head):
    far, rows, lanes = parts.shape
    across = 2 * head // far
    return call(
        last_sum_kernel,
        2,
        (wide(unit, lanes - across), wide(2 * unit // far, head), wide(rows - unit, lanes)),
        [VECTORS],
        [],
        parts,
    )


def down_rows_kernel(part, parts, result):
    for i in range(4):
        for z in range(parts.shape[2] // part):
            first = (4 * z + i) * part
            result[:, first : first + part] = parts[i, :, z * part : (z + 1) * part].astype(f32)


def down_rows(parts, part):
    _, columns, rows = parts.shape
    return call(functools.partial(down_rows_kernel, part), 2, wide(columns, 4 * rows), [VECTORS], [], parts)


def keys_back_kernel(
    early, place, total, received, raw, table, gain_key, partial, grad_residual, tokens, gain_in, grad_queries, grad_gains,
    grad_gain_post, grad_gain_query, k0, k1, k2, k3, grad_tokens, keep, send, sums, grad_projected, gains, weight, sem,
):
    copies = fetch(place, key_columns((k0, k1, k2, k3), weight.shape[1]), weight, sem)
    rows, dim = tokens.shape[0], raw.shape[1]
    here = half_plane(place[0], rows)
    keys = total[0, here] + received[0].astype(f32)
    values = total[1, here] + received[1].astype(f32)
    back, grad_gain_key = rms_back(raw[here], gain_key[...], turn(keys, table[0, here], -table[1, here]))
    grad_projected[:, :dim] = back.astype(bf16)
    grad_projected[:, dim:] = values.astype(bf16)
    wait(copies)
    normed = partial[...] + nt(grad_projected[...], weight[...])
    back, grad_gain_in = rms_back(tokens[...].astype(f32), gain_in[...], normed)
    grad_tokens[...] = grad_residual[...] + back
    model, width = tokens.shape[1], keep.shape[1]
    gains[...] = jnp.zeros_like(gains)
    gains[:, :model] = grad_gain_in
    for i in range(2):
        gains[:, (i + 1) * model : (i + 2) * model] = grad_gains[i : i + 1]
    gains[:, 3 * model : 4 * model] = grad_gain_post[...]
    gains[:, 4 * model : 4 * model + dim] = grad_gain_query[...]
    gains[:, 4 * model + dim : 4 * model + 2 * dim] = grad_gain_key
    block = grad_queries.shape[1] * 3 // 2 // (2 * early[0])
    every = jnp.concatenate([grad_queries[:, early[1] * 2 * block :], grad_projected[...]], axis=1)
    parts = [jnp.concatenate(columns_of(every, i, range(early[0] - early[1]), block), axis=1) for i in range(2)]
    for i in range(2):

        @pl.when(place[NEAR] == i)
        def _():
            keep[...] = parts[i]
            send[:rows] = parts[1 - i]

    extra = jnp.concatenate([gains[:, i * width : (i + 1) * width] for i in range(sums.shape[0])], axis=0)
    sums[...] = extra
    send[rows:] = extra.astype(bf16)


def keys_back(
    far, early, place, total, received, raw, table, gain_key, partial, grad_residual, tokens, gain_in, grad_queries, grad_gains,
    grad_gain_post, grad_gain_query, pieces,
):
    rows, model = tokens.shape
    dim = raw.shape[1]
    width = (far - early) * (HQ + 2) * dim // (2 * far)
    more = -(-(4 * model + 2 * dim) // (16 * width)) * 16
    return call(
        functools.partial(keys_back_kernel, (far, early)),
        4,
        (wide(rows, model), low(rows, width), low(rows + more, width), wide(more, width)),
        [SCALARS, *[VECTORS] * 13, *[ANYWHERE] * 4],
        [
            pltpu.VMEM((rows, 2 * dim), bf16),
            pltpu.VMEM((1, more * width), f32),
            pltpu.VMEM((model, 2 * dim), bf16),
            pltpu.SemaphoreType.DMA((4,)),
        ],
        place, total, received, raw, table, gain_key, partial, grad_residual, tokens, gain_in, grad_queries, grad_gains,
        grad_gain_post, grad_gain_query, *pieces,
    )


def shift(value, by):
    length = lax.axis_size("far")
    pairs = [(i, i + by) for i in range(length) if 0 <= i + by < length]
    return lax.ppermute(value, "far", pairs)


def swap(value, axis):
    return lax.ppermute(value, axis, [(0, 1), (1, 0)])


def diagonal(value):
    return lax.ppermute(value, ("near", "chip"), [(i, 3 - i) for i in range(4)])


def around(values):
    return swap(values[0], "chip"), swap(values[1], "near"), diagonal(values[2])


def far_swap(value, step):
    return lax.ppermute(value, "far", [(i, i ^ step) for i in range(lax.axis_size("far"))])


def after(value, *others):
    return lax.optimization_barrier((value, others))[0]


def halving(value, axis, steps):
    place = lax.axis_index("far")
    for step in steps:
        shape = (*value.shape[:axis], 2, value.shape[axis] // 2, *value.shape[axis + 1 :])
        value = value.reshape(shape)
        bit = place // step % 2
        mine = lax.dynamic_index_in_dim(value, bit, axis, keepdims=False)
        other = lax.dynamic_index_in_dim(value, 1 - bit, axis, keepdims=False)
        value = mine + far_swap(other.astype(bf16), step).astype(f32)
    return value


def shards(
    tokens,
    block_ids,
    w_qkv,
    w_out,
    w_gate,
    w_up,
    w_down,
    gain_in,
    gain_query,
    gain_key,
    gain_attn,
    gain_pre,
    gain_post,
    cotangent,
):
    seq_count, rows, model = tokens.shape
    dim = gain_query.shape[0]
    query_width = HQ * dim
    plane = 2 * rows
    span = WINDOW + plane + BLOCK
    full_len = block_ids.shape[1]
    far_count = lax.axis_size("far")
    near, chip, core = lax.axis_index("near"), lax.axis_index("chip"), lax.axis_index("core")
    far = lax.axis_index("far")
    half_far = far_count // 2
    far_bits = [1 << i for i in reversed(range(far_count.bit_length() - 1))]
    low_bits = far_bits[1:]
    half = far // half_far
    bit = far // low_bits[0] % 2
    place = jnp.stack([near, chip, core, far % 2, half, bit]).astype(jnp.int32)
    start = far * plane
    ff = w_gate.shape[1]
    part = ff // (far_count * 4)
    early = query_width // (w_qkv.shape[1] // far_count)
    tokens = tokens.reshape(rows, model)
    cotangent = cotangent.reshape(rows, model)
    gain_in, gain_query, gain_key, gain_attn, gain_pre, gain_post = (
        g.reshape(1, -1) for g in (gain_in, gain_query, gain_key, gain_attn, gain_pre, gain_post)
    )

    qkv_chip, peer_tokens = swap(w_qkv, "chip"), swap(tokens, "near")
    gates_own, *gates_other = chip_columns(place, w_gate, w_up, far_count)
    split = lax.dynamic_index_in_dim(w_down.reshape(-1, 2, 2, part, model), near, 1, keepdims=False)
    down_own = lax.dynamic_index_in_dim(split, chip, 1, keepdims=False).reshape(-1, model)
    down_other = lax.dynamic_index_in_dim(split, 1 - chip, 1, keepdims=False).reshape(-1, model)
    qkv_core, out_core, down_core = swap(w_qkv, "core"), swap(w_out, "core"), swap(down_own, "core")
    qkv_pieces = w_qkv, qkv_chip, qkv_core, swap(qkv_chip, "core")

    frequency = 10000.0 ** (-jnp.arange(dim // 2, dtype=f32) * 2.0 / dim)
    angles = (start + jnp.arange(plane)).astype(f32)[:, None] * frequency[None, :]
    table = jnp.stack([jnp.cos(angles), jnp.sin(angles)])
    normed_in, pair, raw_keys, every = keys_of(
        place, after(tokens, down_core, out_core, gates_own), peer_tokens, gain_in, gain_key, table, qkv_pieces
    )
    gates_core = swap(gates_own, "core")
    out_chip = swap(after(w_out, qkv_chip), "chip")
    first = swap(after(gates_other[0], qkv_chip), "chip")
    second = swap(after(gates_other[1], out_chip), "chip")
    down_chip = swap(after(down_other, first), "chip")
    out_pieces = w_out, out_chip, out_core, swap(out_chip, "core")
    first_rest, second_rest = far_swap(first, 1), far_swap(second, 1)
    four = first, second, first_rest, second_rest
    gates = gates_own, gates_core, *four, *(swap(p, "core") for p in four)
    downs = down_own, down_chip, down_core, swap(down_chip, "core")

    padded = jnp.pad(block_ids, ((0, 0), (WINDOW, BLOCK)), constant_values=1 << 30)
    key_ids = lax.dynamic_slice_in_dim(padded, start, span, 1)
    query_ids = lax.dynamic_slice_in_dim(block_ids, start + near * rows, rows, 1).reshape(rows, 1)

    planes = (shift(pair, 2), shift(pair, 1), pair, shift(pair, -1))
    queries, raw_queries = queries_of(place, normed_in, gain_query, table, qkv_pieces)
    chances, heads_out, attn_out, residual, normed_pre = attend(
        place, after(queries, first, gates_core), planes, key_ids, query_ids, tokens, gain_attn, gain_pre, out_pieces
    )

    far_normed = far_swap(after(normed_pre, first_rest), half_far)
    blocks = (normed_pre, *around([normed_pre] * 3))
    all_normed, hidden, slope, gelu, own, *sent = forward(place, after(blocks, far_normed), gates, downs)
    far_normed = after(far_normed, second_rest)
    far_normed = (far_normed, *around([far_normed] * 3))
    sent = after(sent, *far_normed)
    output, grad_down_proj, grad_gain_post = turning((own, *around(sent)), residual, cotangent, gain_post)
    far_down = far_swap(grad_down_proj, half_far)
    blocks = (grad_down_proj, *around([grad_down_proj] * 3))
    far_kept = far_hidden(place, after(far_normed, grad_down_proj), gates)
    blocks = after(blocks, far_down, *far_kept)
    all_down, gate_low, up_low, own, *sent = backward(place, blocks, slope, gelu, gates, downs)
    far_down = (far_down, *around([far_down] * 3))
    sent = after(sent, *far_down)
    parts = (own, *around(sent))
    keep_grads, send_grads = weight_grads(
        place, all_normed, all_down, hidden, after(gate_low, *sent), up_low, far_normed, far_down, far_kept, downs
    )
    got_grads = swap(after(send_grads, parts), "core")
    (
        grad_residual, own_right, other_right, grad_gains, grad_gain_query, grad_queries, *sent,
    ) = attend_back(
        far_count, early, place, after(parts, keep_grads), residual, attn_out, cotangent, gain_pre, gain_attn, chances, queries, raw_queries, table, gain_query,
        planes, out_pieces,
    )
    grad_gates, send_other, send_own, grad_down, send_down = add_cores(place, after(keep_grads, grad_queries), got_grads, model)
    total = after(sent[2], send_down) + shift(sent[0], -2).astype(f32)
    total = total + shift(sent[1], -1).astype(f32) + shift(sent[3], 1).astype(f32)
    partial = queries_back(place, after(grad_queries, send_down), qkv_pieces)
    got, got_heads = swap(other_right, "near"), swap(after(heads_out, grad_queries), "near")
    total, grad_gates, send_other, send_own, grad_down, send_down, partial, got, got_heads = lax.optimization_barrier(
        (total, grad_gates, send_other, send_own, grad_down, send_down, partial, got, got_heads)
    )

    received = swap(
        lax.dynamic_slice_in_dim(total, (1 - near) * rows, rows, 1).astype(bf16), "near"
    )
    got_down, got_other, got_own = (far_swap(g, low_bits[0]) for g in (send_down, send_other, send_own))
    keep_first, send_first = first_products(place, every, heads_out, got_heads, own_right, got)
    keep_first, send_first = first_cores(place, keep_first, swap(send_first, "core"))
    got_first = swap(send_first, "chip")
    grad_tokens, own_right, other_right, gains = keys_back(
        far_count, early, place, after(total, send_first), received, raw_keys, table, gain_key, partial, grad_residual, tokens, gain_in,
        grad_queries, grad_gains, grad_gain_post, grad_gain_query, qkv_pieces,
    )
    keep, send, gains = last_products(place, every, after(own_right, got_down), swap(other_right, "near"), gains)
    keep, send, gains = last_cores(place, after(keep, got_other), swap(send, "core"), gains)
    grad_down = add_down(grad_down, got_down)
    sums = last_chips(
        far_count, after(keep_first, got_own), got_first, keep, swap(send, "chip"), gains, query_width // 4
    )
    columns = model // far_count // 2
    down_parts = halving(grad_down, 1, low_bits[1:]).astype(bf16).reshape(2, 2, columns, -1)
    down_parts = down_parts.transpose(1, 0, 2, 3).reshape(4, columns, -1)
    down_parts = lax.all_to_all(down_parts, ("near", "chip"), 0, 0, tiled=True)
    other_gates = add_gates(True, place, after(grad_gates, send), got_other)
    peer_gates = swap(halving(other_gates, 2, low_bits[1:]).astype(bf16), "chip")
    sums, got_own = lax.optimization_barrier((sums, got_own))

    sums = lax.all_to_all(sums, "far", 0, 0, tiled=True)
    qkv_total, out_total, gains = last_sum(sums, model // 4, query_width // 4)
    out_total, gains = out_total.T, gains.reshape(-1)
    own_gates = halving(add_gates(False, place, grad_gates, got_own), 2, low_bits[1:]).astype(bf16)
    mine = [lax.dynamic_index_in_dim(g, core, 0, keepdims=False) for g in (own_gates, peer_gates)]
    theirs = [lax.dynamic_index_in_dim(g, 1 - core, 0, keepdims=False) for g in (own_gates, peer_gates)]
    gate_total, up_total = gather_gates(place, *mine, *(swap(g, "core") for g in theirs))
    down_total = down_rows(down_parts, part).T

    gain_in, gain_pre, gain_attn, gain_post = (gains[i * model : (i + 1) * model] for i in range(4))
    gain_query, gain_key = gains[4 * model :][:dim], gains[4 * model + dim :][:dim]
    return (
        output.reshape(seq_count, rows, model),
        grad_tokens.reshape(seq_count, rows, model),
        qkv_total,
        out_total,
        gate_total,
        up_total,
        down_total,
        gain_in,
        gain_query,
        gain_key,
        gain_attn,
        gain_pre,
        gain_post,
    )


def solution(mesh):
    seq, dp = mesh.devices.shape
    parts = Mesh(mesh.devices.reshape(seq // 2, 2, 2, dp // 2), (*SEQ, *DP))
    rows = P(DP, None)
    whole = P(None)
    placed = (P(DP, SEQ, None), P(DP, None), *[rows] * 5, *[whole] * 6, P(DP, SEQ, None))
    return jax.shard_map(
        shards,
        mesh=parts,
        in_specs=placed,
        out_specs=(*[P(DP, SEQ, None)] * 2, *[P(DP, SEQ)] * 5, *[whole] * 6),
        check_vma=False,
    )
```

```python
import functools

import jax
import jax.numpy as jnp
from jax import lax
from jax.experimental import pallas as pl
from jax.experimental.pallas import tpu as pltpu
from jax.sharding import Mesh, PartitionSpec as P

HQ = 4
WINDOW = 512
BLOCK = 256


epsilon = 1e-06
bf16 = jnp.bfloat16
f32 = jnp.float32
ROOT = 0.7978845608028654

SEQ = ("far", "near")
DP = ("chip", "core")
SQUARE = ("near", "chip", "core")

ANYWHERE = pl.BlockSpec(memory_space=pl.ANY)
VECTORS = pl.BlockSpec(memory_space=pltpu.VMEM)
SCALARS = pl.BlockSpec(memory_space=pltpu.SMEM)


def low(*shape):
    return jax.ShapeDtypeStruct(shape, bf16)


def wide(*shape):
    return jax.ShapeDtypeStruct(shape, f32)


def call(kernel, microseconds, out_shape, in_specs, scratch, *args, megabytes=48):
    return pl.pallas_call(
        kernel,
        out_shape=out_shape,
        in_specs=in_specs,
        out_specs=jax.tree.map(lambda _: VECTORS, out_shape),
        scratch_shapes=scratch,
        cost_estimate=pl.CostEstimate(
            flops=microseconds * 1_000_000_000, bytes_accessed=1 << 20, transcendentals=0
        ),
        compiler_params=pltpu.CompilerParams(vmem_limit_bytes=megabytes << 20),
    )(*args)


def steps(total, size):
    return [(first, min(first + size, total)) for first in range(0, total, size)]


NEAR, CHIP, CORE, PARITY, HALF, BIT = range(6)


def slots(place):
    chip, core = place[CHIP], place[CORE]
    return chip * 2 + core, (1 - chip) * 2 + core, chip * 2 + 1 - core, (1 - chip) * 2 + 1 - core


def at(start, size, multiple=16):
    return pl.ds(pl.multiple_of(start, multiple), size)


def begin(pairs, sem):
    copies = [pltpu.make_async_copy(a, b, sem.at[i]) for i, (a, b) in enumerate(pairs)]
    for c in copies:
        c.start()
    return copies


def fetch(place, pieces, target, sem):
    rows = target.shape[0] // 4
    return begin([(p, target.at[at(s * rows, rows)]) for s, p in zip(slots(place), pieces)], sem)


def fetch_gates(place, pieces, target, sem):
    own, core, chip, other = pieces[0], pieces[1], pieces[2:6], pieces[6:10]
    rows = target.shape[1] // 4
    half = rows // 2
    a, b, c, d = (s * rows for s in slots(place))
    pairs = [(own, target.at[:, at(a, rows)]), (core, target.at[:, at(c, rows)])]
    for start, four in ((b, chip), (d, other)):
        for k in range(2):
            pairs.append((four[k], target.at[place[PARITY], at(start + k * half, half)]))
            pairs.append((four[2 + k], target.at[1 - place[PARITY], at(start + k * half, half)]))
    return begin(pairs, sem)


def wait(copies):
    for c in copies:
        c.wait()


def nn(a, b):
    return jnp.dot(a, b, preferred_element_type=f32)


def nt(a, b):
    return lax.dot_general(a, b, (((1,), (1,)), ((), ())), preferred_element_type=f32)


def tn(a, b):
    return lax.dot_general(a, b, (((0,), (0,)), ((), ())), preferred_element_type=f32)


def rms(value, gain):
    return value * lax.rsqrt(jnp.mean(value * value, axis=-1, keepdims=True) + epsilon) * gain


def rms_back(value, gain, grad):
    scale = lax.rsqrt(jnp.mean(value * value, axis=-1, keepdims=True) + epsilon)
    unit = value * scale
    slope = grad * gain
    back = scale * (slope - unit * jnp.mean(slope * unit, axis=-1, keepdims=True))
    return back, jnp.sum(grad * unit, axis=0, keepdims=True)


def turn(value, cosine, sine):
    half = value.shape[-1] // 2
    a, b = value[:, :half], value[:, half:]
    return jnp.concatenate([a * cosine - b * sine, b * cosine + a * sine], axis=-1)


def half_plane(which, rows):
    return pl.ds(pl.multiple_of(which * rows, 128), rows)


def slice_kernel(far, part, place, gate, up, own, other0, other1, source, sem):
    rows, ff = gate.shape
    copies = begin([(w, source.at[i, :, :ff]) for i, w in enumerate((gate, up))], sem)
    near, chip = place[NEAR], place[CHIP]
    block = 48
    half = rows // 2

    def cut(i, which, target, from_row, to_row):
        for z in range(far):
            first, last = z * part, (z + 1) * part
            lo, hi = first // 128 * 128, min(-(-last // 128) * 128, far * part)
            span = -(-(hi - lo) // 128) * 128 + 128
            shift = (z * 3 + near * 2 + which) * part
            coarse = shift // 128 * 128
            x = source[i, from_row, at(lo + coarse, span, 128)]
            x = pltpu.roll(x, (span - (shift - coarse)) % span, 1)[:, : hi - lo]
            if first > lo:
                column = lax.broadcasted_iota(jnp.int32, x.shape, 1)
                x = jnp.where(column < first - lo, target[to_row, lo:hi], x)
            target[to_row, lo:hi] = x

    wait(copies)
    for k, other in enumerate((other0, other1)):

        def send(r, _):
            cut(place[PARITY], 1 - chip, other, at(k * half + r * block, block), at(r * block, block))
            return 0

        lax.fori_loop(0, half // block, send, 0)
    for i in range(2):

        def keep(r, _):
            here = at(r * block, block)
            cut(i, chip, own.at[i], here, here)
            return 0

        lax.fori_loop(0, rows // block, keep, 0)


def chip_columns(place, gate, up, far):
    rows, ff = gate.shape
    part = ff // (4 * far)
    source = -(-ff // 128) * 128 + 768
    return call(
        functools.partial(slice_kernel, far, part),
        6,
        (low(2, rows, ff // 4), low(rows // 2, ff // 4), low(rows // 2, ff // 4)),
        [SCALARS, ANYWHERE, ANYWHERE],
        [pltpu.VMEM((2, rows, source), bf16), pltpu.SemaphoreType.DMA((2,))],
        place,
        gate,
        up,
    )


def key_columns(pieces, count):
    return [p.at[:, p.shape[1] - count :] for p in pieces]


def query_columns(pieces, count):
    return [p.at[:, :count] for p in pieces]


def keys_kernel(place, own, peer, gain_in, gain_key, table, k0, k1, k2, k3, normed, pair, raw, every, weight, sem):
    copies = fetch(place, key_columns((k0, k1, k2, k3), weight.shape[1]), weight, sem)
    rows, near, width = own.shape[0], place[0], raw.shape[1]
    mine = rms(own[...].astype(f32), gain_in[...]).astype(bf16)
    normed[...] = mine
    every[half_plane(near, rows)] = mine
    every[half_plane(1 - near, rows)] = rms(peer[...].astype(f32), gain_in[...]).astype(bf16)
    wait(copies)
    projected = nn(every[...], weight[...])
    raw[...] = projected[:, :width]
    pair[0] = turn(rms(projected[:, :width], gain_key[...]), table[0], table[1]).astype(bf16)
    pair[1] = projected[:, width:].astype(bf16)


def keys_of(place, own, peer, gain_in, gain_key, table, pieces):
    rows, model = own.shape
    dim = gain_key.shape[1]
    return call(
        keys_kernel,
        2,
        (low(rows, model), low(2, 2 * rows, dim), wide(2 * rows, dim), low(2 * rows, model)),
        [SCALARS, *[VECTORS] * 5, *[ANYWHERE] * 4],
        [pltpu.VMEM((model, 2 * dim), bf16), pltpu.SemaphoreType.DMA((4,))],
        place, own, peer, gain_in, gain_key, table, *pieces,
    )


def queries_kernel(place, normed, gain, table, q0, q1, q2, q3, queries, raw, weight, sem):
    wait(fetch(place, query_columns((q0, q1, q2, q3), weight.shape[1]), weight, sem))
    rows, dim = normed.shape[0], gain.shape[1]
    here = half_plane(place[0], rows)
    cosine, sine = table[0, here], table[1, here]
    for h in range(HQ):
        projected = nn(normed[...], weight[:, h * dim : (h + 1) * dim])
        raw[h * rows : (h + 1) * rows] = projected
        turned = turn(rms(projected, gain[...]), cosine, sine).astype(bf16)
        queries[h * rows : (h + 1) * rows] = turned * jnp.asarray(dim**-0.5, bf16)


def queries_of(place, normed, gain, table, pieces):
    rows, model = normed.shape
    dim = gain.shape[1]
    return call(
        queries_kernel,
        3,
        (low(HQ * rows, dim), wide(HQ * rows, dim)),
        [SCALARS, *[VECTORS] * 3, *[ANYWHERE] * 4],
        [pltpu.VMEM((model, HQ * dim), bf16), pltpu.SemaphoreType.DMA((4,))],
        place, normed, gain, table, *pieces,
    )


def attend_kernel(
    place, queries, kv0, kv1, kv2, kv3, key_ids, query_ids, tokens, gain_attn, gain_pre, o0, o1, o2, o3,
    chances, heads, attn_out, residual, normed_pre, keys, values, weight, sem,
):
    copies = fetch(place, (o0, o1, o2, o3), weight, sem)
    plane, dim = kv0.shape[1], kv0.shape[2]
    for i, kv in enumerate((kv0, kv1, kv2, kv3)):
        keys[i * plane : (i + 1) * plane] = kv[0]
        values[i * plane : (i + 1) * plane] = kv[1]
    rows, span = query_ids.shape[0], key_ids.shape[1]
    row = lax.broadcasted_iota(jnp.int32, (rows, span), 0) + place[0] * rows
    column = lax.broadcasted_iota(jnp.int32, (rows, span), 1)
    same = key_ids[...] == query_ids[...]
    allowed = same | ((key_ids[...] < query_ids[...]) & (column >= row))
    chances[...] = nt(queries[...], keys[...])
    for h in range(HQ):
        here = slice(h * rows, (h + 1) * rows)
        scores = jnp.where(allowed, chances[here], -1e30)
        grown = jnp.exp(scores - jnp.max(scores, axis=-1, keepdims=True))
        chances[here] = grown / jnp.sum(grown, axis=-1, keepdims=True)
    seen = nn(chances[...].astype(bf16), values[...]).astype(bf16)
    for h in range(HQ):
        heads[:, h * dim : (h + 1) * dim] = seen[h * rows : (h + 1) * rows]
    wait(copies)
    out = nn(heads[...], weight[...])
    attn_out[...] = out
    total = tokens[...].astype(f32) + rms(out, gain_attn[...])
    residual[...] = total
    normed_pre[...] = rms(total, gain_pre[...]).astype(bf16)


def attend(place, queries, planes, key_ids, query_ids, tokens, gain_attn, gain_pre, pieces):
    rows, model = tokens.shape
    dim, span = queries.shape[1], key_ids.shape[1]
    return call(
        attend_kernel,
        5,
        (wide(HQ * rows, span), low(rows, HQ * dim), wide(rows, model), wide(rows, model), low(rows, model)),
        [SCALARS, *[VECTORS] * 10, *[ANYWHERE] * 4],
        [
            pltpu.VMEM((span, dim), bf16),
            pltpu.VMEM((span, dim), bf16),
            pltpu.VMEM((HQ * dim, model), bf16),
            pltpu.SemaphoreType.DMA((4,)),
        ],
        place, queries, *planes, key_ids, query_ids, tokens, gain_attn, gain_pre, *pieces,
    )


def gated(gate, up):
    square = gate * gate
    wave = jnp.tanh(ROOT * gate * (1.0 + 0.044715 * square))
    half = 0.5 * (1.0 + wave)
    value = gate * half
    bend = half + 0.5 * ROOT * gate * (1.0 - wave * wave) * (1.0 + 3.0 * 0.044715 * square)
    return (value * up).astype(bf16), (bend * up).astype(bf16), value.astype(bf16)


def forward_kernel(place, x0, x1, x2, x3, *refs):
    gates, downs = refs[:10], refs[10:14]
    whole, hidden, slope, gelu, total, p1, p2, p3 = refs[14:22]
    w_gates, w_down, sem, late_sem = refs[22:]
    copies = fetch_gates(place, gates, w_gates, sem)
    late = fetch(place, downs, w_down, late_sem)
    rows = x0.shape[0]
    for i, x in enumerate((x0, x1, x2, x3)):
        whole[i * rows : (i + 1) * rows] = x[...]
    wait(copies)
    for first, last in steps(w_down.shape[0], 256):
        gate = nn(whole[...], w_gates[0, :, first:last])
        up = nn(whole[...], w_gates[1, :, first:last])
        hidden[:, first:last], slope[:, first:last], gelu[:, first:last] = gated(gate, up)
    wait(late)
    for first, last in steps(w_down.shape[1], 384):
        part = nn(hidden[...], w_down[:, first:last])
        total[:, first:last] = part[:rows]
        for i, p in enumerate((p1, p2, p3)):
            p[:, first:last] = part[(i + 1) * rows : (i + 2) * rows].astype(bf16)


def weight_room(model, ff):
    return [
        pltpu.VMEM((2, model, ff), bf16),
        pltpu.VMEM((ff, model), bf16),
        pltpu.SemaphoreType.DMA((10,)),
        pltpu.SemaphoreType.DMA((6,)),
    ]


def forward(place, blocks, gates, downs):
    rows, model = blocks[0].shape
    ff = gates[0].shape[2]
    return call(
        forward_kernel,
        13,
        (low(4 * rows, model), *[low(4 * rows, ff)] * 3, wide(rows, model), *[low(rows, model)] * 3),
        [SCALARS, *[VECTORS] * 4, *[ANYWHERE] * 14],
        weight_room(model, ff),
        place, *blocks, *gates, *downs,
    )


def backward_kernel(place, x0, x1, x2, x3, slope, gelu, *refs):
    gates, downs = refs[:10], refs[10:14]
    whole, gate_low, up_low, total, p1, p2, p3 = refs[14:21]
    w_gates, w_down, late_sem, sem = refs[21:]
    copies = fetch(place, downs, w_down, sem)
    late = fetch_gates(place, gates, w_gates, late_sem)
    rows = x0.shape[0]
    for i, x in enumerate((x0, x1, x2, x3)):
        whole[i * rows : (i + 1) * rows] = x[...]
    wait(copies)
    for first, last in steps(w_down.shape[0], 256):
        back = nt(whole[...], w_down[first:last])
        gate_low[:, first:last] = (back * slope[:, first:last].astype(f32)).astype(bf16)
        up_low[:, first:last] = (back * gelu[:, first:last].astype(f32)).astype(bf16)
    wait(late)
    for first, last in steps(w_down.shape[1], 384):
        part = nt(gate_low[...], w_gates[0, first:last]) + nt(up_low[...], w_gates[1, first:last])
        total[:, first:last] = part[:rows]
        for i, p in enumerate((p1, p2, p3)):
            p[:, first:last] = part[(i + 1) * rows : (i + 2) * rows].astype(bf16)


def backward(place, blocks, slope, gelu, gates, downs):
    rows, model = blocks[0].shape
    ff = gates[0].shape[2]
    return call(
        backward_kernel,
        15,
        (low(4 * rows, model), *[low(4 * rows, ff)] * 2, wide(rows, model), *[low(rows, model)] * 3),
        [SCALARS, *[VECTORS] * 6, *[ANYWHERE] * 14],
        weight_room(model, ff),
        place, *blocks, slope, gelu, *gates, *downs,
    )


def far_kernel(window, place, own, n0, n1, n2, n3, *refs):
    gates, (hiddens, slope, gelu, w_gates, tokens, room, sem) = refs[:10], refs[10:]
    start, width = window
    copies = fetch_gates(place, gates, w_gates, sem)
    rows = n0.shape[0]
    for i, n in enumerate((n0, n1, n2, n3)):
        tokens[i * rows : (i + 1) * rows] = n[...]
    hiddens[:, : 4 * rows] = own[...].T
    wait(copies)
    for first, last in steps(hiddens.shape[0], 256):
        gate = nn(tokens[...], w_gates[0, :, first:last])
        up = nn(tokens[...], w_gates[1, :, first:last])
        value, room[0, :, first:last], room[1, :, first:last] = gated(gate, up)
        hiddens[first:last, 4 * rows :] = value.T
    here = at(place[HALF] * start, width, 128)
    slope[...] = room[0, :, here]
    gelu[...] = room[1, :, here]


def window_of(ff):
    start = ff // 2 // 128 * 128
    return start, ff - start


def far_hidden(place, hidden, far_normed, gates):
    rows, model = far_normed[0].shape
    ff = gates[0].shape[2]
    start, width = window_of(ff)
    return call(
        functools.partial(far_kernel, (start, width)),
        11,
        (low(ff, 8 * rows), low(4 * rows, width), low(4 * rows, width)),
        [SCALARS, *[VECTORS] * 5, *[ANYWHERE] * 10],
        [
            pltpu.VMEM((2, model, ff), bf16),
            pltpu.VMEM((4 * rows, model), bf16),
            pltpu.VMEM((2, 4 * rows, ff), bf16),
            pltpu.SemaphoreType.DMA((10,)),
        ],
        place, hidden, *far_normed, *gates,
    )


def weights_kernel(
    window, place, h_normed, h_down, h_gate, h_up, n0, n1, n2, n3, d0, d1, d2, d3, h_hiddens, h_slope, h_gelu, w0, w1, w2, w3,
    h_keep, h_send, w_down, grads, tokens, backs, gate_low, up_low, hiddens, slope, gelu, keep, send,
    sem, soon_sem, late_sem, out_sem,
):
    start, width = window
    half, core, bit = place[HALF], place[CORE], place[BIT]
    own, model = h_normed.shape
    rows = own // 4
    columns = at(half * start, width, 128)

    def blocks(parts, target):
        return [(p, target.at[own + i * rows : own + (i + 1) * rows]) for i, p in enumerate(parts)]

    first = begin([(h_gate, gate_low), (h_up, up_low)], sem)
    soon = [*blocks((d0, d1, d2, d3), backs), (h_slope, slope), (h_gelu, gelu), (h_down, backs.at[:own])]
    for slot, piece in zip(slots(place), (w0, w1, w2, w3)):
        soon.append((piece, w_down.at[at(slot * piece.shape[0], piece.shape[0])]))
    soon = begin(soon, soon_sem)
    late = begin([*blocks((n0, n1, n2, n3), tokens), (h_normed, tokens.at[:own]), (h_hiddens, hiddens)], late_sem)
    wait(first)
    grads[core, :, :own] = gate_low[:, columns].T
    grads[1 - core, :, :own] = up_low[:, columns].T
    wait(soon)
    for first, last in steps(width, 256):
        back = nt(backs[own:], w_down[at(half * start + first, last - first)])
        c = slice(first, last)
        grads[core, c, own:] = (back * slope[:, c].astype(f32)).astype(bf16).T
        grads[1 - core, c, own:] = (back * gelu[:, c].astype(f32)).astype(bf16).T
    wait(late)
    kept = hiddens.shape[0] // 2
    part = kept // 2
    results = []
    for i in range(2):
        r = at(half * (kept - start) + i * part, part)
        slot = i ^ bit
        keep[slot, :, :model] = nn(grads[0, r], tokens[...]).astype(bf16)
        send[slot, :, :model] = nn(grads[1, r], tokens[...]).astype(bf16)
    gates = pl.ds(0, model)
    results += [(keep.at[:, :, gates], h_keep.at[:, :, gates]), (send.at[:, :, gates], h_send.at[:, :, gates])]
    done = begin(results, out_sem)
    span = keep.shape[2] - model
    columns = at(half * (model - span), span, 128)
    for i in range(4):
        result = nn(hiddens[i * part : (i + 1) * part], backs[:, columns]).astype(bf16)

        @pl.when(core == i % 2)
        def _():
            keep[i // 2, :, model:] = result

        @pl.when(core != i % 2)
        def _():
            send[i // 2, :, model:] = result

    rest = pl.ds(model, span)
    for i, (a, b) in enumerate(((keep, h_keep), (send, h_send))):
        copy = pltpu.make_async_copy(a.at[:, :, rest], b.at[:, :, rest], out_sem.at[2 + i])
        copy.start()
        done.append(copy)
    wait(done)


def weight_grads(place, normed, down, gate_low, up_low, far_normed, far_down, far_kept, downs):
    own, model = normed.shape
    ff = gate_low.shape[1]
    start, width = window_of(ff)
    part = ff // 4
    span = -(-model // 256) * 128
    shape = (2, part, model + span)
    return pl.pallas_call(
        functools.partial(weights_kernel, (start, width)),
        out_shape=(low(*shape), low(*shape)),
        in_specs=[SCALARS, *[ANYWHERE] * 19],
        out_specs=(ANYWHERE, ANYWHERE),
        scratch_shapes=[
            pltpu.VMEM((ff, model), bf16),
            pltpu.VMEM((2, width, 2 * own), bf16),
            pltpu.VMEM((2 * own, model), bf16),
            pltpu.VMEM((2 * own, model), bf16),
            pltpu.VMEM((own, ff), bf16),
            pltpu.VMEM((own, ff), bf16),
            pltpu.VMEM((ff, 2 * own), bf16),
            pltpu.VMEM((own, width), bf16),
            pltpu.VMEM((own, width), bf16),
            pltpu.VMEM(shape, bf16),
            pltpu.VMEM(shape, bf16),
            pltpu.SemaphoreType.DMA((2,)),
            pltpu.SemaphoreType.DMA((11,)),
            pltpu.SemaphoreType.DMA((6,)),
            pltpu.SemaphoreType.DMA((4,)),
        ],
        cost_estimate=pl.CostEstimate(flops=16_000_000_000, bytes_accessed=1 << 20, transcendentals=0),
        compiler_params=pltpu.CompilerParams(vmem_limit_bytes=48 << 20),
    )(place, normed, down, gate_low, up_low, *far_normed, *far_down, *far_kept, *downs)


def turning_kernel(own, r1, r2, r3, residual, cotangent, gain, output, grad, grad_gain):
    down = own[...] + r1[...].astype(f32) + r2[...].astype(f32) + r3[...].astype(f32)
    output[...] = (residual[...] + rms(down, gain[...])).astype(bf16)
    back, grad_gain[...] = rms_back(down, gain[...], cotangent[...].astype(f32))
    grad[...] = back.astype(bf16)


def turning(parts, residual, cotangent, gain):
    rows, model = residual.shape
    return call(
        turning_kernel,
        1,
        (low(rows, model), low(rows, model), wide(1, model)),
        [VECTORS] * 7,
        [],
        *parts, residual, cotangent, gain,
    )


def cores_kernel(place, keep, got, gates, send_other, send_own, down, send_down, turned):
    model = gates.shape[1]
    gates[...] = keep[0, :, :model].astype(f32) + got[0, :, :model].astype(f32)
    sent = keep[1, :, :model].astype(f32) + got[1, :, :model].astype(f32)
    half, short = model // 2, send_own.shape[0]
    for i in range(2):

        @pl.when(place[CHIP] == i)
        def _():
            for target, j in ((send_own, i), (send_other, 1 - i)):
                for k in range(2):
                    block = sent[k * short : (k + 1) * short, j * half : (j + 1) * half]
                    target[:, k * half : (k + 1) * half] = block.astype(bf16)

    unit, part = down.shape[0], turned.shape[2]
    first = place[HALF] * (turned.shape[1] - 2 * unit)
    for i in range(2):
        turned[i] = (keep[i, :, model:].astype(f32) + got[i, :, model:].astype(f32)).T
        for target, bit in ((down, place[BIT]), (send_down, 1 - place[BIT])):
            target[:, i * part : (i + 1) * part] = turned[i, at(first + bit * unit, unit)].astype(target.dtype)


def add_cores(place, keep, got, model):
    part = keep.shape[1]
    return call(
        cores_kernel,
        4,
        (
            wide(part, model), low(part // 2, model), low(part // 2, model),
            wide(model // 4, 2 * part), low(model // 4, 2 * part),
        ),
        [SCALARS, *[VECTORS] * 2],
        [pltpu.VMEM((2, keep.shape[2] - model, part), f32)],
        place, keep, got,
    )


def gates_kernel(flip, place, gates, got, total):
    half, unit = got.shape[1] // 2, total.shape[1]
    both = jnp.concatenate([got[:, :half].astype(f32), got[:, half:].astype(f32)], axis=0)
    for i in range(2):

        @pl.when(place[CHIP] == (1 - i if flip else i))
        def _():
            turned = (gates[:, i * half : (i + 1) * half] + both).T.astype(bf16)
            for k in range(2):
                total[k] = turned[k * unit : (k + 1) * unit]


def add_gates(flip, place, gates, got):
    part, model = gates.shape
    return call(
        functools.partial(gates_kernel, flip), 2, low(2, model // 4, part), [SCALARS, *[VECTORS] * 2], [], place, gates, got
    )


def gather_gates_kernel(place, own, peer, got_own, got_peer, gate, up):
    part = own.shape[1]
    for core in range(2):
        for chip in range(2):

            @pl.when((place[CORE] == core) & (place[CHIP] == chip))
            def _():
                here, there = (gate, up) if core == 0 else (up, gate)
                for target, first, second in ((here, own, peer), (there, got_own, got_peer)):
                    target[:, chip * part : (chip + 1) * part] = first[...].astype(f32)
                    target[:, (1 - chip) * part : (2 - chip) * part] = second[...].astype(f32)


def gather_gates(place, own, peer, got_own, got_peer):
    rows, part = own.shape
    return call(
        gather_gates_kernel,
        2,
        (wide(rows, 2 * part), wide(rows, 2 * part)),
        [SCALARS, *[VECTORS] * 4],
        [],
        place, own, peer, got_own, got_peer,
    )


def down_kernel(down, got, total):
    part = total.shape[2]
    for i in range(2):
        c = slice(i * part, (i + 1) * part)
        total[i] = (down[:, c] + got[:, c].astype(f32)).astype(bf16)


def add_down(down, got):
    rows, width = down.shape
    return call(down_kernel, 1, low(2, rows, width // 2), [VECTORS] * 2, [], down, got)


def attend_back_kernel(
    far, early, place, h_own, h_r1, h_r2, h_r3, h_residual, h_attn_out, h_cotangent, h_chances, h_queries, h_raw, h_table,
    gain_pre, gain_attn, gain_query,
    kv0, kv1, kv2, kv3, o0, o1, o2, o3,
    grad_residual, keep, send, grad_gains, grad_gain_query, grad_projected, g0, g1, g2, g3,
    own, r1, r2, r3, residual, attn_out, cotangent, chances, queries, raw, table,
    keys, values, attn_low, heads, dull, grad_share, weight, sem, soon_sem, late_sem,
):
    plane, dim = kv0.shape[1], kv0.shape[2]
    soon = begin(
        [
            (h_own, own), (h_r1, r1), (h_r2, r2), (h_r3, r3),
            (h_residual, residual), (h_attn_out, attn_out), (h_cotangent, cotangent),
        ],
        soon_sem,
    )
    copies = fetch(place, (o0, o1, o2, o3), weight, sem)
    late = [(h_chances, chances), (h_queries, queries), (h_raw, raw), (h_table, table)]
    for i, kv in enumerate((kv0, kv1, kv2, kv3)):
        late += [(kv.at[0], keys.at[i * plane : (i + 1) * plane]), (kv.at[1], values.at[i * plane : (i + 1) * plane])]
    copies += begin(late, late_sem)
    wait(soon)
    normed = own[...] + r1[...].astype(f32) + r2[...].astype(f32) + r3[...].astype(f32)
    back, grad_gains[0:1] = rms_back(residual[...], gain_pre[...], normed)
    total = cotangent[...].astype(f32) + back
    grad_residual[...] = total
    back, grad_gains[1:2] = rms_back(attn_out[...], gain_attn[...], total)
    attn_low[...] = back.astype(bf16)
    wait(copies)
    rows = own.shape[0]
    here = half_plane(place[0], rows)
    cosine, sine = table[0, here], table[1, here]
    grad_heads = nt(attn_low[...], weight[...]).astype(bf16)
    for h in range(HQ):
        heads[h * rows : (h + 1) * rows] = grad_heads[:, h * dim : (h + 1) * dim]
    grad_share[...] = nt(heads[...], values[...])
    for h in range(HQ):
        r = slice(h * rows, (h + 1) * rows)
        share, back = chances[r], grad_share[r]
        dull[r] = (share * (back - jnp.sum(share * back, axis=-1, keepdims=True))).astype(bf16)
    turned = nn(dull[...], keys[...]) * (dim**-0.5)
    gain_total = jnp.zeros_like(grad_gain_query)
    for h in range(HQ):
        r = slice(h * rows, (h + 1) * rows)
        back, gain_part = rms_back(raw[r], gain_query[...], turn(turned[r], cosine, -sine))
        gain_total = gain_total + gain_part
        grad_projected[:, h * dim : (h + 1) * dim] = back.astype(bf16)
    grad_gain_query[...] = gain_total
    for i, g in enumerate((g0, g1, g2, g3)):
        c = slice(i * plane, (i + 1) * plane)
        g[0] = tn(dull[:, c], queries[...]).astype(g.dtype)
        g[1] = tn(chances[:, c].astype(bf16), heads[...]).astype(g.dtype)
    block, size = grad_projected.shape[1] * 3 // 2 // (2 * far), attn_low.shape[1] // (2 * far)
    parts = [
        columns_of(grad_projected[...], i, range(early), block) + columns_of(attn_low[...], i, range(far), size) for i in range(2)
    ]
    for i in range(2):

        @pl.when(place[NEAR] == i)
        def _():
            keep[...] = jnp.concatenate(parts[i], axis=1)
            send[...] = jnp.concatenate(parts[1 - i], axis=1)


def attend_back(far, early, place, parts, residual, attn_out, cotangent, gain_pre, gain_attn, chances, queries, raw, table, gain_query, planes, pieces):
    rows, model = residual.shape
    dim, span = queries.shape[1], chances.shape[1]
    plane = planes[0].shape[1]
    sent = low(2, plane, dim)
    width = early * HQ * dim * 3 // 2 // (2 * far) + model // 2
    return call(
        functools.partial(attend_back_kernel, far, early),
        8,
        (
            wide(rows, model), low(rows, width), low(rows, width), wide(2, model), wide(1, dim), low(rows, HQ * dim),
            sent, sent, wide(2, plane, dim), sent,
        ),
        [SCALARS, *[ANYWHERE] * 11, *[VECTORS] * 3, *[ANYWHERE] * 8],
        [
            pltpu.VMEM((rows, model), f32),
            *[pltpu.VMEM((rows, model), bf16)] * 3,
            *[pltpu.VMEM((rows, model), f32)] * 2,
            pltpu.VMEM((rows, model), bf16),
            pltpu.VMEM((HQ * rows, span), f32),
            pltpu.VMEM((HQ * rows, dim), bf16),
            pltpu.VMEM((HQ * rows, dim), f32),
            pltpu.VMEM((2, 2 * rows, dim // 2), f32),
            pltpu.VMEM((span, dim), bf16),
            pltpu.VMEM((span, dim), bf16),
            pltpu.VMEM((rows, model), bf16),
            pltpu.VMEM((HQ * rows, dim), bf16),
            pltpu.VMEM((HQ * rows, span), bf16),
            pltpu.VMEM((HQ * rows, span), f32),
            pltpu.VMEM((HQ * dim, model), bf16),
            pltpu.SemaphoreType.DMA((4,)),
            pltpu.SemaphoreType.DMA((7,)),
            pltpu.SemaphoreType.DMA((12,)),
        ],
        place, *parts, residual, attn_out, cotangent, chances, queries, raw, table, gain_pre, gain_attn, gain_query, *planes, *pieces,
        megabytes=56,
    )


def queries_back_kernel(place, grad, q0, q1, q2, q3, result, weight, sem):
    wait(fetch(place, query_columns((q0, q1, q2, q3), weight.shape[1]), weight, sem))
    result[...] = nt(grad[...], weight[...])


def queries_back(place, grad, pieces):
    rows, width = grad.shape
    model = pieces[0].shape[0] * 4
    return call(
        queries_back_kernel,
        3,
        wide(rows, model),
        [SCALARS, VECTORS, *[ANYWHERE] * 4],
        [pltpu.VMEM((model, width), bf16), pltpu.SemaphoreType.DMA((4,))],
        place, grad, *pieces,
    )


def columns_of(value, near, blocks, size):
    return [value[:, (2 * f + near) * size : (2 * f + near + 1) * size] for f in blocks]


def by_place(index, choices):
    for i, choice in enumerate(choices):
        pl.when(index == i)(choice)


def first_products_kernel(place, every, own_heads, got_heads, own, got, keep, send, right, heads):
    rows, near, core = own.shape[0], place[NEAR], place[CORE]
    for target, mine, theirs in ((right, own, got), (heads, own_heads, got_heads)):
        target[half_plane(near, rows)] = mine[...]
        target[half_plane(1 - near, rows)] = theirs[...]
    unit, head = keep.shape[1], heads.shape[1] // 4
    width = keep.shape[2] - 2 * head
    part = tn(every[...], right[:, :width])
    out = tn(right[:, width:], heads[...])
    for i in range(4):
        here = part[i * unit : (i + 1) * unit]
        there = [out[k * unit : (k + 1) * unit, i * head : (i + 1) * head] for k in range(2)]
        for target, chosen in ((keep, core == i % 2), (send, core != i % 2)):

            @pl.when(chosen)
            def _():
                target[i // 2, :, :width] = here.astype(target.dtype)
                for k in range(2):
                    first = width + k * head
                    target[i // 2, :, first : first + head] = there[k].astype(target.dtype)


def first_products(place, every, own_heads, got_heads, own, got):
    rows, model = own_heads.shape[0], every.shape[1]
    width = own.shape[1] - model // 2 + own_heads.shape[1] // 2
    return call(
        first_products_kernel,
        4,
        (wide(2, model // 4, width), low(2, model // 4, width)),
        [SCALARS, *[VECTORS] * 5],
        [pltpu.VMEM((2 * rows, own.shape[1]), bf16), pltpu.VMEM((2 * rows, own_heads.shape[1]), bf16)],
        place, every, own_heads, got_heads, own, got,
    )


def first_cores_kernel(place, keep, got, new, send):
    chip = place[CHIP]
    new[...] = keep[chip] + got[chip].astype(f32)
    send[...] = (keep[1 - chip] + got[1 - chip].astype(f32)).astype(bf16)


def first_cores(place, keep, got):
    shape = keep.shape[1:]
    return call(first_cores_kernel, 2, (wide(*shape), low(*shape)), [SCALARS, *[VECTORS] * 2], [], place, keep, got)


def last_products_kernel(place, every, own, got, gains, keep, send, total_gains, right):
    rows, near, core = own.shape[0], place[NEAR], place[CORE]
    right[half_plane(near, rows)] = own[...]
    right[half_plane(1 - near, rows)] = got[:rows]
    sums = gains[...] + got[rows:].astype(f32)
    total_gains[...] = sums
    unit = keep.shape[1]
    part = tn(every[...], right[...])
    for i in range(4):
        x, c = i // 2, i % 2
        here = part[i * unit : (i + 1) * unit]

        @pl.when(core == c)
        def _():
            keep[x] = here

        @pl.when(core != c)
        def _():
            send[x * unit : (x + 1) * unit] = here.astype(bf16)

    send[2 * unit :] = sums.astype(bf16)


def last_products(place, every, own, got, gains):
    rows, width = own.shape
    unit, more = every.shape[1] // 4, gains.shape[0]
    return call(
        last_products_kernel,
        3,
        (wide(2, unit, width), low(2 * unit + more, width), wide(more, width)),
        [SCALARS, *[VECTORS] * 4],
        [pltpu.VMEM((2 * rows, width), bf16)],
        place, every, own, got, gains,
    )


def last_cores_kernel(place, keep, got, gains, new, send, total_gains):
    unit, chip = new.shape[0], place[CHIP]
    new[...] = keep[chip] + got[at(chip * unit, unit)].astype(f32)
    send[:unit] = (keep[1 - chip] + got[at((1 - chip) * unit, unit)].astype(f32)).astype(bf16)
    sums = gains[...] + got[2 * unit :].astype(f32)
    total_gains[...] = sums
    send[unit:] = sums.astype(bf16)


def last_cores(place, keep, got, gains):
    _, unit, width = keep.shape
    more = gains.shape[0]
    return call(
        last_cores_kernel,
        1,
        (wide(unit, width), low(unit + more, width), wide(more, width)),
        [SCALARS, *[VECTORS] * 3],
        [],
        place, keep, got, gains,
    )


def layout(far, unit, columns, head, gains):
    size, short = columns // far, 2 * unit // far
    lanes = -(-size // 128) * 128
    free = lanes - size
    beside = unit // (head // free) if free and head % free == 0 else 0
    beside = beside if beside <= short and beside * (head // max(free, 1)) == unit else 0
    rest = (short - beside) * head // lanes
    return size, short, lanes, beside, rest, -(-(unit + rest + -(-gains // lanes)) // 16) * 16


def chips_kernel(count, first, got_first, keep, got, gains, out, room, line, block):
    unit, early = first.shape[0], room.shape[1] - keep.shape[1]
    far, head = out.shape[0], (first.shape[1] - early) // 2
    size, short, lanes, beside, rest, _ = layout(far, unit, room.shape[1], head, count)
    room[:, :early] = first[:, :early] + got_first[:, :early].astype(f32)
    room[:, early:] = keep[...] + got[:unit].astype(f32)
    sums = gains[...] + got[unit:].astype(f32)
    width, more = gains.shape[1], -(-count // lanes)
    line[...] = jnp.zeros_like(line)
    for i in range(0, more * lanes, width):
        here = min(width, more * lanes - i)
        line[:, i : i + here] = sums[i // width : i // width + 1, :here]
    block[...] = jnp.zeros_like(block)
    for i in range(more):
        block[unit + rest + i : unit + rest + i + 1] = line[:, i * lanes : (i + 1) * lanes]
    for half in range(2):
        start = early + half * head
        part = first[:, start : start + head] + got_first[:, start : start + head].astype(f32)
        for k in range(far // 2):
            f = half * (far // 2) + k
            mine = part[k * short : (k + 1) * short]
            block[:unit, :size] = room[:, f * size : (f + 1) * size]
            for g in range(unit // beside if beside else 0):
                block[g * beside : (g + 1) * beside, size:] = mine[:beside, g * (lanes - size) : (g + 1) * (lanes - size)]
            for j in range(head // lanes):
                start_row = unit + j * (short - beside)
                block[start_row : start_row + short - beside] = mine[beside:, j * lanes : (j + 1) * lanes]
            out[f] = block[...].astype(bf16)


def last_chips(far, first, got_first, keep, got, gains, head, count):
    unit, width = keep.shape
    columns = first.shape[1] - 2 * head + width
    _, _, lanes, _, _, rows = layout(far, unit, columns, head, count)
    return call(
        functools.partial(chips_kernel, count),
        3,
        low(far, rows, lanes),
        [VECTORS] * 5,
        [pltpu.VMEM((unit, columns), f32), pltpu.VMEM((1, -(-count // lanes) * lanes), f32), pltpu.VMEM((rows, lanes), f32)],
        first, got_first, keep, got, gains,
    )


def last_sum_kernel(count, parts, total, out, gains):
    unit, head = total.shape[0], out.shape[1]
    far = parts.shape[0]
    size, short, lanes, beside, rest, _ = layout(far, unit, total.shape[1] * far, head, count)
    sums = jnp.sum(parts[...].astype(f32), axis=0)
    total[...] = sums[:unit, :size]
    for g in range(unit // beside if beside else 0):
        out[:beside, g * (lanes - size) : (g + 1) * (lanes - size)] = sums[g * beside : (g + 1) * beside, size:]
    for j in range(head // lanes):
        start_row = unit + j * (short - beside)
        out[beside:, j * lanes : (j + 1) * lanes] = sums[start_row : start_row + short - beside]
    for i in range(-(-count // lanes)):
        gains[:, i * lanes : (i + 1) * lanes] = sums[unit + rest + i : unit + rest + i + 1]


def last_sum(parts, unit, columns, head, count):
    far, _, lanes = parts.shape
    return call(
        functools.partial(last_sum_kernel, count),
        2,
        (wide(unit, columns // far), wide(2 * unit // far, head), wide(1, -(-count // lanes) * lanes)),
        [VECTORS],
        [],
        parts,
    )


def down_rows_kernel(part, parts, result):
    for i in range(4):
        for z in range(parts.shape[2] // part):
            first = (4 * z + i) * part
            result[:, first : first + part] = parts[i, :, z * part : (z + 1) * part].astype(f32)


def down_rows(parts, part):
    _, columns, rows = parts.shape
    return call(functools.partial(down_rows_kernel, part), 2, wide(columns, 4 * rows), [VECTORS], [], parts)


def keys_back_kernel(
    early, place, total, received, raw, table, gain_key, partial, grad_residual, tokens, gain_in, grad_queries, grad_gains,
    grad_gain_post, grad_gain_query, k0, k1, k2, k3, grad_tokens, keep, send, sums, grad_projected, gains, weight, sem,
):
    copies = fetch(place, key_columns((k0, k1, k2, k3), weight.shape[1]), weight, sem)
    rows, dim = tokens.shape[0], raw.shape[1]
    here = half_plane(place[0], rows)
    keys = total[0, here] + received[0].astype(f32)
    values = total[1, here] + received[1].astype(f32)
    back, grad_gain_key = rms_back(raw[here], gain_key[...], turn(keys, table[0, here], -table[1, here]))
    grad_projected[:, :dim] = back.astype(bf16)
    grad_projected[:, dim:] = values.astype(bf16)
    wait(copies)
    normed = partial[...] + nt(grad_projected[...], weight[...])
    back, grad_gain_in = rms_back(tokens[...].astype(f32), gain_in[...], normed)
    grad_tokens[...] = grad_residual[...] + back
    model, width = tokens.shape[1], keep.shape[1]
    gains[...] = jnp.zeros_like(gains)
    gains[:, :model] = grad_gain_in
    for i in range(2):
        gains[:, (i + 1) * model : (i + 2) * model] = grad_gains[i : i + 1]
    gains[:, 3 * model : 4 * model] = grad_gain_post[...]
    gains[:, 4 * model : 4 * model + dim] = grad_gain_query[...]
    gains[:, 4 * model + dim : 4 * model + 2 * dim] = grad_gain_key
    block = grad_queries.shape[1] * 3 // 2 // (2 * early[0])
    every = jnp.concatenate([grad_queries[:, early[1] * 2 * block :], grad_projected[...]], axis=1)
    parts = [jnp.concatenate(columns_of(every, i, range(early[0] - early[1]), block), axis=1) for i in range(2)]
    for i in range(2):

        @pl.when(place[NEAR] == i)
        def _():
            keep[...] = parts[i]
            send[:rows] = parts[1 - i]

    extra = jnp.concatenate([gains[:, i * width : (i + 1) * width] for i in range(sums.shape[0])], axis=0)
    sums[...] = extra
    send[rows:] = extra.astype(bf16)


def keys_back(
    far, early, place, total, received, raw, table, gain_key, partial, grad_residual, tokens, gain_in, grad_queries, grad_gains,
    grad_gain_post, grad_gain_query, pieces,
):
    rows, model = tokens.shape
    dim = raw.shape[1]
    width = (far - early) * (HQ + 2) * dim // (2 * far)
    more = -(-(4 * model + 2 * dim) // (16 * width)) * 16
    return call(
        functools.partial(keys_back_kernel, (far, early)),
        4,
        (wide(rows, model), low(rows, width), low(rows + more, width), wide(more, width)),
        [SCALARS, *[VECTORS] * 13, *[ANYWHERE] * 4],
        [
            pltpu.VMEM((rows, 2 * dim), bf16),
            pltpu.VMEM((1, more * width), f32),
            pltpu.VMEM((model, 2 * dim), bf16),
            pltpu.SemaphoreType.DMA((4,)),
        ],
        place, total, received, raw, table, gain_key, partial, grad_residual, tokens, gain_in, grad_queries, grad_gains,
        grad_gain_post, grad_gain_query, *pieces,
    )


def shift(value, by):
    length = lax.axis_size("far")
    pairs = [(i, i + by) for i in range(length) if 0 <= i + by < length]
    return lax.ppermute(value, "far", pairs)


def swap(value, axis):
    return lax.ppermute(value, axis, [(0, 1), (1, 0)])


def diagonal(value):
    return lax.ppermute(value, ("near", "chip"), [(i, 3 - i) for i in range(4)])


def around(values):
    return swap(values[0], "chip"), swap(values[1], "near"), diagonal(values[2])


def far_swap(value, step):
    return lax.ppermute(value, "far", [(i, i ^ step) for i in range(lax.axis_size("far"))])


def after(value, *others):
    return lax.optimization_barrier((value, others))[0]


def halving(value, axis, steps):
    place = lax.axis_index("far")
    for step in steps:
        shape = (*value.shape[:axis], 2, value.shape[axis] // 2, *value.shape[axis + 1 :])
        value = value.reshape(shape)
        bit = place // step % 2
        mine = lax.dynamic_index_in_dim(value, bit, axis, keepdims=False)
        other = lax.dynamic_index_in_dim(value, 1 - bit, axis, keepdims=False)
        value = mine + far_swap(other.astype(bf16), step).astype(f32)
    return value


def shards(
    tokens,
    block_ids,
    w_qkv,
    w_out,
    w_gate,
    w_up,
    w_down,
    gain_in,
    gain_query,
    gain_key,
    gain_attn,
    gain_pre,
    gain_post,
    cotangent,
):
    seq_count, rows, model = tokens.shape
    dim = gain_query.shape[0]
    query_width = HQ * dim
    plane = 2 * rows
    span = WINDOW + plane + BLOCK
    full_len = block_ids.shape[1]
    far_count = lax.axis_size("far")
    near, chip, core = lax.axis_index("near"), lax.axis_index("chip"), lax.axis_index("core")
    far = lax.axis_index("far")
    half_far = far_count // 2
    far_bits = [1 << i for i in reversed(range(far_count.bit_length() - 1))]
    low_bits = far_bits[1:]
    half = far // half_far
    bit = far // low_bits[0] % 2
    place = jnp.stack([near, chip, core, far % 2, half, bit]).astype(jnp.int32)
    start = far * plane
    ff = w_gate.shape[1]
    part = ff // (far_count * 4)
    early = query_width // (w_qkv.shape[1] // far_count)
    tokens = tokens.reshape(rows, model)
    cotangent = cotangent.reshape(rows, model)
    gain_in, gain_query, gain_key, gain_attn, gain_pre, gain_post = (
        g.reshape(1, -1) for g in (gain_in, gain_query, gain_key, gain_attn, gain_pre, gain_post)
    )

    qkv_chip, peer_tokens = swap(w_qkv, "chip"), swap(tokens, "near")
    gates_own, *gates_other = chip_columns(place, w_gate, w_up, far_count)
    split = lax.dynamic_index_in_dim(w_down.reshape(-1, 2, 2, part, model), near, 1, keepdims=False)
    down_own = lax.dynamic_index_in_dim(split, chip, 1, keepdims=False).reshape(-1, model)
    down_other = lax.dynamic_index_in_dim(split, 1 - chip, 1, keepdims=False).reshape(-1, model)
    qkv_core, out_core, down_core = swap(w_qkv, "core"), swap(w_out, "core"), swap(down_own, "core")
    qkv_pieces = w_qkv, qkv_chip, qkv_core, swap(qkv_chip, "core")

    frequency = 10000.0 ** (-jnp.arange(dim // 2, dtype=f32) * 2.0 / dim)
    angles = (start + jnp.arange(plane)).astype(f32)[:, None] * frequency[None, :]
    table = jnp.stack([jnp.cos(angles), jnp.sin(angles)])
    normed_in, pair, raw_keys, every = keys_of(
        place, after(tokens, down_core, out_core, gates_own), peer_tokens, gain_in, gain_key, table, qkv_pieces
    )
    gates_core = swap(gates_own, "core")
    out_chip = swap(after(w_out, qkv_chip), "chip")
    first = swap(after(gates_other[0], qkv_chip), "chip")
    second = swap(after(gates_other[1], out_chip), "chip")
    down_chip = swap(after(down_other, first), "chip")
    out_pieces = w_out, out_chip, out_core, swap(out_chip, "core")
    first_rest, second_rest = far_swap(first, 1), far_swap(second, 1)
    four = first, second, first_rest, second_rest
    gates = gates_own, gates_core, *four, *(swap(p, "core") for p in four)
    downs = down_own, down_chip, down_core, swap(down_chip, "core")

    padded = jnp.pad(block_ids, ((0, 0), (WINDOW, BLOCK)), constant_values=1 << 30)
    key_ids = lax.dynamic_slice_in_dim(padded, start, span, 1)
    query_ids = lax.dynamic_slice_in_dim(block_ids, start + near * rows, rows, 1).reshape(rows, 1)

    planes = (shift(pair, 2), shift(pair, 1), pair, shift(pair, -1))
    queries, raw_queries = queries_of(place, normed_in, gain_query, table, qkv_pieces)
    chances, heads_out, attn_out, residual, normed_pre = attend(
        place, after(queries, first, gates_core), planes, key_ids, query_ids, tokens, gain_attn, gain_pre, out_pieces
    )

    far_normed = far_swap(after(normed_pre, first_rest), half_far)
    blocks = (normed_pre, *around([normed_pre] * 3))
    all_normed, hidden, slope, gelu, own, *sent = forward(place, after(blocks, far_normed), gates, downs)
    far_normed = after(far_normed, second_rest)
    far_normed = (far_normed, *around([far_normed] * 3))
    sent = after(sent, *far_normed)
    output, grad_down_proj, grad_gain_post = turning((own, *around(sent)), residual, cotangent, gain_post)
    far_down = far_swap(grad_down_proj, half_far)
    blocks = (grad_down_proj, *around([grad_down_proj] * 3))
    far_kept = far_hidden(place, hidden, after(far_normed, grad_down_proj), gates)
    blocks = after(blocks, far_down, *far_kept)
    all_down, gate_low, up_low, own, *sent = backward(place, blocks, slope, gelu, gates, downs)
    far_down = (far_down, *around([far_down] * 3))
    sent = after(sent, *far_down)
    parts = (own, *around(sent))
    keep_grads, send_grads = weight_grads(
        place, all_normed, all_down, after(gate_low, *sent), up_low, far_normed, far_down, far_kept, downs
    )
    got_grads = swap(after(send_grads, parts), "core")
    (
        grad_residual, own_right, other_right, grad_gains, grad_gain_query, grad_queries, *sent,
    ) = attend_back(
        far_count, early, place, after(parts, keep_grads), residual, attn_out, cotangent, gain_pre, gain_attn, chances, queries, raw_queries, table, gain_query,
        planes, out_pieces,
    )
    grad_gates, send_other, send_own, grad_down, send_down = add_cores(place, after(keep_grads, grad_queries), got_grads, model)
    total = after(sent[2], send_down) + shift(sent[0], -2).astype(f32)
    total = total + shift(sent[1], -1).astype(f32) + shift(sent[3], 1).astype(f32)
    partial = queries_back(place, after(grad_queries, send_down), qkv_pieces)
    got, got_heads = swap(other_right, "near"), swap(after(heads_out, grad_queries), "near")
    total, grad_gates, send_other, send_own, grad_down, send_down, partial, got, got_heads = lax.optimization_barrier(
        (total, grad_gates, send_other, send_own, grad_down, send_down, partial, got, got_heads)
    )

    received = swap(
        lax.dynamic_slice_in_dim(total, (1 - near) * rows, rows, 1).astype(bf16), "near"
    )
    got_down, got_other, got_own = (far_swap(g, low_bits[0]) for g in (send_down, send_other, send_own))
    keep_first, send_first = first_products(place, every, heads_out, got_heads, own_right, got)
    keep_first, send_first = first_cores(place, keep_first, swap(send_first, "core"))
    got_first = swap(send_first, "chip")
    grad_tokens, own_right, other_right, gains = keys_back(
        far_count, early, place, after(total, send_first), received, raw_keys, table, gain_key, partial, grad_residual, tokens, gain_in,
        grad_queries, grad_gains, grad_gain_post, grad_gain_query, qkv_pieces,
    )
    keep, send, gains = last_products(place, every, after(own_right, got_down), swap(other_right, "near"), gains)
    keep, send, gains = last_cores(place, after(keep, got_other), swap(send, "core"), gains)
    grad_down = add_down(grad_down, got_down)
    sums = last_chips(
        far_count, keep_first, got_first, keep, swap(send, "chip"), gains, query_width // 4, 4 * model + 2 * dim
    )
    columns = model // far_count // 2
    down_parts = halving(grad_down, 1, low_bits[1:]).astype(bf16).reshape(2, 2, columns, -1)
    down_parts = down_parts.transpose(1, 0, 2, 3).reshape(4, columns, -1)
    down_parts = lax.all_to_all(down_parts, ("near", "chip"), 0, 0, tiled=True)
    other_gates = add_gates(True, place, after(grad_gates, send), got_other)
    peer_gates = swap(halving(other_gates, 2, low_bits[1:]).astype(bf16), "chip")
    sums, got_own = lax.optimization_barrier((sums, got_own))

    sums = lax.all_to_all(sums, "far", 0, 0, tiled=True)
    qkv_total, out_total, gains = last_sum(sums, model // 4, w_qkv.shape[1] // 2, query_width // 4, 4 * model + 2 * dim)
    out_total, gains = out_total.T, gains.reshape(-1)
    own_gates = halving(add_gates(False, place, grad_gates, got_own), 2, low_bits[1:]).astype(bf16)
    mine = [lax.dynamic_index_in_dim(g, core, 0, keepdims=False) for g in (own_gates, peer_gates)]
    theirs = [lax.dynamic_index_in_dim(g, 1 - core, 0, keepdims=False) for g in (own_gates, peer_gates)]
    gate_total, up_total = gather_gates(place, *mine, *(swap(g, "core") for g in theirs))
    down_total = down_rows(down_parts, part).T

    gain_in, gain_pre, gain_attn, gain_post = (gains[i * model : (i + 1) * model] for i in range(4))
    gain_query, gain_key = gains[4 * model :][:dim], gains[4 * model + dim :][:dim]
    return (
        output.reshape(seq_count, rows, model),
        grad_tokens.reshape(seq_count, rows, model),
        qkv_total,
        out_total,
        gate_total,
        up_total,
        down_total,
        gain_in,
        gain_query,
        gain_key,
        gain_attn,
        gain_pre,
        gain_post,
    )


def solution(mesh):
    seq, dp = mesh.devices.shape
    parts = Mesh(mesh.devices.reshape(seq // 2, 2, 2, dp // 2), (*SEQ, *DP))
    rows = P(DP, None)
    whole = P(None)
    placed = (P(DP, SEQ, None), P(DP, None), *[rows] * 5, *[whole] * 6, P(DP, SEQ, None))
    return jax.shard_map(
        shards,
        mesh=parts,
        in_specs=placed,
        out_specs=(*[P(DP, SEQ, None)] * 2, *[P(DP, SEQ)] * 5, *[whole] * 6),
        check_vma=False,
    )
```

```python
import functools

import jax
import jax.numpy as jnp
from jax import lax
from jax.experimental import pallas as pl
from jax.experimental.pallas import tpu as pltpu
from jax.sharding import Mesh, PartitionSpec as P

HQ = 4
WINDOW = 512
BLOCK = 256


epsilon = 1e-06
bf16 = jnp.bfloat16
f32 = jnp.float32
ROOT = 0.7978845608028654

SEQ = ("far", "near")
DP = ("chip", "core")
SQUARE = ("near", "chip", "core")

ANYWHERE = pl.BlockSpec(memory_space=pl.ANY)
VECTORS = pl.BlockSpec(memory_space=pltpu.VMEM)
SCALARS = pl.BlockSpec(memory_space=pltpu.SMEM)


def low(*shape):
    return jax.ShapeDtypeStruct(shape, bf16)


def wide(*shape):
    return jax.ShapeDtypeStruct(shape, f32)


def call(kernel, microseconds, out_shape, in_specs, scratch, *args, megabytes=48):
    return pl.pallas_call(
        kernel,
        out_shape=out_shape,
        in_specs=in_specs,
        out_specs=jax.tree.map(lambda _: VECTORS, out_shape),
        scratch_shapes=scratch,
        cost_estimate=pl.CostEstimate(
            flops=microseconds * 1_000_000_000, bytes_accessed=1 << 20, transcendentals=0
        ),
        compiler_params=pltpu.CompilerParams(vmem_limit_bytes=megabytes << 20),
    )(*args)


def steps(total, size):
    return [(first, min(first + size, total)) for first in range(0, total, size)]


NEAR, CHIP, CORE, PARITY, HALF, BIT = range(6)


def slots(place):
    chip, core = place[CHIP], place[CORE]
    return chip * 2 + core, (1 - chip) * 2 + core, chip * 2 + 1 - core, (1 - chip) * 2 + 1 - core


def at(start, size, multiple=16):
    return pl.ds(pl.multiple_of(start, multiple), size)


def begin(pairs, sem):
    copies = [pltpu.make_async_copy(a, b, sem.at[i]) for i, (a, b) in enumerate(pairs)]
    for c in copies:
        c.start()
    return copies


def fetch(place, pieces, target, sem):
    rows = target.shape[0] // 4
    return begin([(p, target.at[at(s * rows, rows)]) for s, p in zip(slots(place), pieces)], sem)


def fetch_gates(place, pieces, target, sem):
    own, core, chip, other = pieces[0], pieces[1], pieces[2:6], pieces[6:10]
    rows = target.shape[1] // 4
    half = rows // 2
    a, b, c, d = (s * rows for s in slots(place))
    pairs = [(own, target.at[:, at(a, rows)]), (core, target.at[:, at(c, rows)])]
    for start, four in ((b, chip), (d, other)):
        for k in range(2):
            pairs.append((four[k], target.at[place[PARITY], at(start + k * half, half)]))
            pairs.append((four[2 + k], target.at[1 - place[PARITY], at(start + k * half, half)]))
    return begin(pairs, sem)


def wait(copies):
    for c in copies:
        c.wait()


def nn(a, b):
    return jnp.dot(a, b, preferred_element_type=f32)


def nt(a, b):
    return lax.dot_general(a, b, (((1,), (1,)), ((), ())), preferred_element_type=f32)


def tn(a, b):
    return lax.dot_general(a, b, (((0,), (0,)), ((), ())), preferred_element_type=f32)


def rms(value, gain):
    return value * lax.rsqrt(jnp.mean(value * value, axis=-1, keepdims=True) + epsilon) * gain


def rms_back(value, gain, grad):
    scale = lax.rsqrt(jnp.mean(value * value, axis=-1, keepdims=True) + epsilon)
    unit = value * scale
    slope = grad * gain
    back = scale * (slope - unit * jnp.mean(slope * unit, axis=-1, keepdims=True))
    return back, jnp.sum(grad * unit, axis=0, keepdims=True)


def turn(value, cosine, sine):
    half = value.shape[-1] // 2
    a, b = value[:, :half], value[:, half:]
    return jnp.concatenate([a * cosine - b * sine, b * cosine + a * sine], axis=-1)


def half_plane(which, rows):
    return pl.ds(pl.multiple_of(which * rows, 128), rows)


def slice_kernel(far, part, place, gate, up, own, other0, other1, source, sem):
    rows, ff = gate.shape
    copies = begin([(w, source.at[i, :, :ff]) for i, w in enumerate((gate, up))], sem)
    near, chip = place[NEAR], place[CHIP]
    block = 48
    half = rows // 2

    def cut(i, which, target, from_row, to_row):
        for z in range(far):
            first, last = z * part, (z + 1) * part
            lo, hi = first // 128 * 128, min(-(-last // 128) * 128, far * part)
            span = -(-(hi - lo) // 128) * 128 + 128
            shift = (z * 3 + near * 2 + which) * part
            coarse = shift // 128 * 128
            x = source[i, from_row, at(lo + coarse, span, 128)]
            x = pltpu.roll(x, (span - (shift - coarse)) % span, 1)[:, : hi - lo]
            if first > lo:
                column = lax.broadcasted_iota(jnp.int32, x.shape, 1)
                x = jnp.where(column < first - lo, target[to_row, lo:hi], x)
            target[to_row, lo:hi] = x

    wait(copies)
    for k, other in enumerate((other0, other1)):

        def send(r, _):
            cut(place[PARITY], 1 - chip, other, at(k * half + r * block, block), at(r * block, block))
            return 0

        lax.fori_loop(0, half // block, send, 0)
    for i in range(2):

        def keep(r, _):
            here = at(r * block, block)
            cut(i, chip, own.at[i], here, here)
            return 0

        lax.fori_loop(0, rows // block, keep, 0)


def chip_columns(place, gate, up, far):
    rows, ff = gate.shape
    part = ff // (4 * far)
    source = -(-ff // 128) * 128 + 768
    return call(
        functools.partial(slice_kernel, far, part),
        6,
        (low(2, rows, ff // 4), low(rows // 2, ff // 4), low(rows // 2, ff // 4)),
        [SCALARS, ANYWHERE, ANYWHERE],
        [pltpu.VMEM((2, rows, source), bf16), pltpu.SemaphoreType.DMA((2,))],
        place,
        gate,
        up,
    )


def key_columns(pieces, count):
    return [p.at[:, p.shape[1] - count :] for p in pieces]


def query_columns(pieces, count):
    return [p.at[:, :count] for p in pieces]


def keys_kernel(place, own, peer, gain_in, gain_key, table, k0, k1, k2, k3, normed, pair, raw, every, weight, sem):
    copies = fetch(place, key_columns((k0, k1, k2, k3), weight.shape[1]), weight, sem)
    rows, near, width = own.shape[0], place[0], raw.shape[1]
    mine = rms(own[...].astype(f32), gain_in[...]).astype(bf16)
    normed[...] = mine
    every[half_plane(near, rows)] = mine
    every[half_plane(1 - near, rows)] = rms(peer[...].astype(f32), gain_in[...]).astype(bf16)
    wait(copies)
    projected = nn(every[...], weight[...])
    raw[...] = projected[:, :width]
    pair[0] = turn(rms(projected[:, :width], gain_key[...]), table[0], table[1]).astype(bf16)
    pair[1] = projected[:, width:].astype(bf16)


def keys_of(place, own, peer, gain_in, gain_key, table, pieces):
    rows, model = own.shape
    dim = gain_key.shape[1]
    return call(
        keys_kernel,
        2,
        (low(rows, model), low(2, 2 * rows, dim), wide(2 * rows, dim), low(2 * rows, model)),
        [SCALARS, *[VECTORS] * 5, *[ANYWHERE] * 4],
        [pltpu.VMEM((model, 2 * dim), bf16), pltpu.SemaphoreType.DMA((4,))],
        place, own, peer, gain_in, gain_key, table, *pieces,
    )


def queries_kernel(place, normed, gain, table, q0, q1, q2, q3, queries, raw, weight, sem):
    wait(fetch(place, query_columns((q0, q1, q2, q3), weight.shape[1]), weight, sem))
    rows, dim = normed.shape[0], gain.shape[1]
    here = half_plane(place[0], rows)
    cosine, sine = table[0, here], table[1, here]
    for h in range(HQ):
        projected = nn(normed[...], weight[:, h * dim : (h + 1) * dim])
        raw[h * rows : (h + 1) * rows] = projected
        turned = turn(rms(projected, gain[...]), cosine, sine).astype(bf16)
        queries[h * rows : (h + 1) * rows] = turned * jnp.asarray(dim**-0.5, bf16)


def queries_of(place, normed, gain, table, pieces):
    rows, model = normed.shape
    dim = gain.shape[1]
    return call(
        queries_kernel,
        6,
        (low(HQ * rows, dim), wide(HQ * rows, dim)),
        [SCALARS, *[VECTORS] * 3, *[ANYWHERE] * 4],
        [pltpu.VMEM((model, HQ * dim), bf16), pltpu.SemaphoreType.DMA((4,))],
        place, normed, gain, table, *pieces,
    )


def attend_kernel(
    place, queries, kv0, kv1, kv2, kv3, key_ids, query_ids, tokens, gain_attn, gain_pre, o0, o1, o2, o3,
    chances, heads, attn_out, residual, normed_pre, keys, values, weight, sem,
):
    copies = fetch(place, (o0, o1, o2, o3), weight, sem)
    plane, dim = kv0.shape[1], kv0.shape[2]
    for i, kv in enumerate((kv0, kv1, kv2, kv3)):
        keys[i * plane : (i + 1) * plane] = kv[0]
        values[i * plane : (i + 1) * plane] = kv[1]
    rows, span = query_ids.shape[0], key_ids.shape[1]
    row = lax.broadcasted_iota(jnp.int32, (rows, span), 0) + place[0] * rows
    column = lax.broadcasted_iota(jnp.int32, (rows, span), 1)
    same = key_ids[...] == query_ids[...]
    allowed = same | ((key_ids[...] < query_ids[...]) & (column >= row))
    chances[...] = nt(queries[...], keys[...])
    for h in range(HQ):
        here = slice(h * rows, (h + 1) * rows)
        scores = jnp.where(allowed, chances[here], -1e30)
        grown = jnp.exp(scores - jnp.max(scores, axis=-1, keepdims=True))
        chances[here] = grown / jnp.sum(grown, axis=-1, keepdims=True)
    seen = nn(chances[...].astype(bf16), values[...]).astype(bf16)
    for h in range(HQ):
        heads[:, h * dim : (h + 1) * dim] = seen[h * rows : (h + 1) * rows]
    wait(copies)
    out = nn(heads[...], weight[...])
    attn_out[...] = out
    total = tokens[...].astype(f32) + rms(out, gain_attn[...])
    residual[...] = total
    normed_pre[...] = rms(total, gain_pre[...]).astype(bf16)


def attend(place, queries, planes, key_ids, query_ids, tokens, gain_attn, gain_pre, pieces):
    rows, model = tokens.shape
    dim, span = queries.shape[1], key_ids.shape[1]
    return call(
        attend_kernel,
        2,
        (wide(HQ * rows, span), low(rows, HQ * dim), wide(rows, model), wide(rows, model), low(rows, model)),
        [SCALARS, *[VECTORS] * 10, *[ANYWHERE] * 4],
        [
            pltpu.VMEM((span, dim), bf16),
            pltpu.VMEM((span, dim), bf16),
            pltpu.VMEM((HQ * dim, model), bf16),
            pltpu.SemaphoreType.DMA((4,)),
        ],
        place, queries, *planes, key_ids, query_ids, tokens, gain_attn, gain_pre, *pieces,
    )


def gated(gate, up):
    square = gate * gate
    wave = jnp.tanh(ROOT * gate * (1.0 + 0.044715 * square))
    half = 0.5 * (1.0 + wave)
    value = gate * half
    bend = half + 0.5 * ROOT * gate * (1.0 - wave * wave) * (1.0 + 3.0 * 0.044715 * square)
    return (value * up).astype(bf16), (bend * up).astype(bf16), value.astype(bf16)


def forward_kernel(place, x0, x1, x2, x3, *refs):
    gates, downs = refs[:10], refs[10:14]
    whole, hidden, slope, gelu, total, p1, p2, p3 = refs[14:22]
    w_gates, w_down, sem, late_sem = refs[22:]
    copies = fetch_gates(place, gates, w_gates, sem)
    late = fetch(place, downs, w_down, late_sem)
    rows = x0.shape[0]
    for i, x in enumerate((x0, x1, x2, x3)):
        whole[i * rows : (i + 1) * rows] = x[...]
    wait(copies)
    for first, last in steps(w_down.shape[0], 256):
        gate = nn(whole[...], w_gates[0, :, first:last])
        up = nn(whole[...], w_gates[1, :, first:last])
        hidden[:, first:last], slope[:, first:last], gelu[:, first:last] = gated(gate, up)
    wait(late)
    for first, last in steps(w_down.shape[1], 384):
        part = nn(hidden[...], w_down[:, first:last])
        total[:, first:last] = part[:rows]
        for i, p in enumerate((p1, p2, p3)):
            p[:, first:last] = part[(i + 1) * rows : (i + 2) * rows].astype(bf16)


def weight_room(model, ff):
    return [
        pltpu.VMEM((2, model, ff), bf16),
        pltpu.VMEM((ff, model), bf16),
        pltpu.SemaphoreType.DMA((10,)),
        pltpu.SemaphoreType.DMA((6,)),
    ]


def forward(place, blocks, gates, downs):
    rows, model = blocks[0].shape
    ff = gates[0].shape[2]
    return call(
        forward_kernel,
        13,
        (low(4 * rows, model), *[low(4 * rows, ff)] * 3, wide(rows, model), *[low(rows, model)] * 3),
        [SCALARS, *[VECTORS] * 4, *[ANYWHERE] * 14],
        weight_room(model, ff),
        place, *blocks, *gates, *downs,
    )


def backward_kernel(place, x0, x1, x2, x3, slope, gelu, *refs):
    gates, downs = refs[:10], refs[10:14]
    whole, gate_low, up_low, total, p1, p2, p3 = refs[14:21]
    w_gates, w_down, late_sem, sem = refs[21:]
    copies = fetch(place, downs, w_down, sem)
    late = fetch_gates(place, gates, w_gates, late_sem)
    rows = x0.shape[0]
    for i, x in enumerate((x0, x1, x2, x3)):
        whole[i * rows : (i + 1) * rows] = x[...]
    wait(copies)
    for first, last in steps(w_down.shape[0], 256):
        back = nt(whole[...], w_down[first:last])
        gate_low[:, first:last] = (back * slope[:, first:last].astype(f32)).astype(bf16)
        up_low[:, first:last] = (back * gelu[:, first:last].astype(f32)).astype(bf16)
    wait(late)
    for first, last in steps(w_down.shape[1], 384):
        part = nt(gate_low[...], w_gates[0, first:last]) + nt(up_low[...], w_gates[1, first:last])
        total[:, first:last] = part[:rows]
        for i, p in enumerate((p1, p2, p3)):
            p[:, first:last] = part[(i + 1) * rows : (i + 2) * rows].astype(bf16)


def backward(place, blocks, slope, gelu, gates, downs):
    rows, model = blocks[0].shape
    ff = gates[0].shape[2]
    return call(
        backward_kernel,
        15,
        (low(4 * rows, model), *[low(4 * rows, ff)] * 2, wide(rows, model), *[low(rows, model)] * 3),
        [SCALARS, *[VECTORS] * 6, *[ANYWHERE] * 14],
        weight_room(model, ff),
        place, *blocks, slope, gelu, *gates, *downs,
    )


def far_kernel(window, place, own, n0, n1, n2, n3, *refs):
    gates, (hiddens, slope, gelu, w_gates, tokens, room, sem) = refs[:10], refs[10:]
    start, width = window
    copies = fetch_gates(place, gates, w_gates, sem)
    rows = n0.shape[0]
    for i, n in enumerate((n0, n1, n2, n3)):
        tokens[i * rows : (i + 1) * rows] = n[...]
    hiddens[:, : 4 * rows] = own[...].T
    wait(copies)
    for first, last in steps(hiddens.shape[0], 256):
        gate = nn(tokens[...], w_gates[0, :, first:last])
        up = nn(tokens[...], w_gates[1, :, first:last])
        value, room[0, :, first:last], room[1, :, first:last] = gated(gate, up)
        hiddens[first:last, 4 * rows :] = value.T
    here = at(place[HALF] * start, width, 128)
    slope[...] = room[0, :, here]
    gelu[...] = room[1, :, here]


def window_of(ff):
    start = ff // 2 // 128 * 128
    return start, ff - start


def far_hidden(place, hidden, far_normed, gates):
    rows, model = far_normed[0].shape
    ff = gates[0].shape[2]
    start, width = window_of(ff)
    return call(
        functools.partial(far_kernel, (start, width)),
        11,
        (low(ff, 8 * rows), low(4 * rows, width), low(4 * rows, width)),
        [SCALARS, *[VECTORS] * 5, *[ANYWHERE] * 10],
        [
            pltpu.VMEM((2, model, ff), bf16),
            pltpu.VMEM((4 * rows, model), bf16),
            pltpu.VMEM((2, 4 * rows, ff), bf16),
            pltpu.SemaphoreType.DMA((10,)),
        ],
        place, hidden, *far_normed, *gates,
    )


def weights_kernel(
    window, place, h_normed, h_down, h_gate, h_up, n0, n1, n2, n3, d0, d1, d2, d3, h_hiddens, h_slope, h_gelu, w0, w1, w2, w3,
    h_keep, h_send, w_down, grads, tokens, backs, gate_low, up_low, hiddens, slope, gelu, keep, send,
    sem, soon_sem, late_sem, out_sem,
):
    start, width = window
    half, core, bit = place[HALF], place[CORE], place[BIT]
    own, model = h_normed.shape
    rows = own // 4
    columns = at(half * start, width, 128)

    def blocks(parts, target):
        return [(p, target.at[own + i * rows : own + (i + 1) * rows]) for i, p in enumerate(parts)]

    first = begin([(h_gate, gate_low), (h_up, up_low)], sem)
    soon = [*blocks((d0, d1, d2, d3), backs), (h_slope, slope), (h_gelu, gelu), (h_down, backs.at[:own])]
    for slot, piece in zip(slots(place), (w0, w1, w2, w3)):
        soon.append((piece, w_down.at[at(slot * piece.shape[0], piece.shape[0])]))
    soon = begin(soon, soon_sem)
    late = begin([*blocks((n0, n1, n2, n3), tokens), (h_normed, tokens.at[:own]), (h_hiddens, hiddens)], late_sem)
    wait(first)
    grads[core, :, :own] = gate_low[:, columns].T
    grads[1 - core, :, :own] = up_low[:, columns].T
    wait(soon)
    for first, last in steps(width, 256):
        back = nt(backs[own:], w_down[at(half * start + first, last - first)])
        c = slice(first, last)
        grads[core, c, own:] = (back * slope[:, c].astype(f32)).astype(bf16).T
        grads[1 - core, c, own:] = (back * gelu[:, c].astype(f32)).astype(bf16).T
    wait(late)
    kept = hiddens.shape[0] // 2
    part = kept // 2
    results = []
    for i in range(2):
        r = at(half * (kept - start) + i * part, part)
        slot = i ^ bit
        keep[slot, :, :model] = nn(grads[0, r], tokens[...]).astype(bf16)
        send[slot, :, :model] = nn(grads[1, r], tokens[...]).astype(bf16)
    gates = pl.ds(0, model)
    results += [(keep.at[:, :, gates], h_keep.at[:, :, gates]), (send.at[:, :, gates], h_send.at[:, :, gates])]
    done = begin(results, out_sem)
    span = keep.shape[2] - model
    columns = at(half * (model - span), span, 128)
    for i in range(4):
        result = nn(hiddens[i * part : (i + 1) * part], backs[:, columns]).astype(bf16)

        @pl.when(core == i % 2)
        def _():
            keep[i // 2, :, model:] = result

        @pl.when(core != i % 2)
        def _():
            send[i // 2, :, model:] = result

    rest = pl.ds(model, span)
    for i, (a, b) in enumerate(((keep, h_keep), (send, h_send))):
        copy = pltpu.make_async_copy(a.at[:, :, rest], b.at[:, :, rest], out_sem.at[2 + i])
        copy.start()
        done.append(copy)
    wait(done)


def weight_grads(place, normed, down, gate_low, up_low, far_normed, far_down, far_kept, downs):
    own, model = normed.shape
    ff = gate_low.shape[1]
    start, width = window_of(ff)
    part = ff // 4
    span = -(-model // 256) * 128
    shape = (2, part, model + span)
    return pl.pallas_call(
        functools.partial(weights_kernel, (start, width)),
        out_shape=(low(*shape), low(*shape)),
        in_specs=[SCALARS, *[ANYWHERE] * 19],
        out_specs=(ANYWHERE, ANYWHERE),
        scratch_shapes=[
            pltpu.VMEM((ff, model), bf16),
            pltpu.VMEM((2, width, 2 * own), bf16),
            pltpu.VMEM((2 * own, model), bf16),
            pltpu.VMEM((2 * own, model), bf16),
            pltpu.VMEM((own, ff), bf16),
            pltpu.VMEM((own, ff), bf16),
            pltpu.VMEM((ff, 2 * own), bf16),
            pltpu.VMEM((own, width), bf16),
            pltpu.VMEM((own, width), bf16),
            pltpu.VMEM(shape, bf16),
            pltpu.VMEM(shape, bf16),
            pltpu.SemaphoreType.DMA((2,)),
            pltpu.SemaphoreType.DMA((11,)),
            pltpu.SemaphoreType.DMA((6,)),
            pltpu.SemaphoreType.DMA((4,)),
        ],
        cost_estimate=pl.CostEstimate(flops=16_000_000_000, bytes_accessed=1 << 20, transcendentals=0),
        compiler_params=pltpu.CompilerParams(vmem_limit_bytes=48 << 20),
    )(place, normed, down, gate_low, up_low, *far_normed, *far_down, *far_kept, *downs)


def turning_kernel(own, r1, r2, r3, residual, cotangent, gain, output, grad, grad_gain):
    down = own[...] + r1[...].astype(f32) + r2[...].astype(f32) + r3[...].astype(f32)
    output[...] = (residual[...] + rms(down, gain[...])).astype(bf16)
    back, grad_gain[...] = rms_back(down, gain[...], cotangent[...].astype(f32))
    grad[...] = back.astype(bf16)


def turning(parts, residual, cotangent, gain):
    rows, model = residual.shape
    return call(
        turning_kernel,
        1,
        (low(rows, model), low(rows, model), wide(1, model)),
        [VECTORS] * 7,
        [],
        *parts, residual, cotangent, gain,
    )


def cores_kernel(place, keep, got, gates, send_other, send_own, down, send_down, turned):
    model = gates.shape[1]
    gates[...] = keep[0, :, :model].astype(f32) + got[0, :, :model].astype(f32)
    sent = keep[1, :, :model].astype(f32) + got[1, :, :model].astype(f32)
    half, short = model // 2, send_own.shape[0]
    for i in range(2):

        @pl.when(place[CHIP] == i)
        def _():
            for target, j in ((send_own, i), (send_other, 1 - i)):
                for k in range(2):
                    block = sent[k * short : (k + 1) * short, j * half : (j + 1) * half]
                    target[:, k * half : (k + 1) * half] = block.astype(bf16)

    unit, part = down.shape[0], turned.shape[2]
    first = place[HALF] * (turned.shape[1] - 2 * unit)
    for i in range(2):
        turned[i] = (keep[i, :, model:].astype(f32) + got[i, :, model:].astype(f32)).T
        for target, bit in ((down, place[BIT]), (send_down, 1 - place[BIT])):
            target[:, i * part : (i + 1) * part] = turned[i, at(first + bit * unit, unit)].astype(target.dtype)


def add_cores(place, keep, got, model):
    part = keep.shape[1]
    return call(
        cores_kernel,
        4,
        (
            wide(part, model), low(part // 2, model), low(part // 2, model),
            wide(model // 4, 2 * part), low(model // 4, 2 * part),
        ),
        [SCALARS, *[VECTORS] * 2],
        [pltpu.VMEM((2, keep.shape[2] - model, part), f32)],
        place, keep, got,
    )


def gates_kernel(flip, place, gates, got, total):
    half, unit = got.shape[1] // 2, total.shape[1]
    both = jnp.concatenate([got[:, :half].astype(f32), got[:, half:].astype(f32)], axis=0)
    for i in range(2):

        @pl.when(place[CHIP] == (1 - i if flip else i))
        def _():
            turned = (gates[:, i * half : (i + 1) * half] + both).T.astype(bf16)
            for k in range(2):
                total[k] = turned[k * unit : (k + 1) * unit]


def add_gates(flip, place, gates, got):
    part, model = gates.shape
    return call(
        functools.partial(gates_kernel, flip), 2, low(2, model // 4, part), [SCALARS, *[VECTORS] * 2], [], place, gates, got
    )


def gather_gates_kernel(place, own, peer, got_own, got_peer, gate, up):
    part = own.shape[1]
    for core in range(2):
        for chip in range(2):

            @pl.when((place[CORE] == core) & (place[CHIP] == chip))
            def _():
                here, there = (gate, up) if core == 0 else (up, gate)
                for target, first, second in ((here, own, peer), (there, got_own, got_peer)):
                    target[:, chip * part : (chip + 1) * part] = first[...].astype(f32)
                    target[:, (1 - chip) * part : (2 - chip) * part] = second[...].astype(f32)


def gather_gates(place, own, peer, got_own, got_peer):
    rows, part = own.shape
    return call(
        gather_gates_kernel,
        2,
        (wide(rows, 2 * part), wide(rows, 2 * part)),
        [SCALARS, *[VECTORS] * 4],
        [],
        place, own, peer, got_own, got_peer,
    )


def down_kernel(down, got, total):
    part = total.shape[2]
    for i in range(2):
        c = slice(i * part, (i + 1) * part)
        total[i] = (down[:, c] + got[:, c].astype(f32)).astype(bf16)


def add_down(down, got):
    rows, width = down.shape
    return call(down_kernel, 1, low(2, rows, width // 2), [VECTORS] * 2, [], down, got)


def attend_back_kernel(
    far, early, place, h_own, h_r1, h_r2, h_r3, h_residual, h_attn_out, h_cotangent, h_chances, h_queries, h_raw, h_table,
    gain_pre, gain_attn, gain_query,
    kv0, kv1, kv2, kv3, o0, o1, o2, o3,
    grad_residual, keep, send, grad_gains, grad_gain_query, grad_projected, g0, g1, g2, g3,
    own, r1, r2, r3, residual, attn_out, cotangent, chances, queries, raw, table,
    keys, values, attn_low, heads, dull, grad_share, weight, sem, soon_sem, late_sem,
):
    plane, dim = kv0.shape[1], kv0.shape[2]
    soon = begin(
        [
            (h_own, own), (h_r1, r1), (h_r2, r2), (h_r3, r3),
            (h_residual, residual), (h_attn_out, attn_out), (h_cotangent, cotangent),
        ],
        soon_sem,
    )
    copies = fetch(place, (o0, o1, o2, o3), weight, sem)
    late = [(h_chances, chances), (h_queries, queries), (h_raw, raw), (h_table, table)]
    for i, kv in enumerate((kv0, kv1, kv2, kv3)):
        late += [(kv.at[0], keys.at[i * plane : (i + 1) * plane]), (kv.at[1], values.at[i * plane : (i + 1) * plane])]
    copies += begin(late, late_sem)
    wait(soon)
    normed = own[...] + r1[...].astype(f32) + r2[...].astype(f32) + r3[...].astype(f32)
    back, grad_gains[0:1] = rms_back(residual[...], gain_pre[...], normed)
    total = cotangent[...].astype(f32) + back
    grad_residual[...] = total
    back, grad_gains[1:2] = rms_back(attn_out[...], gain_attn[...], total)
    attn_low[...] = back.astype(bf16)
    wait(copies)
    rows = own.shape[0]
    here = half_plane(place[0], rows)
    cosine, sine = table[0, here], table[1, here]
    grad_heads = nt(attn_low[...], weight[...]).astype(bf16)
    for h in range(HQ):
        heads[h * rows : (h + 1) * rows] = grad_heads[:, h * dim : (h + 1) * dim]
    grad_share[...] = nt(heads[...], values[...])
    for h in range(HQ):
        r = slice(h * rows, (h + 1) * rows)
        share, back = chances[r], grad_share[r]
        dull[r] = (share * (back - jnp.sum(share * back, axis=-1, keepdims=True))).astype(bf16)
    turned = nn(dull[...], keys[...]) * (dim**-0.5)
    gain_total = jnp.zeros_like(grad_gain_query)
    for h in range(HQ):
        r = slice(h * rows, (h + 1) * rows)
        back, gain_part = rms_back(raw[r], gain_query[...], turn(turned[r], cosine, -sine))
        gain_total = gain_total + gain_part
        grad_projected[:, h * dim : (h + 1) * dim] = back.astype(bf16)
    grad_gain_query[...] = gain_total
    for i, g in enumerate((g0, g1, g2, g3)):
        c = slice(i * plane, (i + 1) * plane)
        g[0] = tn(dull[:, c], queries[...]).astype(g.dtype)
        g[1] = tn(chances[:, c].astype(bf16), heads[...]).astype(g.dtype)
    block, size = grad_projected.shape[1] * 3 // 2 // (2 * far), attn_low.shape[1] // (2 * far)
    parts = [
        columns_of(grad_projected[...], i, range(early), block) + columns_of(attn_low[...], i, range(far), size) for i in range(2)
    ]
    for i in range(2):

        @pl.when(place[NEAR] == i)
        def _():
            keep[...] = jnp.concatenate(parts[i], axis=1)
            send[...] = jnp.concatenate(parts[1 - i], axis=1)


def attend_back(far, early, place, parts, residual, attn_out, cotangent, gain_pre, gain_attn, chances, queries, raw, table, gain_query, planes, pieces):
    rows, model = residual.shape
    dim, span = queries.shape[1], chances.shape[1]
    plane = planes[0].shape[1]
    sent = low(2, plane, dim)
    width = early * HQ * dim * 3 // 2 // (2 * far) + model // 2
    return call(
        functools.partial(attend_back_kernel, far, early),
        8,
        (
            wide(rows, model), low(rows, width), low(rows, width), wide(2, model), wide(1, dim), low(rows, HQ * dim),
            sent, sent, wide(2, plane, dim), sent,
        ),
        [SCALARS, *[ANYWHERE] * 11, *[VECTORS] * 3, *[ANYWHERE] * 8],
        [
            pltpu.VMEM((rows, model), f32),
            *[pltpu.VMEM((rows, model), bf16)] * 3,
            *[pltpu.VMEM((rows, model), f32)] * 2,
            pltpu.VMEM((rows, model), bf16),
            pltpu.VMEM((HQ * rows, span), f32),
            pltpu.VMEM((HQ * rows, dim), bf16),
            pltpu.VMEM((HQ * rows, dim), f32),
            pltpu.VMEM((2, 2 * rows, dim // 2), f32),
            pltpu.VMEM((span, dim), bf16),
            pltpu.VMEM((span, dim), bf16),
            pltpu.VMEM((rows, model), bf16),
            pltpu.VMEM((HQ * rows, dim), bf16),
            pltpu.VMEM((HQ * rows, span), bf16),
            pltpu.VMEM((HQ * rows, span), f32),
            pltpu.VMEM((HQ * dim, model), bf16),
            pltpu.SemaphoreType.DMA((4,)),
            pltpu.SemaphoreType.DMA((7,)),
            pltpu.SemaphoreType.DMA((12,)),
        ],
        place, *parts, residual, attn_out, cotangent, chances, queries, raw, table, gain_pre, gain_attn, gain_query, *planes, *pieces,
        megabytes=56,
    )


def queries_back_kernel(place, grad, q0, q1, q2, q3, result, weight, sem):
    wait(fetch(place, query_columns((q0, q1, q2, q3), weight.shape[1]), weight, sem))
    result[...] = nt(grad[...], weight[...])


def queries_back(place, grad, pieces):
    rows, width = grad.shape
    model = pieces[0].shape[0] * 4
    return call(
        queries_back_kernel,
        4,
        wide(rows, model),
        [SCALARS, VECTORS, *[ANYWHERE] * 4],
        [pltpu.VMEM((model, width), bf16), pltpu.SemaphoreType.DMA((4,))],
        place, grad, *pieces,
    )


def columns_of(value, near, blocks, size):
    return [value[:, (2 * f + near) * size : (2 * f + near + 1) * size] for f in blocks]


def by_place(index, choices):
    for i, choice in enumerate(choices):
        pl.when(index == i)(choice)


def first_products_kernel(place, every, own_heads, got_heads, own, got, keep, send, right, heads):
    rows, near, core = own.shape[0], place[NEAR], place[CORE]
    for target, mine, theirs in ((right, own, got), (heads, own_heads, got_heads)):
        target[half_plane(near, rows)] = mine[...]
        target[half_plane(1 - near, rows)] = theirs[...]
    unit, head = keep.shape[1], heads.shape[1] // 4
    width = keep.shape[2] - 2 * head
    part = tn(every[...], right[:, :width])
    out = tn(right[:, width:], heads[...])
    for i in range(4):
        here = part[i * unit : (i + 1) * unit]
        there = [out[k * unit : (k + 1) * unit, i * head : (i + 1) * head] for k in range(2)]
        for target, chosen in ((keep, core == i % 2), (send, core != i % 2)):

            @pl.when(chosen)
            def _():
                target[i // 2, :, :width] = here.astype(target.dtype)
                for k in range(2):
                    first = width + k * head
                    target[i // 2, :, first : first + head] = there[k].astype(target.dtype)


def first_products(place, every, own_heads, got_heads, own, got):
    rows, model = own_heads.shape[0], every.shape[1]
    width = own.shape[1] - model // 2 + own_heads.shape[1] // 2
    return call(
        first_products_kernel,
        4,
        (wide(2, model // 4, width), low(2, model // 4, width)),
        [SCALARS, *[VECTORS] * 5],
        [pltpu.VMEM((2 * rows, own.shape[1]), bf16), pltpu.VMEM((2 * rows, own_heads.shape[1]), bf16)],
        place, every, own_heads, got_heads, own, got,
    )


def first_cores_kernel(place, keep, got, new, send):
    chip = place[CHIP]
    new[...] = keep[chip] + got[chip].astype(f32)
    send[...] = (keep[1 - chip] + got[1 - chip].astype(f32)).astype(bf16)


def first_cores(place, keep, got):
    shape = keep.shape[1:]
    return call(first_cores_kernel, 2, (wide(*shape), low(*shape)), [SCALARS, *[VECTORS] * 2], [], place, keep, got)


def last_products_kernel(place, every, own, got, gains, keep, send, total_gains, right):
    rows, near, core = own.shape[0], place[NEAR], place[CORE]
    right[half_plane(near, rows)] = own[...]
    right[half_plane(1 - near, rows)] = got[:rows]
    sums = gains[...] + got[rows:].astype(f32)
    total_gains[...] = sums
    unit = keep.shape[1]
    part = tn(every[...], right[...])
    for i in range(4):
        x, c = i // 2, i % 2
        here = part[i * unit : (i + 1) * unit]

        @pl.when(core == c)
        def _():
            keep[x] = here

        @pl.when(core != c)
        def _():
            send[x * unit : (x + 1) * unit] = here.astype(bf16)

    send[2 * unit :] = sums.astype(bf16)


def last_products(place, every, own, got, gains):
    rows, width = own.shape
    unit, more = every.shape[1] // 4, gains.shape[0]
    return call(
        last_products_kernel,
        2,
        (wide(2, unit, width), low(2 * unit + more, width), wide(more, width)),
        [SCALARS, *[VECTORS] * 4],
        [pltpu.VMEM((2 * rows, width), bf16)],
        place, every, own, got, gains,
    )


def last_cores_kernel(place, keep, got, gains, new, send, total_gains):
    unit, chip = new.shape[0], place[CHIP]
    new[...] = keep[chip] + got[at(chip * unit, unit)].astype(f32)
    send[:unit] = (keep[1 - chip] + got[at((1 - chip) * unit, unit)].astype(f32)).astype(bf16)
    sums = gains[...] + got[2 * unit :].astype(f32)
    total_gains[...] = sums
    send[unit:] = sums.astype(bf16)


def last_cores(place, keep, got, gains):
    _, unit, width = keep.shape
    more = gains.shape[0]
    return call(
        last_cores_kernel,
        1,
        (wide(unit, width), low(unit + more, width), wide(more, width)),
        [SCALARS, *[VECTORS] * 3],
        [],
        place, keep, got, gains,
    )


def layout(far, unit, columns, head, gains):
    size, short = columns // far, 2 * unit // far
    lanes = -(-size // 128) * 128
    free = lanes - size
    beside = unit // (head // free) if free and head % free == 0 else 0
    beside = beside if beside <= short and beside * (head // max(free, 1)) == unit else 0
    rest = (short - beside) * head // lanes
    return size, short, lanes, beside, rest, -(-(unit + rest + -(-gains // lanes)) // 16) * 16


def chips_kernel(count, first, got_first, keep, got, gains, out, room, line, block):
    unit, early = first.shape[0], room.shape[1] - keep.shape[1]
    far, head = out.shape[0], (first.shape[1] - early) // 2
    size, short, lanes, beside, rest, _ = layout(far, unit, room.shape[1], head, count)
    room[:, :early] = first[:, :early] + got_first[:, :early].astype(f32)
    room[:, early:] = keep[...] + got[:unit].astype(f32)
    sums = gains[...] + got[unit:].astype(f32)
    width, more = gains.shape[1], -(-count // lanes)
    line[...] = jnp.zeros_like(line)
    for i in range(0, more * lanes, width):
        here = min(width, more * lanes - i)
        line[:, i : i + here] = sums[i // width : i // width + 1, :here]
    block[...] = jnp.zeros_like(block)
    for i in range(more):
        block[unit + rest + i : unit + rest + i + 1] = line[:, i * lanes : (i + 1) * lanes]
    for half in range(2):
        start = early + half * head
        part = first[:, start : start + head] + got_first[:, start : start + head].astype(f32)
        for k in range(far // 2):
            f = half * (far // 2) + k
            mine = part[k * short : (k + 1) * short]
            block[:unit, :size] = room[:, f * size : (f + 1) * size]
            for g in range(unit // beside if beside else 0):
                block[g * beside : (g + 1) * beside, size:] = mine[:beside, g * (lanes - size) : (g + 1) * (lanes - size)]
            for j in range(head // lanes):
                start_row = unit + j * (short - beside)
                block[start_row : start_row + short - beside] = mine[beside:, j * lanes : (j + 1) * lanes]
            out[f] = block[...].astype(bf16)


def last_chips(far, first, got_first, keep, got, gains, head, count):
    unit, width = keep.shape
    columns = first.shape[1] - 2 * head + width
    _, _, lanes, _, _, rows = layout(far, unit, columns, head, count)
    return call(
        functools.partial(chips_kernel, count),
        3,
        low(far, rows, lanes),
        [VECTORS] * 5,
        [pltpu.VMEM((unit, columns), f32), pltpu.VMEM((1, -(-count // lanes) * lanes), f32), pltpu.VMEM((rows, lanes), f32)],
        first, got_first, keep, got, gains,
    )


def last_sum_kernel(count, parts, total, out, gains):
    unit, head = total.shape[0], out.shape[1]
    far = parts.shape[0]
    size, short, lanes, beside, rest, _ = layout(far, unit, total.shape[1] * far, head, count)
    sums = jnp.sum(parts[...].astype(f32), axis=0)
    total[...] = sums[:unit, :size]
    for g in range(unit // beside if beside else 0):
        out[:beside, g * (lanes - size) : (g + 1) * (lanes - size)] = sums[g * beside : (g + 1) * beside, size:]
    for j in range(head // lanes):
        start_row = unit + j * (short - beside)
        out[beside:, j * lanes : (j + 1) * lanes] = sums[start_row : start_row + short - beside]
    for i in range(-(-count // lanes)):
        gains[:, i * lanes : (i + 1) * lanes] = sums[unit + rest + i : unit + rest + i + 1]


def last_sum(parts, unit, columns, head, count):
    far, _, lanes = parts.shape
    return call(
        functools.partial(last_sum_kernel, count),
        2,
        (wide(unit, columns // far), wide(2 * unit // far, head), wide(1, -(-count // lanes) * lanes)),
        [VECTORS],
        [],
        parts,
    )


def down_rows_kernel(part, parts, result):
    for i in range(4):
        for z in range(parts.shape[2] // part):
            first = (4 * z + i) * part
            result[:, first : first + part] = parts[i, :, z * part : (z + 1) * part].astype(f32)


def down_rows(parts, part):
    _, columns, rows = parts.shape
    return call(functools.partial(down_rows_kernel, part), 2, wide(columns, 4 * rows), [VECTORS], [], parts)


def keys_back_kernel(
    early, place, total, received, raw, table, gain_key, partial, grad_residual, tokens, gain_in, grad_queries, grad_gains,
    grad_gain_post, grad_gain_query, k0, k1, k2, k3, grad_tokens, keep, send, sums, grad_projected, gains, weight, sem,
):
    copies = fetch(place, key_columns((k0, k1, k2, k3), weight.shape[1]), weight, sem)
    rows, dim = tokens.shape[0], raw.shape[1]
    here = half_plane(place[0], rows)
    keys = total[0, here] + received[0].astype(f32)
    values = total[1, here] + received[1].astype(f32)
    back, grad_gain_key = rms_back(raw[here], gain_key[...], turn(keys, table[0, here], -table[1, here]))
    grad_projected[:, :dim] = back.astype(bf16)
    grad_projected[:, dim:] = values.astype(bf16)
    wait(copies)
    normed = partial[...] + nt(grad_projected[...], weight[...])
    back, grad_gain_in = rms_back(tokens[...].astype(f32), gain_in[...], normed)
    grad_tokens[...] = grad_residual[...] + back
    model, width = tokens.shape[1], keep.shape[1]
    gains[...] = jnp.zeros_like(gains)
    gains[:, :model] = grad_gain_in
    for i in range(2):
        gains[:, (i + 1) * model : (i + 2) * model] = grad_gains[i : i + 1]
    gains[:, 3 * model : 4 * model] = grad_gain_post[...]
    gains[:, 4 * model : 4 * model + dim] = grad_gain_query[...]
    gains[:, 4 * model + dim : 4 * model + 2 * dim] = grad_gain_key
    block = grad_queries.shape[1] * 3 // 2 // (2 * early[0])
    every = jnp.concatenate([grad_queries[:, early[1] * 2 * block :], grad_projected[...]], axis=1)
    parts = [jnp.concatenate(columns_of(every, i, range(early[0] - early[1]), block), axis=1) for i in range(2)]
    for i in range(2):

        @pl.when(place[NEAR] == i)
        def _():
            keep[...] = parts[i]
            send[:rows] = parts[1 - i]

    extra = jnp.concatenate([gains[:, i * width : (i + 1) * width] for i in range(sums.shape[0])], axis=0)
    sums[...] = extra
    send[rows:] = extra.astype(bf16)


def keys_back(
    far, early, place, total, received, raw, table, gain_key, partial, grad_residual, tokens, gain_in, grad_queries, grad_gains,
    grad_gain_post, grad_gain_query, pieces,
):
    rows, model = tokens.shape
    dim = raw.shape[1]
    width = (far - early) * (HQ + 2) * dim // (2 * far)
    more = -(-(4 * model + 2 * dim) // (16 * width)) * 16
    return call(
        functools.partial(keys_back_kernel, (far, early)),
        4,
        (wide(rows, model), low(rows, width), low(rows + more, width), wide(more, width)),
        [SCALARS, *[VECTORS] * 13, *[ANYWHERE] * 4],
        [
            pltpu.VMEM((rows, 2 * dim), bf16),
            pltpu.VMEM((1, more * width), f32),
            pltpu.VMEM((model, 2 * dim), bf16),
            pltpu.SemaphoreType.DMA((4,)),
        ],
        place, total, received, raw, table, gain_key, partial, grad_residual, tokens, gain_in, grad_queries, grad_gains,
        grad_gain_post, grad_gain_query, *pieces,
    )


def shift(value, by):
    length = lax.axis_size("far")
    pairs = [(i, i + by) for i in range(length) if 0 <= i + by < length]
    return lax.ppermute(value, "far", pairs)


def swap(value, axis):
    return lax.ppermute(value, axis, [(0, 1), (1, 0)])


def diagonal(value):
    return lax.ppermute(value, ("near", "chip"), [(i, 3 - i) for i in range(4)])


def around(values):
    return swap(values[0], "chip"), swap(values[1], "near"), diagonal(values[2])


def far_swap(value, step):
    return lax.ppermute(value, "far", [(i, i ^ step) for i in range(lax.axis_size("far"))])


def after(value, *others):
    return lax.optimization_barrier((value, others))[0]


def halving(value, axis, steps):
    place = lax.axis_index("far")
    for step in steps:
        shape = (*value.shape[:axis], 2, value.shape[axis] // 2, *value.shape[axis + 1 :])
        value = value.reshape(shape)
        bit = place // step % 2
        mine = lax.dynamic_index_in_dim(value, bit, axis, keepdims=False)
        other = lax.dynamic_index_in_dim(value, 1 - bit, axis, keepdims=False)
        value = mine + far_swap(other.astype(bf16), step).astype(f32)
    return value


def shards(
    tokens,
    block_ids,
    w_qkv,
    w_out,
    w_gate,
    w_up,
    w_down,
    gain_in,
    gain_query,
    gain_key,
    gain_attn,
    gain_pre,
    gain_post,
    cotangent,
):
    seq_count, rows, model = tokens.shape
    dim = gain_query.shape[0]
    query_width = HQ * dim
    plane = 2 * rows
    span = WINDOW + plane + BLOCK
    full_len = block_ids.shape[1]
    far_count = lax.axis_size("far")
    near, chip, core = lax.axis_index("near"), lax.axis_index("chip"), lax.axis_index("core")
    far = lax.axis_index("far")
    half_far = far_count // 2
    far_bits = [1 << i for i in reversed(range(far_count.bit_length() - 1))]
    low_bits = far_bits[1:]
    half = far // half_far
    bit = far // low_bits[0] % 2
    place = jnp.stack([near, chip, core, far % 2, half, bit]).astype(jnp.int32)
    start = far * plane
    ff = w_gate.shape[1]
    part = ff // (far_count * 4)
    early = query_width // (w_qkv.shape[1] // far_count)
    tokens = tokens.reshape(rows, model)
    cotangent = cotangent.reshape(rows, model)
    gain_in, gain_query, gain_key, gain_attn, gain_pre, gain_post = (
        g.reshape(1, -1) for g in (gain_in, gain_query, gain_key, gain_attn, gain_pre, gain_post)
    )

    qkv_chip, peer_tokens = swap(w_qkv, "chip"), swap(tokens, "near")
    gates_own, *gates_other = chip_columns(place, w_gate, w_up, far_count)
    split = lax.dynamic_index_in_dim(w_down.reshape(-1, 2, 2, part, model), near, 1, keepdims=False)
    down_own = lax.dynamic_index_in_dim(split, chip, 1, keepdims=False).reshape(-1, model)
    down_other = lax.dynamic_index_in_dim(split, 1 - chip, 1, keepdims=False).reshape(-1, model)
    qkv_core, out_core, down_core = swap(w_qkv, "core"), swap(w_out, "core"), swap(down_own, "core")
    qkv_pieces = w_qkv, qkv_chip, qkv_core, swap(qkv_chip, "core")

    frequency = 10000.0 ** (-jnp.arange(dim // 2, dtype=f32) * 2.0 / dim)
    angles = (start + jnp.arange(plane)).astype(f32)[:, None] * frequency[None, :]
    table = jnp.stack([jnp.cos(angles), jnp.sin(angles)])
    normed_in, pair, raw_keys, every = keys_of(
        place, after(tokens, down_core, out_core, gates_own), peer_tokens, gain_in, gain_key, table, qkv_pieces
    )
    gates_core = swap(gates_own, "core")
    out_chip = swap(after(w_out, qkv_chip), "chip")
    first = swap(after(gates_other[0], qkv_chip), "chip")
    second = swap(after(gates_other[1], out_chip), "chip")
    down_chip = swap(after(down_other, first), "chip")
    out_pieces = w_out, out_chip, out_core, swap(out_chip, "core")
    first_rest, second_rest = far_swap(first, 1), far_swap(second, 1)
    four = first, second, first_rest, second_rest
    gates = gates_own, gates_core, *four, *(swap(p, "core") for p in four)
    downs = down_own, down_chip, down_core, swap(down_chip, "core")

    padded = jnp.pad(block_ids, ((0, 0), (WINDOW, BLOCK)), constant_values=1 << 30)
    key_ids = lax.dynamic_slice_in_dim(padded, start, span, 1)
    query_ids = lax.dynamic_slice_in_dim(block_ids, start + near * rows, rows, 1).reshape(rows, 1)

    planes = (shift(pair, 2), shift(pair, 1), pair, shift(pair, -1))
    queries, raw_queries = queries_of(place, normed_in, gain_query, table, qkv_pieces)
    chances, heads_out, attn_out, residual, normed_pre = attend(
        place, after(queries, first, gates_core), planes, key_ids, query_ids, tokens, gain_attn, gain_pre, out_pieces
    )

    far_normed = far_swap(after(normed_pre, first_rest), half_far)
    blocks = (normed_pre, *around([normed_pre] * 3))
    all_normed, hidden, slope, gelu, own, *sent = forward(place, after(blocks, far_normed), gates, downs)
    far_normed = after(far_normed, second_rest)
    far_normed = (far_normed, *around([far_normed] * 3))
    sent = after(sent, *far_normed)
    output, grad_down_proj, grad_gain_post = turning((own, *around(sent)), residual, cotangent, gain_post)
    far_down = far_swap(grad_down_proj, half_far)
    blocks = (grad_down_proj, *around([grad_down_proj] * 3))
    far_kept = far_hidden(place, hidden, after(far_normed, grad_down_proj), gates)
    blocks = after(blocks, far_down, *far_kept)
    all_down, gate_low, up_low, own, *sent = backward(place, blocks, slope, gelu, gates, downs)
    far_down = (far_down, *around([far_down] * 3))
    sent = after(sent, *far_down)
    parts = (own, *around(sent))
    keep_grads, send_grads = weight_grads(
        place, all_normed, all_down, after(gate_low, *sent), up_low, far_normed, far_down, far_kept, downs
    )
    got_grads = swap(after(send_grads, parts), "core")
    (
        grad_residual, own_right, other_right, grad_gains, grad_gain_query, grad_queries, *sent,
    ) = attend_back(
        far_count, early, place, after(parts, keep_grads), residual, attn_out, cotangent, gain_pre, gain_attn, chances, queries, raw_queries, table, gain_query,
        planes, out_pieces,
    )
    grad_gates, send_other, send_own, grad_down, send_down = add_cores(place, after(keep_grads, grad_queries), got_grads, model)
    total = after(sent[2], send_down) + shift(sent[0], -2).astype(f32)
    total = total + shift(sent[1], -1).astype(f32) + shift(sent[3], 1).astype(f32)
    partial = queries_back(place, after(grad_queries, send_down), qkv_pieces)
    got, got_heads = swap(other_right, "near"), swap(after(heads_out, grad_queries), "near")
    total, grad_gates, send_other, send_own, grad_down, send_down, partial, got, got_heads = lax.optimization_barrier(
        (total, grad_gates, send_other, send_own, grad_down, send_down, partial, got, got_heads)
    )

    received = swap(
        lax.dynamic_slice_in_dim(total, (1 - near) * rows, rows, 1).astype(bf16), "near"
    )
    got_down, got_other, got_own = (far_swap(g, low_bits[0]) for g in (send_down, send_other, send_own))
    keep_first, send_first = first_products(place, every, heads_out, got_heads, own_right, got)
    keep_first, send_first = first_cores(place, keep_first, swap(send_first, "core"))
    got_first = swap(send_first, "chip")
    grad_tokens, own_right, other_right, gains = keys_back(
        far_count, early, place, after(total, send_first), received, raw_keys, table, gain_key, partial, grad_residual, tokens, gain_in,
        grad_queries, grad_gains, grad_gain_post, grad_gain_query, qkv_pieces,
    )
    keep, send, gains = last_products(place, every, after(own_right, got_down), swap(other_right, "near"), gains)
    keep, send, gains = last_cores(place, after(keep, got_other), swap(send, "core"), gains)
    grad_down = add_down(grad_down, got_down)
    sums = last_chips(
        far_count, keep_first, got_first, keep, swap(send, "chip"), gains, query_width // 4, 4 * model + 2 * dim
    )
    columns = model // far_count // 2
    down_parts = halving(grad_down, 1, low_bits[1:]).astype(bf16).reshape(2, 2, columns, -1)
    down_parts = down_parts.transpose(1, 0, 2, 3).reshape(4, columns, -1)
    down_parts = lax.all_to_all(down_parts, ("near", "chip"), 0, 0, tiled=True)
    other_gates = add_gates(True, place, after(grad_gates, send), got_other)
    peer_gates = swap(halving(other_gates, 2, low_bits[1:]).astype(bf16), "chip")
    sums, got_own = lax.optimization_barrier((sums, got_own))

    sums = lax.all_to_all(sums, "far", 0, 0, tiled=True)
    qkv_total, out_total, gains = last_sum(sums, model // 4, w_qkv.shape[1] // 2, query_width // 4, 4 * model + 2 * dim)
    out_total, gains = out_total.T, gains.reshape(-1)
    own_gates = halving(add_gates(False, place, grad_gates, got_own), 2, low_bits[1:]).astype(bf16)
    mine = [lax.dynamic_index_in_dim(g, core, 0, keepdims=False) for g in (own_gates, peer_gates)]
    theirs = [lax.dynamic_index_in_dim(g, 1 - core, 0, keepdims=False) for g in (own_gates, peer_gates)]
    gate_total, up_total = gather_gates(place, *mine, *(swap(g, "core") for g in theirs))
    down_total = down_rows(down_parts, part).T

    gain_in, gain_pre, gain_attn, gain_post = (gains[i * model : (i + 1) * model] for i in range(4))
    gain_query, gain_key = gains[4 * model :][:dim], gains[4 * model + dim :][:dim]
    return (
        output.reshape(seq_count, rows, model),
        grad_tokens.reshape(seq_count, rows, model),
        qkv_total,
        out_total,
        gate_total,
        up_total,
        down_total,
        gain_in,
        gain_query,
        gain_key,
        gain_attn,
        gain_pre,
        gain_post,
    )


def solution(mesh):
    seq, dp = mesh.devices.shape
    parts = Mesh(mesh.devices.reshape(seq // 2, 2, 2, dp // 2), (*SEQ, *DP))
    rows = P(DP, None)
    whole = P(None)
    placed = (P(DP, SEQ, None), P(DP, None), *[rows] * 5, *[whole] * 6, P(DP, SEQ, None))
    return jax.shard_map(
        shards,
        mesh=parts,
        in_specs=placed,
        out_specs=(*[P(DP, SEQ, None)] * 2, *[P(DP, SEQ)] * 5, *[whole] * 6),
        check_vma=False,
    )
```

```python
import functools

import jax
import jax.numpy as jnp
from jax import lax
from jax.experimental import pallas as pl
from jax.experimental.pallas import tpu as pltpu
from jax.sharding import Mesh, PartitionSpec as P

HQ = 4
WINDOW = 512
BLOCK = 256


epsilon = 1e-06
bf16 = jnp.bfloat16
f32 = jnp.float32
ROOT = 0.7978845608028654

SEQ = ("far", "near")
DP = ("chip", "core")
SQUARE = ("near", "chip", "core")

ANYWHERE = pl.BlockSpec(memory_space=pl.ANY)
VECTORS = pl.BlockSpec(memory_space=pltpu.VMEM)
SCALARS = pl.BlockSpec(memory_space=pltpu.SMEM)


def low(*shape):
    return jax.ShapeDtypeStruct(shape, bf16)


def wide(*shape):
    return jax.ShapeDtypeStruct(shape, f32)


def call(kernel, microseconds, out_shape, in_specs, scratch, *args, megabytes=48):
    return pl.pallas_call(
        kernel,
        out_shape=out_shape,
        in_specs=in_specs,
        out_specs=jax.tree.map(lambda _: VECTORS, out_shape),
        scratch_shapes=scratch,
        cost_estimate=pl.CostEstimate(
            flops=microseconds * 1_000_000_000, bytes_accessed=1 << 20, transcendentals=0
        ),
        compiler_params=pltpu.CompilerParams(vmem_limit_bytes=megabytes << 20),
    )(*args)


def steps(total, size):
    return [(first, min(first + size, total)) for first in range(0, total, size)]


NEAR, CHIP, CORE, PARITY, HALF, BIT = range(6)


def slots(place):
    chip, core = place[CHIP], place[CORE]
    return chip * 2 + core, (1 - chip) * 2 + core, chip * 2 + 1 - core, (1 - chip) * 2 + 1 - core


def at(start, size, multiple=16):
    return pl.ds(pl.multiple_of(start, multiple), size)


def begin(pairs, sem):
    copies = [pltpu.make_async_copy(a, b, sem.at[i]) for i, (a, b) in enumerate(pairs)]
    for c in copies:
        c.start()
    return copies


def fetch(place, pieces, target, sem):
    rows = target.shape[0] // 4
    return begin([(p, target.at[at(s * rows, rows)]) for s, p in zip(slots(place), pieces)], sem)


def fetch_gates(place, pieces, target, sem):
    own, core, chip, other = pieces[0], pieces[1], pieces[2:6], pieces[6:10]
    rows = target.shape[1] // 4
    half = rows // 2
    a, b, c, d = (s * rows for s in slots(place))
    pairs = [(own, target.at[:, at(a, rows)]), (core, target.at[:, at(c, rows)])]
    for start, four in ((b, chip), (d, other)):
        for k in range(2):
            pairs.append((four[k], target.at[place[PARITY], at(start + k * half, half)]))
            pairs.append((four[2 + k], target.at[1 - place[PARITY], at(start + k * half, half)]))
    return begin(pairs, sem)


def wait(copies):
    for c in copies:
        c.wait()


def nn(a, b):
    return jnp.dot(a, b, preferred_element_type=f32)


def nt(a, b):
    return lax.dot_general(a, b, (((1,), (1,)), ((), ())), preferred_element_type=f32)


def tn(a, b):
    return lax.dot_general(a, b, (((0,), (0,)), ((), ())), preferred_element_type=f32)


def rms(value, gain):
    return value * lax.rsqrt(jnp.mean(value * value, axis=-1, keepdims=True) + epsilon) * gain


def rms_back(value, gain, grad):
    scale = lax.rsqrt(jnp.mean(value * value, axis=-1, keepdims=True) + epsilon)
    unit = value * scale
    slope = grad * gain
    back = scale * (slope - unit * jnp.mean(slope * unit, axis=-1, keepdims=True))
    return back, jnp.sum(grad * unit, axis=0, keepdims=True)


def turn(value, cosine, sine):
    half = value.shape[-1] // 2
    a, b = value[:, :half], value[:, half:]
    return jnp.concatenate([a * cosine - b * sine, b * cosine + a * sine], axis=-1)


def half_plane(which, rows):
    return pl.ds(pl.multiple_of(which * rows, 128), rows)


def slice_kernel(far, part, place, gate, up, own, other0, other1, source, sem):
    rows, ff = gate.shape
    copies = begin([(w, source.at[i, :, :ff]) for i, w in enumerate((gate, up))], sem)
    near, chip = place[NEAR], place[CHIP]
    block = 48
    half = rows // 2

    def cut(i, which, target, from_row, to_row):
        for z in range(far):
            first, last = z * part, (z + 1) * part
            lo, hi = first // 128 * 128, min(-(-last // 128) * 128, far * part)
            span = -(-(hi - lo) // 128) * 128 + 128
            shift = (z * 3 + near * 2 + which) * part
            coarse = shift // 128 * 128
            x = source[i, from_row, at(lo + coarse, span, 128)]
            x = pltpu.roll(x, (span - (shift - coarse)) % span, 1)[:, : hi - lo]
            if first > lo:
                column = lax.broadcasted_iota(jnp.int32, x.shape, 1)
                x = jnp.where(column < first - lo, target[to_row, lo:hi], x)
            target[to_row, lo:hi] = x

    wait(copies)
    for k, other in enumerate((other0, other1)):

        def send(r, _):
            cut(place[PARITY], 1 - chip, other, at(k * half + r * block, block), at(r * block, block))
            return 0

        lax.fori_loop(0, half // block, send, 0)
    for i in range(2):

        def keep(r, _):
            here = at(r * block, block)
            cut(i, chip, own.at[i], here, here)
            return 0

        lax.fori_loop(0, rows // block, keep, 0)


def chip_columns(place, gate, up, far):
    rows, ff = gate.shape
    part = ff // (4 * far)
    source = -(-ff // 128) * 128 + 768
    return call(
        functools.partial(slice_kernel, far, part),
        6,
        (low(2, rows, ff // 4), low(rows // 2, ff // 4), low(rows // 2, ff // 4)),
        [SCALARS, ANYWHERE, ANYWHERE],
        [pltpu.VMEM((2, rows, source), bf16), pltpu.SemaphoreType.DMA((2,))],
        place,
        gate,
        up,
    )


def key_columns(pieces, count):
    return [p.at[:, p.shape[1] - count :] for p in pieces]


def query_columns(pieces, count):
    return [p.at[:, :count] for p in pieces]


def keys_kernel(place, own, peer, gain_in, gain_key, table, k0, k1, k2, k3, normed, pair, raw, every, weight, sem):
    copies = fetch(place, key_columns((k0, k1, k2, k3), weight.shape[1]), weight, sem)
    rows, near, width = own.shape[0], place[0], raw.shape[1]
    mine = rms(own[...].astype(f32), gain_in[...]).astype(bf16)
    normed[...] = mine
    every[half_plane(near, rows)] = mine
    every[half_plane(1 - near, rows)] = rms(peer[...].astype(f32), gain_in[...]).astype(bf16)
    wait(copies)
    projected = nn(every[...], weight[...])
    raw[...] = projected[:, :width]
    pair[0] = turn(rms(projected[:, :width], gain_key[...]), table[0], table[1]).astype(bf16)
    pair[1] = projected[:, width:].astype(bf16)


def keys_of(place, own, peer, gain_in, gain_key, table, pieces):
    rows, model = own.shape
    dim = gain_key.shape[1]
    return call(
        keys_kernel,
        2,
        (low(rows, model), low(2, 2 * rows, dim), wide(2 * rows, dim), low(2 * rows, model)),
        [SCALARS, *[VECTORS] * 5, *[ANYWHERE] * 4],
        [pltpu.VMEM((model, 2 * dim), bf16), pltpu.SemaphoreType.DMA((4,))],
        place, own, peer, gain_in, gain_key, table, *pieces,
    )


def queries_kernel(place, normed, gain, table, q0, q1, q2, q3, queries, raw, weight, sem):
    wait(fetch(place, query_columns((q0, q1, q2, q3), weight.shape[1]), weight, sem))
    rows, dim = normed.shape[0], gain.shape[1]
    here = half_plane(place[0], rows)
    cosine, sine = table[0, here], table[1, here]
    for h in range(HQ):
        projected = nn(normed[...], weight[:, h * dim : (h + 1) * dim])
        raw[h * rows : (h + 1) * rows] = projected
        turned = turn(rms(projected, gain[...]), cosine, sine).astype(bf16)
        queries[h * rows : (h + 1) * rows] = turned * jnp.asarray(dim**-0.5, bf16)


def queries_of(place, normed, gain, table, pieces):
    rows, model = normed.shape
    dim = gain.shape[1]
    return call(
        queries_kernel,
        6,
        (low(HQ * rows, dim), wide(HQ * rows, dim)),
        [SCALARS, *[VECTORS] * 3, *[ANYWHERE] * 4],
        [pltpu.VMEM((model, HQ * dim), bf16), pltpu.SemaphoreType.DMA((4,))],
        place, normed, gain, table, *pieces,
    )


def attend_kernel(
    place, queries, kv0, kv1, kv2, kv3, key_ids, query_ids, tokens, gain_attn, gain_pre, o0, o1, o2, o3,
    chances, heads, attn_out, residual, normed_pre, keys, values, weight, sem,
):
    copies = fetch(place, (o0, o1, o2, o3), weight, sem)
    plane, dim = kv0.shape[1], kv0.shape[2]
    for i, kv in enumerate((kv0, kv1, kv2, kv3)):
        keys[i * plane : (i + 1) * plane] = kv[0]
        values[i * plane : (i + 1) * plane] = kv[1]
    rows, span = query_ids.shape[0], key_ids.shape[1]
    row = lax.broadcasted_iota(jnp.int32, (rows, span), 0) + place[0] * rows
    column = lax.broadcasted_iota(jnp.int32, (rows, span), 1)
    same = key_ids[...] == query_ids[...]
    allowed = same | ((key_ids[...] < query_ids[...]) & (column >= row))
    chances[...] = nt(queries[...], keys[...])
    for h in range(HQ):
        here = slice(h * rows, (h + 1) * rows)
        scores = jnp.where(allowed, chances[here], -1e30)
        grown = jnp.exp(scores - jnp.max(scores, axis=-1, keepdims=True))
        chances[here] = grown / jnp.sum(grown, axis=-1, keepdims=True)
    seen = nn(chances[...].astype(bf16), values[...]).astype(bf16)
    for h in range(HQ):
        heads[:, h * dim : (h + 1) * dim] = seen[h * rows : (h + 1) * rows]
    wait(copies)
    out = nn(heads[...], weight[...])
    attn_out[...] = out
    total = tokens[...].astype(f32) + rms(out, gain_attn[...])
    residual[...] = total
    normed_pre[...] = rms(total, gain_pre[...]).astype(bf16)


def attend(place, queries, planes, key_ids, query_ids, tokens, gain_attn, gain_pre, pieces):
    rows, model = tokens.shape
    dim, span = queries.shape[1], key_ids.shape[1]
    return call(
        attend_kernel,
        2,
        (wide(HQ * rows, span), low(rows, HQ * dim), wide(rows, model), wide(rows, model), low(rows, model)),
        [SCALARS, *[VECTORS] * 10, *[ANYWHERE] * 4],
        [
            pltpu.VMEM((span, dim), bf16),
            pltpu.VMEM((span, dim), bf16),
            pltpu.VMEM((HQ * dim, model), bf16),
            pltpu.SemaphoreType.DMA((4,)),
        ],
        place, queries, *planes, key_ids, query_ids, tokens, gain_attn, gain_pre, *pieces,
    )


def gated(gate, up):
    square = gate * gate
    wave = jnp.tanh(ROOT * gate * (1.0 + 0.044715 * square))
    half = 0.5 * (1.0 + wave)
    value = gate * half
    bend = half + 0.5 * ROOT * gate * (1.0 - wave * wave) * (1.0 + 3.0 * 0.044715 * square)
    return (value * up).astype(bf16), (bend * up).astype(bf16), value.astype(bf16)


def forward_kernel(place, x0, x1, x2, x3, *refs):
    gates, downs = refs[:10], refs[10:14]
    whole, hidden, slope, gelu, total, p1, p2, p3 = refs[14:22]
    w_gates, w_down, sem, late_sem = refs[22:]
    copies = fetch_gates(place, gates, w_gates, sem)
    late = fetch(place, downs, w_down, late_sem)
    rows = x0.shape[0]
    for i, x in enumerate((x0, x1, x2, x3)):
        whole[i * rows : (i + 1) * rows] = x[...]
    wait(copies)
    for first, last in steps(w_down.shape[0], 256):
        gate = nn(whole[...], w_gates[0, :, first:last])
        up = nn(whole[...], w_gates[1, :, first:last])
        hidden[:, first:last], slope[:, first:last], gelu[:, first:last] = gated(gate, up)
    wait(late)
    for first, last in steps(w_down.shape[1], 384):
        part = nn(hidden[...], w_down[:, first:last])
        total[:, first:last] = part[:rows]
        for i, p in enumerate((p1, p2, p3)):
            p[:, first:last] = part[(i + 1) * rows : (i + 2) * rows].astype(bf16)


def weight_room(model, ff):
    return [
        pltpu.VMEM((2, model, ff), bf16),
        pltpu.VMEM((ff, model), bf16),
        pltpu.SemaphoreType.DMA((10,)),
        pltpu.SemaphoreType.DMA((6,)),
    ]


def forward(place, blocks, gates, downs):
    rows, model = blocks[0].shape
    ff = gates[0].shape[2]
    return call(
        forward_kernel,
        13,
        (low(4 * rows, model), *[low(4 * rows, ff)] * 3, wide(rows, model), *[low(rows, model)] * 3),
        [SCALARS, *[VECTORS] * 4, *[ANYWHERE] * 14],
        weight_room(model, ff),
        place, *blocks, *gates, *downs,
    )


def backward_kernel(place, x0, x1, x2, x3, slope, gelu, *refs):
    gates, downs = refs[:10], refs[10:14]
    whole, gate_low, up_low, total, p1, p2, p3 = refs[14:21]
    w_gates, w_down, late_sem, sem = refs[21:]
    copies = fetch(place, downs, w_down, sem)
    late = fetch_gates(place, gates, w_gates, late_sem)
    rows = x0.shape[0]
    for i, x in enumerate((x0, x1, x2, x3)):
        whole[i * rows : (i + 1) * rows] = x[...]
    wait(copies)
    for first, last in steps(w_down.shape[0], 256):
        back = nt(whole[...], w_down[first:last])
        gate_low[:, first:last] = (back * slope[:, first:last].astype(f32)).astype(bf16)
        up_low[:, first:last] = (back * gelu[:, first:last].astype(f32)).astype(bf16)
    wait(late)
    for first, last in steps(w_down.shape[1], 384):
        part = nt(gate_low[...], w_gates[0, first:last]) + nt(up_low[...], w_gates[1, first:last])
        total[:, first:last] = part[:rows]
        for i, p in enumerate((p1, p2, p3)):
            p[:, first:last] = part[(i + 1) * rows : (i + 2) * rows].astype(bf16)


def backward(place, blocks, slope, gelu, gates, downs):
    rows, model = blocks[0].shape
    ff = gates[0].shape[2]
    return call(
        backward_kernel,
        15,
        (low(4 * rows, model), *[low(4 * rows, ff)] * 2, wide(rows, model), *[low(rows, model)] * 3),
        [SCALARS, *[VECTORS] * 6, *[ANYWHERE] * 14],
        weight_room(model, ff),
        place, *blocks, slope, gelu, *gates, *downs,
    )


def far_kernel(window, place, own, n0, n1, n2, n3, *refs):
    gates, (hiddens, slope, gelu, w_gates, tokens, room, sem) = refs[:10], refs[10:]
    start, width = window
    copies = fetch_gates(place, gates, w_gates, sem)
    rows = n0.shape[0]
    for i, n in enumerate((n0, n1, n2, n3)):
        tokens[i * rows : (i + 1) * rows] = n[...]
    hiddens[:, : 4 * rows] = own[...].T
    wait(copies)
    for first, last in steps(hiddens.shape[0], 256):
        gate = nn(tokens[...], w_gates[0, :, first:last])
        up = nn(tokens[...], w_gates[1, :, first:last])
        value, bend, share = gated(gate, up)
        hiddens[first:last, 4 * rows :] = value.T
        if first >= width or last <= start:

            @pl.when(place[HALF] == int(first >= width))
            def _():
                room[0, :, first:last], room[1, :, first:last] = bend, share

        else:
            room[0, :, first:last], room[1, :, first:last] = bend, share
    here = at(place[HALF] * start, width, 128)
    slope[...] = room[0, :, here]
    gelu[...] = room[1, :, here]


def window_of(ff):
    start = ff // 2 // 128 * 128
    return start, ff - start


def far_hidden(place, hidden, far_normed, gates):
    rows, model = far_normed[0].shape
    ff = gates[0].shape[2]
    start, width = window_of(ff)
    return call(
        functools.partial(far_kernel, (start, width)),
        11,
        (low(ff, 8 * rows), low(4 * rows, width), low(4 * rows, width)),
        [SCALARS, *[VECTORS] * 5, *[ANYWHERE] * 10],
        [
            pltpu.VMEM((2, model, ff), bf16),
            pltpu.VMEM((4 * rows, model), bf16),
            pltpu.VMEM((2, 4 * rows, ff), bf16),
            pltpu.SemaphoreType.DMA((10,)),
        ],
        place, hidden, *far_normed, *gates,
    )


def weights_kernel(
    window, place, h_normed, h_down, h_gate, h_up, n0, n1, n2, n3, d0, d1, d2, d3, h_hiddens, h_slope, h_gelu, w0, w1, w2, w3,
    h_keep, h_send, w_down, grads, tokens, backs, gate_low, up_low, hiddens, slope, gelu, keep, send,
    sem, soon_sem, late_sem, out_sem,
):
    start, width = window
    half, core, bit = place[HALF], place[CORE], place[BIT]
    own, model = h_normed.shape
    rows = own // 4
    columns = at(half * start, width, 128)

    def blocks(parts, target):
        return [(p, target.at[own + i * rows : own + (i + 1) * rows]) for i, p in enumerate(parts)]

    first = begin([(h_gate, gate_low), (h_up, up_low)], sem)
    soon = [*blocks((d0, d1, d2, d3), backs), (h_slope, slope), (h_gelu, gelu), (h_down, backs.at[:own])]
    for slot, piece in zip(slots(place), (w0, w1, w2, w3)):
        soon.append((piece, w_down.at[at(slot * piece.shape[0], piece.shape[0])]))
    soon = begin(soon, soon_sem)
    late = begin([*blocks((n0, n1, n2, n3), tokens), (h_normed, tokens.at[:own]), (h_hiddens, hiddens)], late_sem)
    wait(first)
    grads[core, :, :own] = gate_low[:, columns].T
    grads[1 - core, :, :own] = up_low[:, columns].T
    wait(soon)
    for first, last in steps(width, 256):
        back = nt(backs[own:], w_down[at(half * start + first, last - first)])
        c = slice(first, last)
        grads[core, c, own:] = (back * slope[:, c].astype(f32)).astype(bf16).T
        grads[1 - core, c, own:] = (back * gelu[:, c].astype(f32)).astype(bf16).T
    wait(late)
    kept = hiddens.shape[0] // 2
    part = kept // 2
    results = []
    for i in range(2):
        r = at(half * (kept - start) + i * part, part)
        slot = i ^ bit
        keep[slot, :, :model] = nn(grads[0, r], tokens[...]).astype(bf16)
        send[slot, :, :model] = nn(grads[1, r], tokens[...]).astype(bf16)
    gates = pl.ds(0, model)
    results += [(keep.at[:, :, gates], h_keep.at[:, :, gates]), (send.at[:, :, gates], h_send.at[:, :, gates])]
    done = begin(results, out_sem)
    span = keep.shape[2] - model
    columns = at(half * (model - span), span, 128)
    for i in range(4):
        result = nn(hiddens[i * part : (i + 1) * part], backs[:, columns]).astype(bf16)

        @pl.when(core == i % 2)
        def _():
            keep[i // 2, :, model:] = result

        @pl.when(core != i % 2)
        def _():
            send[i // 2, :, model:] = result

    rest = pl.ds(model, span)
    for i, (a, b) in enumerate(((keep, h_keep), (send, h_send))):
        copy = pltpu.make_async_copy(a.at[:, :, rest], b.at[:, :, rest], out_sem.at[2 + i])
        copy.start()
        done.append(copy)
    wait(done)


def weight_grads(place, normed, down, gate_low, up_low, far_normed, far_down, far_kept, downs):
    own, model = normed.shape
    ff = gate_low.shape[1]
    start, width = window_of(ff)
    part = ff // 4
    span = -(-model // 256) * 128
    shape = (2, part, model + span)
    return pl.pallas_call(
        functools.partial(weights_kernel, (start, width)),
        out_shape=(low(*shape), low(*shape)),
        in_specs=[SCALARS, *[ANYWHERE] * 19],
        out_specs=(ANYWHERE, ANYWHERE),
        scratch_shapes=[
            pltpu.VMEM((ff, model), bf16),
            pltpu.VMEM((2, width, 2 * own), bf16),
            pltpu.VMEM((2 * own, model), bf16),
            pltpu.VMEM((2 * own, model), bf16),
            pltpu.VMEM((own, ff), bf16),
            pltpu.VMEM((own, ff), bf16),
            pltpu.VMEM((ff, 2 * own), bf16),
            pltpu.VMEM((own, width), bf16),
            pltpu.VMEM((own, width), bf16),
            pltpu.VMEM(shape, bf16),
            pltpu.VMEM(shape, bf16),
            pltpu.SemaphoreType.DMA((2,)),
            pltpu.SemaphoreType.DMA((11,)),
            pltpu.SemaphoreType.DMA((6,)),
            pltpu.SemaphoreType.DMA((4,)),
        ],
        cost_estimate=pl.CostEstimate(flops=16_000_000_000, bytes_accessed=1 << 20, transcendentals=0),
        compiler_params=pltpu.CompilerParams(vmem_limit_bytes=48 << 20),
    )(place, normed, down, gate_low, up_low, *far_normed, *far_down, *far_kept, *downs)


def turning_kernel(own, r1, r2, r3, residual, cotangent, gain, output, grad, grad_gain):
    down = own[...] + r1[...].astype(f32) + r2[...].astype(f32) + r3[...].astype(f32)
    output[...] = (residual[...] + rms(down, gain[...])).astype(bf16)
    back, grad_gain[...] = rms_back(down, gain[...], cotangent[...].astype(f32))
    grad[...] = back.astype(bf16)


def turning(parts, residual, cotangent, gain):
    rows, model = residual.shape
    return call(
        turning_kernel,
        1,
        (low(rows, model), low(rows, model), wide(1, model)),
        [VECTORS] * 7,
        [],
        *parts, residual, cotangent, gain,
    )


def cores_kernel(place, keep, got, gates, send_other, send_own, down, send_down, turned):
    model = gates.shape[1]
    gates[...] = keep[0, :, :model].astype(f32) + got[0, :, :model].astype(f32)
    sent = keep[1, :, :model].astype(f32) + got[1, :, :model].astype(f32)
    half, short = model // 2, send_own.shape[0]
    for i in range(2):

        @pl.when(place[CHIP] == i)
        def _():
            for target, j in ((send_own, i), (send_other, 1 - i)):
                for k in range(2):
                    block = sent[k * short : (k + 1) * short, j * half : (j + 1) * half]
                    target[:, k * half : (k + 1) * half] = block.astype(bf16)

    unit, part = down.shape[0], turned.shape[2]
    first = place[HALF] * (turned.shape[1] - 2 * unit)
    for i in range(2):
        turned[i] = (keep[i, :, model:].astype(f32) + got[i, :, model:].astype(f32)).T
        for target, bit in ((down, place[BIT]), (send_down, 1 - place[BIT])):
            target[:, i * part : (i + 1) * part] = turned[i, at(first + bit * unit, unit)].astype(target.dtype)


def add_cores(place, keep, got, model):
    part = keep.shape[1]
    return call(
        cores_kernel,
        4,
        (
            wide(part, model), low(part // 2, model), low(part // 2, model),
            wide(model // 4, 2 * part), low(model // 4, 2 * part),
        ),
        [SCALARS, *[VECTORS] * 2],
        [pltpu.VMEM((2, keep.shape[2] - model, part), f32)],
        place, keep, got,
    )


def gates_kernel(flip, place, gates, got, total):
    half, unit = got.shape[1] // 2, total.shape[1]
    both = jnp.concatenate([got[:, :half].astype(f32), got[:, half:].astype(f32)], axis=0)
    for i in range(2):

        @pl.when(place[CHIP] == (1 - i if flip else i))
        def _():
            turned = (gates[:, i * half : (i + 1) * half] + both).T.astype(bf16)
            for k in range(2):
                total[k] = turned[k * unit : (k + 1) * unit]


def add_gates(flip, place, gates, got):
    part, model = gates.shape
    return call(
        functools.partial(gates_kernel, flip), 2, low(2, model // 4, part), [SCALARS, *[VECTORS] * 2], [], place, gates, got
    )


def gather_gates_kernel(place, own, peer, got_own, got_peer, gate, up):
    part = own.shape[1]
    for core in range(2):
        for chip in range(2):

            @pl.when((place[CORE] == core) & (place[CHIP] == chip))
            def _():
                here, there = (gate, up) if core == 0 else (up, gate)
                for target, first, second in ((here, own, peer), (there, got_own, got_peer)):
                    target[:, chip * part : (chip + 1) * part] = first[...].astype(f32)
                    target[:, (1 - chip) * part : (2 - chip) * part] = second[...].astype(f32)


def gather_gates(place, own, peer, got_own, got_peer):
    rows, part = own.shape
    return call(
        gather_gates_kernel,
        2,
        (wide(rows, 2 * part), wide(rows, 2 * part)),
        [SCALARS, *[VECTORS] * 4],
        [],
        place, own, peer, got_own, got_peer,
    )


def down_kernel(down, got, total):
    part = total.shape[2]
    for i in range(2):
        c = slice(i * part, (i + 1) * part)
        total[i] = (down[:, c] + got[:, c].astype(f32)).astype(bf16)


def add_down(down, got):
    rows, width = down.shape
    return call(down_kernel, 1, low(2, rows, width // 2), [VECTORS] * 2, [], down, got)


def attend_back_kernel(
    far, early, place, h_own, h_r1, h_r2, h_r3, h_residual, h_attn_out, h_cotangent, h_chances, h_queries, h_raw, h_table,
    gain_pre, gain_attn, gain_query,
    kv0, kv1, kv2, kv3, o0, o1, o2, o3,
    grad_residual, keep, send, grad_gains, grad_gain_query, grad_projected, g0, g1, g2, g3,
    own, r1, r2, r3, residual, attn_out, cotangent, chances, queries, raw, table,
    keys, values, attn_low, heads, dull, grad_share, weight, sem, soon_sem, late_sem,
):
    plane, dim = kv0.shape[1], kv0.shape[2]
    soon = begin(
        [
            (h_own, own), (h_r1, r1), (h_r2, r2), (h_r3, r3),
            (h_residual, residual), (h_attn_out, attn_out), (h_cotangent, cotangent),
        ],
        soon_sem,
    )
    copies = fetch(place, (o0, o1, o2, o3), weight, sem)
    late = [(h_chances, chances), (h_queries, queries), (h_raw, raw), (h_table, table)]
    for i, kv in enumerate((kv0, kv1, kv2, kv3)):
        late += [(kv.at[0], keys.at[i * plane : (i + 1) * plane]), (kv.at[1], values.at[i * plane : (i + 1) * plane])]
    copies += begin(late, late_sem)
    wait(soon)
    normed = own[...] + r1[...].astype(f32) + r2[...].astype(f32) + r3[...].astype(f32)
    back, grad_gains[0:1] = rms_back(residual[...], gain_pre[...], normed)
    total = cotangent[...].astype(f32) + back
    grad_residual[...] = total
    back, grad_gains[1:2] = rms_back(attn_out[...], gain_attn[...], total)
    attn_low[...] = back.astype(bf16)
    wait(copies)
    rows = own.shape[0]
    here = half_plane(place[0], rows)
    cosine, sine = table[0, here], table[1, here]
    grad_heads = nt(attn_low[...], weight[...]).astype(bf16)
    for h in range(HQ):
        heads[h * rows : (h + 1) * rows] = grad_heads[:, h * dim : (h + 1) * dim]
    grad_share[...] = nt(heads[...], values[...])
    for h in range(HQ):
        r = slice(h * rows, (h + 1) * rows)
        share, back = chances[r], grad_share[r]
        dull[r] = (share * (back - jnp.sum(share * back, axis=-1, keepdims=True))).astype(bf16)
    turned = nn(dull[...], keys[...]) * (dim**-0.5)
    gain_total = jnp.zeros_like(grad_gain_query)
    for h in range(HQ):
        r = slice(h * rows, (h + 1) * rows)
        back, gain_part = rms_back(raw[r], gain_query[...], turn(turned[r], cosine, -sine))
        gain_total = gain_total + gain_part
        grad_projected[:, h * dim : (h + 1) * dim] = back.astype(bf16)
    grad_gain_query[...] = gain_total
    for i, g in enumerate((g0, g1, g2, g3)):
        c = slice(i * plane, (i + 1) * plane)
        g[0] = tn(dull[:, c], queries[...]).astype(g.dtype)
        g[1] = tn(chances[:, c].astype(bf16), heads[...]).astype(g.dtype)
    block, size = grad_projected.shape[1] * 3 // 2 // (2 * far), attn_low.shape[1] // (2 * far)
    parts = [
        columns_of(grad_projected[...], i, range(early), block) + columns_of(attn_low[...], i, range(far), size) for i in range(2)
    ]
    for i in range(2):

        @pl.when(place[NEAR] == i)
        def _():
            keep[...] = jnp.concatenate(parts[i], axis=1)
            send[...] = jnp.concatenate(parts[1 - i], axis=1)


def attend_back(far, early, place, parts, residual, attn_out, cotangent, gain_pre, gain_attn, chances, queries, raw, table, gain_query, planes, pieces):
    rows, model = residual.shape
    dim, span = queries.shape[1], chances.shape[1]
    plane = planes[0].shape[1]
    sent = low(2, plane, dim)
    width = early * HQ * dim * 3 // 2 // (2 * far) + model // 2
    return call(
        functools.partial(attend_back_kernel, far, early),
        8,
        (
            wide(rows, model), low(rows, width), low(rows, width), wide(2, model), wide(1, dim), low(rows, HQ * dim),
            sent, sent, wide(2, plane, dim), sent,
        ),
        [SCALARS, *[ANYWHERE] * 11, *[VECTORS] * 3, *[ANYWHERE] * 8],
        [
            pltpu.VMEM((rows, model), f32),
            *[pltpu.VMEM((rows, model), bf16)] * 3,
            *[pltpu.VMEM((rows, model), f32)] * 2,
            pltpu.VMEM((rows, model), bf16),
            pltpu.VMEM((HQ * rows, span), f32),
            pltpu.VMEM((HQ * rows, dim), bf16),
            pltpu.VMEM((HQ * rows, dim), f32),
            pltpu.VMEM((2, 2 * rows, dim // 2), f32),
            pltpu.VMEM((span, dim), bf16),
            pltpu.VMEM((span, dim), bf16),
            pltpu.VMEM((rows, model), bf16),
            pltpu.VMEM((HQ * rows, dim), bf16),
            pltpu.VMEM((HQ * rows, span), bf16),
            pltpu.VMEM((HQ * rows, span), f32),
            pltpu.VMEM((HQ * dim, model), bf16),
            pltpu.SemaphoreType.DMA((4,)),
            pltpu.SemaphoreType.DMA((7,)),
            pltpu.SemaphoreType.DMA((12,)),
        ],
        place, *parts, residual, attn_out, cotangent, chances, queries, raw, table, gain_pre, gain_attn, gain_query, *planes, *pieces,
        megabytes=56,
    )


def queries_back_kernel(place, grad, q0, q1, q2, q3, result, weight, sem):
    wait(fetch(place, query_columns((q0, q1, q2, q3), weight.shape[1]), weight, sem))
    result[...] = nt(grad[...], weight[...])


def queries_back(place, grad, pieces):
    rows, width = grad.shape
    model = pieces[0].shape[0] * 4
    return call(
        queries_back_kernel,
        4,
        wide(rows, model),
        [SCALARS, VECTORS, *[ANYWHERE] * 4],
        [pltpu.VMEM((model, width), bf16), pltpu.SemaphoreType.DMA((4,))],
        place, grad, *pieces,
    )


def columns_of(value, near, blocks, size):
    return [value[:, (2 * f + near) * size : (2 * f + near + 1) * size] for f in blocks]


def by_place(index, choices):
    for i, choice in enumerate(choices):
        pl.when(index == i)(choice)


def first_products_kernel(place, every, own_heads, got_heads, own, got, keep, send, right, heads):
    rows, near, core = own.shape[0], place[NEAR], place[CORE]
    for target, mine, theirs in ((right, own, got), (heads, own_heads, got_heads)):
        target[half_plane(near, rows)] = mine[...]
        target[half_plane(1 - near, rows)] = theirs[...]
    unit, head = keep.shape[1], heads.shape[1] // 4
    width = keep.shape[2] - 2 * head
    part = tn(every[...], right[:, :width])
    out = tn(right[:, width:], heads[...])
    for i in range(4):
        here = part[i * unit : (i + 1) * unit]
        there = [out[k * unit : (k + 1) * unit, i * head : (i + 1) * head] for k in range(2)]
        for target, chosen in ((keep, core == i % 2), (send, core != i % 2)):

            @pl.when(chosen)
            def _():
                target[i // 2, :, :width] = here.astype(target.dtype)
                for k in range(2):
                    first = width + k * head
                    target[i // 2, :, first : first + head] = there[k].astype(target.dtype)


def first_products(place, every, own_heads, got_heads, own, got):
    rows, model = own_heads.shape[0], every.shape[1]
    width = own.shape[1] - model // 2 + own_heads.shape[1] // 2
    return call(
        first_products_kernel,
        4,
        (wide(2, model // 4, width), low(2, model // 4, width)),
        [SCALARS, *[VECTORS] * 5],
        [pltpu.VMEM((2 * rows, own.shape[1]), bf16), pltpu.VMEM((2 * rows, own_heads.shape[1]), bf16)],
        place, every, own_heads, got_heads, own, got,
    )


def first_cores_kernel(place, keep, got, new, send):
    chip = place[CHIP]
    new[...] = keep[chip] + got[chip].astype(f32)
    send[...] = (keep[1 - chip] + got[1 - chip].astype(f32)).astype(bf16)


def first_cores(place, keep, got):
    shape = keep.shape[1:]
    return call(first_cores_kernel, 2, (wide(*shape), low(*shape)), [SCALARS, *[VECTORS] * 2], [], place, keep, got)


def last_products_kernel(place, every, own, got, gains, keep, send, total_gains, right):
    rows, near, core = own.shape[0], place[NEAR], place[CORE]
    right[half_plane(near, rows)] = own[...]
    right[half_plane(1 - near, rows)] = got[:rows]
    sums = gains[...] + got[rows:].astype(f32)
    total_gains[...] = sums
    unit = keep.shape[1]
    part = tn(every[...], right[...])
    for i in range(4):
        x, c = i // 2, i % 2
        here = part[i * unit : (i + 1) * unit]

        @pl.when(core == c)
        def _():
            keep[x] = here

        @pl.when(core != c)
        def _():
            send[x * unit : (x + 1) * unit] = here.astype(bf16)

    send[2 * unit :] = sums.astype(bf16)


def last_products(place, every, own, got, gains):
    rows, width = own.shape
    unit, more = every.shape[1] // 4, gains.shape[0]
    return call(
        last_products_kernel,
        2,
        (wide(2, unit, width), low(2 * unit + more, width), wide(more, width)),
        [SCALARS, *[VECTORS] * 4],
        [pltpu.VMEM((2 * rows, width), bf16)],
        place, every, own, got, gains,
    )


def last_cores_kernel(place, keep, got, gains, new, send, total_gains):
    unit, chip = new.shape[0], place[CHIP]
    new[...] = keep[chip] + got[at(chip * unit, unit)].astype(f32)
    send[:unit] = (keep[1 - chip] + got[at((1 - chip) * unit, unit)].astype(f32)).astype(bf16)
    sums = gains[...] + got[2 * unit :].astype(f32)
    total_gains[...] = sums
    send[unit:] = sums.astype(bf16)


def last_cores(place, keep, got, gains):
    _, unit, width = keep.shape
    more = gains.shape[0]
    return call(
        last_cores_kernel,
        1,
        (wide(unit, width), low(unit + more, width), wide(more, width)),
        [SCALARS, *[VECTORS] * 3],
        [],
        place, keep, got, gains,
    )


def layout(far, unit, columns, head, gains):
    size, short = columns // far, 2 * unit // far
    lanes = -(-size // 128) * 128
    free = lanes - size
    beside = unit // (head // free) if free and head % free == 0 else 0
    beside = beside if beside <= short and beside * (head // max(free, 1)) == unit else 0
    rest = (short - beside) * head // lanes
    return size, short, lanes, beside, rest, -(-(unit + rest + -(-gains // lanes)) // 16) * 16


def chips_kernel(count, first, got_first, keep, got, gains, out, room, line, block):
    unit, early = first.shape[0], room.shape[1] - keep.shape[1]
    far, head = out.shape[0], (first.shape[1] - early) // 2
    size, short, lanes, beside, rest, _ = layout(far, unit, room.shape[1], head, count)
    room[:, :early] = first[:, :early] + got_first[:, :early].astype(f32)
    room[:, early:] = keep[...] + got[:unit].astype(f32)
    sums = gains[...] + got[unit:].astype(f32)
    width, more = gains.shape[1], -(-count // lanes)
    line[...] = jnp.zeros_like(line)
    for i in range(0, more * lanes, width):
        here = min(width, more * lanes - i)
        line[:, i : i + here] = sums[i // width : i // width + 1, :here]
    block[...] = jnp.zeros_like(block)
    for i in range(more):
        block[unit + rest + i : unit + rest + i + 1] = line[:, i * lanes : (i + 1) * lanes]
    for half in range(2):
        start = early + half * head
        part = first[:, start : start + head] + got_first[:, start : start + head].astype(f32)
        for k in range(far // 2):
            f = half * (far // 2) + k
            mine = part[k * short : (k + 1) * short]
            block[:unit, :size] = room[:, f * size : (f + 1) * size]
            for g in range(unit // beside if beside else 0):
                block[g * beside : (g + 1) * beside, size:] = mine[:beside, g * (lanes - size) : (g + 1) * (lanes - size)]
            for j in range(head // lanes):
                start_row = unit + j * (short - beside)
                block[start_row : start_row + short - beside] = mine[beside:, j * lanes : (j + 1) * lanes]
            out[f] = block[...].astype(bf16)


def last_chips(far, first, got_first, keep, got, gains, head, count):
    unit, width = keep.shape
    columns = first.shape[1] - 2 * head + width
    _, _, lanes, _, _, rows = layout(far, unit, columns, head, count)
    return call(
        functools.partial(chips_kernel, count),
        3,
        low(far, rows, lanes),
        [VECTORS] * 5,
        [pltpu.VMEM((unit, columns), f32), pltpu.VMEM((1, -(-count // lanes) * lanes), f32), pltpu.VMEM((rows, lanes), f32)],
        first, got_first, keep, got, gains,
    )


def last_sum_kernel(count, parts, total, out, gains):
    unit, head = total.shape[0], out.shape[1]
    far = parts.shape[0]
    size, short, lanes, beside, rest, _ = layout(far, unit, total.shape[1] * far, head, count)
    sums = jnp.sum(parts[...].astype(f32), axis=0)
    total[...] = sums[:unit, :size]
    for g in range(unit // beside if beside else 0):
        out[:beside, g * (lanes - size) : (g + 1) * (lanes - size)] = sums[g * beside : (g + 1) * beside, size:]
    for j in range(head // lanes):
        start_row = unit + j * (short - beside)
        out[beside:, j * lanes : (j + 1) * lanes] = sums[start_row : start_row + short - beside]
    for i in range(-(-count // lanes)):
        gains[:, i * lanes : (i + 1) * lanes] = sums[unit + rest + i : unit + rest + i + 1]


def last_sum(parts, unit, columns, head, count):
    far, _, lanes = parts.shape
    return call(
        functools.partial(last_sum_kernel, count),
        2,
        (wide(unit, columns // far), wide(2 * unit // far, head), wide(1, -(-count // lanes) * lanes)),
        [VECTORS],
        [],
        parts,
    )


def down_rows_kernel(part, parts, result):
    for i in range(4):
        for z in range(parts.shape[2] // part):
            first = (4 * z + i) * part
            result[:, first : first + part] = parts[i, :, z * part : (z + 1) * part].astype(f32)


def down_rows(parts, part):
    _, columns, rows = parts.shape
    return call(functools.partial(down_rows_kernel, part), 2, wide(columns, 4 * rows), [VECTORS], [], parts)


def keys_back_kernel(
    early, place, total, received, raw, table, gain_key, partial, grad_residual, tokens, gain_in, grad_queries, grad_gains,
    grad_gain_post, grad_gain_query, k0, k1, k2, k3, grad_tokens, keep, send, sums, grad_projected, gains, weight, sem,
):
    copies = fetch(place, key_columns((k0, k1, k2, k3), weight.shape[1]), weight, sem)
    rows, dim = tokens.shape[0], raw.shape[1]
    here = half_plane(place[0], rows)
    keys = total[0, here] + received[0].astype(f32)
    values = total[1, here] + received[1].astype(f32)
    back, grad_gain_key = rms_back(raw[here], gain_key[...], turn(keys, table[0, here], -table[1, here]))
    grad_projected[:, :dim] = back.astype(bf16)
    grad_projected[:, dim:] = values.astype(bf16)
    wait(copies)
    normed = partial[...] + nt(grad_projected[...], weight[...])
    back, grad_gain_in = rms_back(tokens[...].astype(f32), gain_in[...], normed)
    grad_tokens[...] = grad_residual[...] + back
    model, width = tokens.shape[1], keep.shape[1]
    gains[...] = jnp.zeros_like(gains)
    gains[:, :model] = grad_gain_in
    for i in range(2):
        gains[:, (i + 1) * model : (i + 2) * model] = grad_gains[i : i + 1]
    gains[:, 3 * model : 4 * model] = grad_gain_post[...]
    gains[:, 4 * model : 4 * model + dim] = grad_gain_query[...]
    gains[:, 4 * model + dim : 4 * model + 2 * dim] = grad_gain_key
    block = grad_queries.shape[1] * 3 // 2 // (2 * early[0])
    every = jnp.concatenate([grad_queries[:, early[1] * 2 * block :], grad_projected[...]], axis=1)
    parts = [jnp.concatenate(columns_of(every, i, range(early[0] - early[1]), block), axis=1) for i in range(2)]
    for i in range(2):

        @pl.when(place[NEAR] == i)
        def _():
            keep[...] = parts[i]
            send[:rows] = parts[1 - i]

    extra = jnp.concatenate([gains[:, i * width : (i + 1) * width] for i in range(sums.shape[0])], axis=0)
    sums[...] = extra
    send[rows:] = extra.astype(bf16)


def keys_back(
    far, early, place, total, received, raw, table, gain_key, partial, grad_residual, tokens, gain_in, grad_queries, grad_gains,
    grad_gain_post, grad_gain_query, pieces,
):
    rows, model = tokens.shape
    dim = raw.shape[1]
    width = (far - early) * (HQ + 2) * dim // (2 * far)
    more = -(-(4 * model + 2 * dim) // (16 * width)) * 16
    return call(
        functools.partial(keys_back_kernel, (far, early)),
        4,
        (wide(rows, model), low(rows, width), low(rows + more, width), wide(more, width)),
        [SCALARS, *[VECTORS] * 13, *[ANYWHERE] * 4],
        [
            pltpu.VMEM((rows, 2 * dim), bf16),
            pltpu.VMEM((1, more * width), f32),
            pltpu.VMEM((model, 2 * dim), bf16),
            pltpu.SemaphoreType.DMA((4,)),
        ],
        place, total, received, raw, table, gain_key, partial, grad_residual, tokens, gain_in, grad_queries, grad_gains,
        grad_gain_post, grad_gain_query, *pieces,
    )


def shift(value, by):
    length = lax.axis_size("far")
    pairs = [(i, i + by) for i in range(length) if 0 <= i + by < length]
    return lax.ppermute(value, "far", pairs)


def swap(value, axis):
    return lax.ppermute(value, axis, [(0, 1), (1, 0)])


def diagonal(value):
    return lax.ppermute(value, ("near", "chip"), [(i, 3 - i) for i in range(4)])


def around(values):
    return swap(values[0], "chip"), swap(values[1], "near"), diagonal(values[2])


def far_swap(value, step):
    return lax.ppermute(value, "far", [(i, i ^ step) for i in range(lax.axis_size("far"))])


def after(value, *others):
    return lax.optimization_barrier((value, others))[0]


def halving(value, axis, steps):
    place = lax.axis_index("far")
    for step in steps:
        shape = (*value.shape[:axis], 2, value.shape[axis] // 2, *value.shape[axis + 1 :])
        value = value.reshape(shape)
        bit = place // step % 2
        mine = lax.dynamic_index_in_dim(value, bit, axis, keepdims=False)
        other = lax.dynamic_index_in_dim(value, 1 - bit, axis, keepdims=False)
        value = mine + far_swap(other.astype(bf16), step).astype(f32)
    return value


def shards(
    tokens,
    block_ids,
    w_qkv,
    w_out,
    w_gate,
    w_up,
    w_down,
    gain_in,
    gain_query,
    gain_key,
    gain_attn,
    gain_pre,
    gain_post,
    cotangent,
):
    seq_count, rows, model = tokens.shape
    dim = gain_query.shape[0]
    query_width = HQ * dim
    plane = 2 * rows
    span = WINDOW + plane + BLOCK
    full_len = block_ids.shape[1]
    far_count = lax.axis_size("far")
    near, chip, core = lax.axis_index("near"), lax.axis_index("chip"), lax.axis_index("core")
    far = lax.axis_index("far")
    half_far = far_count // 2
    far_bits = [1 << i for i in reversed(range(far_count.bit_length() - 1))]
    low_bits = far_bits[1:]
    half = far // half_far
    bit = far // low_bits[0] % 2
    place = jnp.stack([near, chip, core, far % 2, half, bit]).astype(jnp.int32)
    start = far * plane
    ff = w_gate.shape[1]
    part = ff // (far_count * 4)
    early = query_width // (w_qkv.shape[1] // far_count)
    tokens = tokens.reshape(rows, model)
    cotangent = cotangent.reshape(rows, model)
    gain_in, gain_query, gain_key, gain_attn, gain_pre, gain_post = (
        g.reshape(1, -1) for g in (gain_in, gain_query, gain_key, gain_attn, gain_pre, gain_post)
    )

    qkv_chip, peer_tokens = swap(w_qkv, "chip"), swap(tokens, "near")
    gates_own, *gates_other = chip_columns(place, w_gate, w_up, far_count)
    split = lax.dynamic_index_in_dim(w_down.reshape(-1, 2, 2, part, model), near, 1, keepdims=False)
    down_own = lax.dynamic_index_in_dim(split, chip, 1, keepdims=False).reshape(-1, model)
    down_other = lax.dynamic_index_in_dim(split, 1 - chip, 1, keepdims=False).reshape(-1, model)
    qkv_core, out_core, down_core = swap(w_qkv, "core"), swap(w_out, "core"), swap(down_own, "core")
    qkv_pieces = w_qkv, qkv_chip, qkv_core, swap(qkv_chip, "core")

    frequency = 10000.0 ** (-jnp.arange(dim // 2, dtype=f32) * 2.0 / dim)
    angles = (start + jnp.arange(plane)).astype(f32)[:, None] * frequency[None, :]
    table = jnp.stack([jnp.cos(angles), jnp.sin(angles)])
    normed_in, pair, raw_keys, every = keys_of(
        place, after(tokens, down_core, out_core, gates_own), peer_tokens, gain_in, gain_key, table, qkv_pieces
    )
    gates_core = swap(gates_own, "core")
    out_chip = swap(after(w_out, qkv_chip), "chip")
    first = swap(after(gates_other[0], qkv_chip), "chip")
    second = swap(after(gates_other[1], out_chip), "chip")
    down_chip = swap(after(down_other, first), "chip")
    out_pieces = w_out, out_chip, out_core, swap(out_chip, "core")
    first_rest, second_rest = far_swap(first, 1), far_swap(second, 1)
    four = first, second, first_rest, second_rest
    gates = gates_own, gates_core, *four, *(swap(p, "core") for p in four)
    downs = down_own, down_chip, down_core, swap(down_chip, "core")

    padded = jnp.pad(block_ids, ((0, 0), (WINDOW, BLOCK)), constant_values=1 << 30)
    key_ids = lax.dynamic_slice_in_dim(padded, start, span, 1)
    query_ids = lax.dynamic_slice_in_dim(block_ids, start + near * rows, rows, 1).reshape(rows, 1)

    planes = (shift(pair, 2), shift(pair, 1), pair, shift(pair, -1))
    queries, raw_queries = queries_of(place, normed_in, gain_query, table, qkv_pieces)
    chances, heads_out, attn_out, residual, normed_pre = attend(
        place, after(queries, first, gates_core), planes, key_ids, query_ids, tokens, gain_attn, gain_pre, out_pieces
    )

    far_normed = far_swap(after(normed_pre, first_rest), half_far)
    blocks = (normed_pre, *around([normed_pre] * 3))
    all_normed, hidden, slope, gelu, own, *sent = forward(place, after(blocks, far_normed), gates, downs)
    far_normed = after(far_normed, second_rest)
    far_normed = (far_normed, *around([far_normed] * 3))
    sent = after(sent, *far_normed)
    output, grad_down_proj, grad_gain_post = turning((own, *around(sent)), residual, cotangent, gain_post)
    far_down = far_swap(grad_down_proj, half_far)
    blocks = (grad_down_proj, *around([grad_down_proj] * 3))
    far_kept = far_hidden(place, hidden, after(far_normed, grad_down_proj), gates)
    blocks = after(blocks, far_down, *far_kept)
    all_down, gate_low, up_low, own, *sent = backward(place, blocks, slope, gelu, gates, downs)
    far_down = (far_down, *around([far_down] * 3))
    sent = after(sent, *far_down)
    parts = (own, *around(sent))
    keep_grads, send_grads = weight_grads(
        place, all_normed, all_down, after(gate_low, *sent), up_low, far_normed, far_down, far_kept, downs
    )
    got_grads = swap(after(send_grads, parts), "core")
    (
        grad_residual, own_right, other_right, grad_gains, grad_gain_query, grad_queries, *sent,
    ) = attend_back(
        far_count, early, place, after(parts, keep_grads), residual, attn_out, cotangent, gain_pre, gain_attn, chances, queries, raw_queries, table, gain_query,
        planes, out_pieces,
    )
    grad_gates, send_other, send_own, grad_down, send_down = add_cores(place, after(keep_grads, grad_queries), got_grads, model)
    total = after(sent[2], send_down) + shift(sent[0], -2).astype(f32)
    total = total + shift(sent[1], -1).astype(f32) + shift(sent[3], 1).astype(f32)
    partial = queries_back(place, after(grad_queries, send_down), qkv_pieces)
    got, got_heads = swap(other_right, "near"), swap(after(heads_out, grad_queries), "near")
    total, grad_gates, send_other, send_own, grad_down, send_down, partial, got, got_heads = lax.optimization_barrier(
        (total, grad_gates, send_other, send_own, grad_down, send_down, partial, got, got_heads)
    )

    received = swap(
        lax.dynamic_slice_in_dim(total, (1 - near) * rows, rows, 1).astype(bf16), "near"
    )
    got_down, got_other, got_own = (far_swap(g, low_bits[0]) for g in (send_down, send_other, send_own))
    keep_first, send_first = first_products(place, every, heads_out, got_heads, own_right, got)
    keep_first, send_first = first_cores(place, keep_first, swap(send_first, "core"))
    got_first = swap(send_first, "chip")
    grad_tokens, own_right, other_right, gains = keys_back(
        far_count, early, place, after(total, send_first), received, raw_keys, table, gain_key, partial, grad_residual, tokens, gain_in,
        grad_queries, grad_gains, grad_gain_post, grad_gain_query, qkv_pieces,
    )
    keep, send, gains = last_products(place, every, after(own_right, got_down), swap(other_right, "near"), gains)
    keep, send, gains = last_cores(place, after(keep, got_other), swap(send, "core"), gains)
    grad_down = add_down(grad_down, got_down)
    sums = last_chips(
        far_count, keep_first, got_first, keep, swap(send, "chip"), gains, query_width // 4, 4 * model + 2 * dim
    )
    columns = model // far_count // 2
    down_parts = halving(grad_down, 1, low_bits[1:]).astype(bf16).reshape(2, 2, columns, -1)
    down_parts = down_parts.transpose(1, 0, 2, 3).reshape(4, columns, -1)
    down_parts = lax.all_to_all(down_parts, ("near", "chip"), 0, 0, tiled=True)
    other_gates = add_gates(True, place, after(grad_gates, send), got_other)
    peer_gates = swap(halving(other_gates, 2, low_bits[1:]).astype(bf16), "chip")
    sums, got_own = lax.optimization_barrier((sums, got_own))

    sums = lax.all_to_all(sums, "far", 0, 0, tiled=True)
    qkv_total, out_total, gains = last_sum(sums, model // 4, w_qkv.shape[1] // 2, query_width // 4, 4 * model + 2 * dim)
    out_total, gains = out_total.T, gains.reshape(-1)
    own_gates = halving(add_gates(False, place, grad_gates, got_own), 2, low_bits[1:]).astype(bf16)
    mine = [lax.dynamic_index_in_dim(g, core, 0, keepdims=False) for g in (own_gates, peer_gates)]
    theirs = [lax.dynamic_index_in_dim(g, 1 - core, 0, keepdims=False) for g in (own_gates, peer_gates)]
    gate_total, up_total = gather_gates(place, *mine, *(swap(g, "core") for g in theirs))
    down_total = down_rows(down_parts, part).T

    gain_in, gain_pre, gain_attn, gain_post = (gains[i * model : (i + 1) * model] for i in range(4))
    gain_query, gain_key = gains[4 * model :][:dim], gains[4 * model + dim :][:dim]
    return (
        output.reshape(seq_count, rows, model),
        grad_tokens.reshape(seq_count, rows, model),
        qkv_total,
        out_total,
        gate_total,
        up_total,
        down_total,
        gain_in,
        gain_query,
        gain_key,
        gain_attn,
        gain_pre,
        gain_post,
    )


def solution(mesh):
    seq, dp = mesh.devices.shape
    parts = Mesh(mesh.devices.reshape(seq // 2, 2, 2, dp // 2), (*SEQ, *DP))
    rows = P(DP, None)
    whole = P(None)
    placed = (P(DP, SEQ, None), P(DP, None), *[rows] * 5, *[whole] * 6, P(DP, SEQ, None))
    return jax.shard_map(
        shards,
        mesh=parts,
        in_specs=placed,
        out_specs=(*[P(DP, SEQ, None)] * 2, *[P(DP, SEQ)] * 5, *[whole] * 6),
        check_vma=False,
    )
```
